512 devices in a mesh: col: 8 (over z_lo, core), row: 64 (over y, x, z_hi).
Axes of the slice: x: 4, y: 8, z: 8 (z_hi: 2, z_lo: 4; z = z_hi * 4 + z_lo), core: 2. Of those that a mesh axis runs over, the one named last changes fastest.
Arguments:
- trace: float32 [64, 64, 2048], P('col', None, 'row'), may hold values from -6 to 6
- step_coeff: float32 [64], P('col'), may hold values from -1 to 1
- pair_coeff: float32 [64], P('col'), may hold values from -1 to 1
- challenges: float32 [64], P('col'), may hold values from -0.25 to 0.25
Outputs:
- extension: float32 [2, 64, 64, 8192], P(None, 'col', None, 'row')
- quotient_values: float32 [2, 64, 8192], P(None, None, 'row')
- quotient_coeffs: float32 [2, 64, 8192], P(None, 'row')
The draws below stay inside these ranges and needn't reach their ends.
All inputs are finite; a program needn't handle non-finite values.
Results may differ from the reference program's by a relative error of at most 0.0001.
Values sent between devices are 32-bit elements; how exact they have to be, the bound alone decides.
A program may use at most 64 MiB of HBM per device.

```python
import math
import jax
import jax.numpy as jnp
from jax import lax

NC = 64
ROWS_DEV = 2048
SEGS = 64


def steps_of(own_key, extent, shards, smallest, top_value):
    def one(position, parts):
        heights = jax.random.uniform(jax.random.fold_in(jax.random.fold_in(own_key, 6), position), (parts,), jnp.float32, smallest / len(shards), top_value / len(shards))
        return jnp.repeat(jnp.exp(heights), extent[position] // parts).reshape((-1,) + (1,) * (len(extent) - position - 1))

    loudness = one(*shards[0])
    for cut in shards[1:]:
        loudness = loudness * one(*cut)
    return loudness


def normal_values(key, extent, scale, bound, shards=(), dtype=jnp.bfloat16):
    drawn = scale * jax.random.normal(key, extent, jnp.float32)
    if shards:
        drawn = drawn * steps_of(key, extent, shards, -0.22, 0.18)
    return jnp.clip(drawn, -bound, bound).astype(dtype)


def setup_inputs(seed: int = 0) -> dict:
    seeds = jax.random.split(jax.random.key(seed), 5)
    return {
        "trace": normal_values(seeds[0], (NC, SEGS, ROWS_DEV), 1.0, 6.0, ((0, 8), (2, 64)), jnp.float32),
        "step_coeff": jnp.clip(jax.random.uniform(seeds[1], (NC,), jnp.float32, -1.0, 1.0) * steps_of(seeds[1], (NC,), ((0, 8),), -0.4, 0.0), -1.0, 1.0),
        "pair_coeff": jnp.clip(jax.random.uniform(seeds[2], (NC,), jnp.float32, -1.0, 1.0) * steps_of(seeds[2], (NC,), ((0, 8),), -0.4, 0.0), -1.0, 1.0),
        "challenges": jnp.clip(jax.random.uniform(seeds[3], (NC,), jnp.float32, -0.25, 0.25) * steps_of(seeds[3], (NC,), ((0, 8),), -0.4, 0.0), -0.25, 0.25),
    }


def reference(trace, step_coeff, pair_coeff, challenges):
    trace_len = SEGS * ROWS_DEV
    coset_len = 4 * trace_len
    series = trace.reshape(NC // 2, 2, trace_len)
    degree = jnp.arange(trace_len).astype(jnp.float32) * (-math.pi / coset_len)
    twist_factor = jnp.cos(degree) + 1j * jnp.sin(degree)
    params = jnp.stack([challenges, challenges * step_coeff, challenges * pair_coeff], axis=1).reshape(NC // 2, 2, 3)

    def one_pair(running, inputs):
        pair_series, pair_params = inputs
        coeffs = jnp.fft.ifft(pair_series, axis=-1) * twist_factor
        padded = jnp.pad(coeffs, ((0, 0), (0, coset_len - trace_len)))
        values = jnp.fft.fft(padded, axis=-1)
        following = jnp.roll(values, -4, axis=1)
        partner = values[::-1]
        residue = pair_params[:, 0:1] * following - pair_params[:, 1:2] * values - pair_params[:, 2:3] * values * partner
        summed = lax.optimization_barrier(jnp.sum(residue, axis=0))
        return ((running[0] + jnp.real(summed), running[1] + jnp.imag(summed)), jnp.stack([jnp.real(values), jnp.imag(values)]))
    start_sums = (jnp.zeros((coset_len,), jnp.float32), jnp.zeros((coset_len,), jnp.float32))
    (sum_real, sum_imag), stacked = lax.scan(one_pair, start_sums, (series, params))
    extension = stacked.transpose(1, 0, 2, 3).reshape(2, NC, SEGS, 4 * ROWS_DEV)
    points = jnp.arange(coset_len)
    zero_angle = ((2 * points + 1) % 8).astype(jnp.float32) * (-math.pi / 4)
    zero_real = jnp.cos(zero_angle) - 1.0
    zero_imag = jnp.sin(zero_angle)
    modulus_sq = zero_real * zero_real + zero_imag * zero_imag
    value_real = (sum_real * zero_real + sum_imag * zero_imag) / modulus_sq
    value_imag = (sum_imag * zero_real - sum_real * zero_imag) / modulus_sq
    combined = value_real + 1j * value_imag
    quotient = jnp.fft.ifft(combined) * math.sqrt(coset_len)
    shift_angle = points.astype(jnp.float32) * (math.pi / coset_len)
    quotient = quotient * (jnp.cos(shift_angle) + 1j * jnp.sin(shift_angle))
    quotient_out = jnp.stack([jnp.real(quotient), jnp.imag(quotient)]).reshape(2, 4 * ROWS_DEV, SEGS).transpose(0, 2, 1)
    values_out = jnp.stack([value_real, value_imag]).reshape(2, SEGS, 4 * ROWS_DEV)
    return (extension, values_out, quotient_out)
```

```python
import math

import jax
import jax.numpy as jnp
import numpy as np
from jax import lax
from jax.experimental import pallas as pl
from jax.experimental.pallas import tpu as pltpu
from jax.sharding import PartitionSpec as P

SEG = 64
COLS = 8
PAIRS = 4
RUN = 32
LANES = 128
TRACE_LEN = SEG * SEG * RUN
COSET_LEN = 4 * TRACE_LEN
MESH = pl.DeviceIdType.MESH
F32 = jnp.float32
BF16 = jnp.bfloat16


def halves(matrix):
    high = matrix.astype(BF16)
    low = (matrix - high.astype(np.float64)).astype(BF16)
    return np.stack([high, low])


def complex_rows(angle):
    return np.stack([np.cos(angle), np.sin(angle)])


def real_form(angle, out_order, in_order):
    cosine, sine = np.cos(angle), np.sin(angle)
    grid = np.stack([np.stack([cosine, -sine]), np.stack([sine, cosine])])
    places = {"co": (0, 2), "oc": (2, 0), "ci": (1, 3), "ic": (3, 1)}
    rows, cols = angle.shape
    return grid.transpose(places[out_order] + places[in_order]).reshape(2 * rows, 2 * cols)


def build_tables():
    tau = 2.0 * np.pi
    seg = np.arange(SEG)
    run = np.arange(RUN)
    first = real_form(tau * np.outer(seg, seg) / SEG, "oc", "ci")
    middle = []
    vectors = []
    lane = np.arange(LANES)
    offset = lane // 4 + (2 * (lane % 4) + 1) / 8.0
    rim = RUN + (2 * (lane % 4) + 1) / 8.0
    rim_here = (lane >= LANES - 16).astype(np.float64)
    beta = np.tile(run, PAIRS)
    for u in range(SEG):
        angle = tau * np.outer(SEG * seg + u, seg) / (SEG * SEG)
        matrix = real_form(angle, "co", "ic")
        middle.append(np.stack([halves(matrix), halves(matrix.T)]))
        vectors.append(
            np.concatenate(
                [
                    complex_rows(tau * beta * u / TRACE_LEN),
                    complex_rows(-tau * offset * u / TRACE_LEN),
                    complex_rows(-tau * rim * u / TRACE_LEN),
                    complex_rows(tau * (2 * lane + 1) * u / (2 * COSET_LEN)),
                ]
            )
        )
    twist_in = complex_rows(tau * beta * (64 * seg[:, None] - 2048) / TRACE_LEN)
    twist_out = complex_rows(-tau * offset * (64 * seg[:, None] - 2048) / TRACE_LEN) / TRACE_LEN
    twist_rim = (
        complex_rows(-tau * rim * (64 * seg[:, None] - 2048) / TRACE_LEN) / TRACE_LEN * rim_here
    )
    twist_quot = complex_rows(
        tau * (2 * lane + 1) * (64 * seg[:, None]) / (2 * COSET_LEN)
    ) / math.sqrt(COSET_LEN)
    twists = np.concatenate([twist_in, twist_out, twist_rim, twist_quot])
    spread = np.zeros((PAIRS, RUN, 5, LANES))
    mean = np.zeros((PAIRS, RUN, LANES))
    for j in range(PAIRS):
        spread[j, :, j, :] = 1.0 / np.sin(np.pi * (offset[None, :] - run[:, None]) / RUN)
        own = (lane >= LANES - 16) & ((lane - (LANES - 16)) // 4 == j)
        spread[j, :, 4, :] = own / np.sin(np.pi * (rim[None, :] - run[:, None]) / RUN)
        mean[j, :, j] = 1.0 / TRACE_LEN
    spread = spread.reshape(LANES, 5 * LANES)
    half = np.arange(SEG)
    order = np.concatenate([2 * half, 2 * half + 1])
    last = real_form(tau * np.outer(order, 2 * lane + 1) / 256.0, "co", "ci")
    shape = (2 * (lane % 4) + 1) / 8.0
    gain = np.exp(-1j * np.pi * shape) * np.sin(np.pi * shape)
    vanish = 1.0 / (np.exp(-1j * np.pi * (2 * (lane % 4) + 1) / 4.0) - 1.0)
    scales = []
    for value in (gain, gain * vanish, gain * gain * vanish):
        scales += [value.real, value.imag]
    scales += [np.zeros(LANES)] * 2
    return {
        "vectors": np.stack(vectors).astype(np.float32),
        "middle": np.stack(middle),
        "first": np.stack([halves(first), halves(first.T)]),
        "twists": twists.astype(np.float32),
        "spread": halves(spread),
        "mean": mean.reshape(LANES, LANES).astype(BF16),
        "last": halves(last),
        "scales": np.stack(scales).astype(np.float32),
    }


def parts_of(value):
    high = value.astype(BF16)
    low = (value - high.astype(F32)).astype(BF16)
    return high, low


def left_dot(table, value):
    high, low = parts_of(value)
    left = jnp.concatenate([table[0], table[0], table[1]], axis=1)
    right = jnp.concatenate([high, low, high], axis=0)
    return jnp.dot(left, right, preferred_element_type=F32)


def right_dot(value, table):
    high, low = parts_of(value)
    left = jnp.concatenate([high, low, high], axis=1)
    right = jnp.concatenate([table[0], table[0], table[1]], axis=0)
    return jnp.dot(left, right, preferred_element_type=F32)


def turn(real, imag, cosine, sine):
    return real * cosine - imag * sine, real * sine + imag * cosine


def kernel(
    trace_hbm, step_ref, pair_ref, chal_ref,
    vectors_hbm, middle_hbm, first_hbm, twists_hbm, spread_hbm, mean_hbm, last_hbm, scales_hbm,
    ext_hbm, val_hbm, quot_hbm,
    trace, vectors, middle, first, twists, spread, mean, last, scales,
    ext, val, quot,
    send1, recv1, send2, recv2, send3, recv3, send4, recv4, send5, recv5,
    load_sems, store_sems, send_sems, recv_sems,
):
    me = lax.axis_index("row")
    col = lax.axis_index("col")

    barrier = pltpu.get_barrier_semaphore()

    def greet_row(k, carry):
        pl.semaphore_signal(
            barrier, inc=1, device_id={"row": lax.rem(me + k, SEG)}, device_id_type=MESH
        )
        return carry

    def greet_col(k, carry):
        pl.semaphore_signal(
            barrier, inc=1, device_id={"col": lax.rem(col + k, COLS)}, device_id_type=MESH
        )
        return carry

    loads = [
        pltpu.make_async_copy(src, dst, load_sems.at[i])
        for i, (src, dst) in enumerate(
            [
                (trace_hbm, trace),
                (first_hbm, first),
                (vectors_hbm.at[me], vectors),
                (middle_hbm.at[me], middle),
                (twists_hbm, twists),
                (spread_hbm, spread),
                (mean_hbm, mean),
                (scales_hbm, scales),
                (last_hbm, last),
            ]
        )
    ]
    for load in loads:
        load.start()
    lax.fori_loop(1, SEG, greet_row, 0)
    lax.fori_loop(1, COLS, greet_col, 0)

    loads[0].wait()
    loads[1].wait()
    grid = jnp.concatenate(
        [
            jnp.concatenate([trace[2 * j + c] for j in range(PAIRS)], axis=1)
            for c in range(2)
        ],
        axis=0,
    )
    head = left_dot(first[0], grid)
    send1[...] = head.reshape(SEG, 2, LANES)
    recv1[me] = send1[me]
    pl.semaphore_wait(barrier, SEG - 1 + COLS - 1)

    def post1(k, carry):
        peer = lax.rem(me + k, SEG)
        pltpu.make_async_remote_copy(
            src_ref=send1.at[peer], dst_ref=recv1.at[me],
            send_sem=send_sems.at[0], recv_sem=recv_sems.at[0],
            device_id={"row": peer}, device_id_type=MESH,
        ).start()
        return carry

    lax.fori_loop(1, SEG, post1, 0)

    for load in loads[2:]:
        load.wait()
    head_high, head_low = parts_of(head[:8])
    sums = jnp.dot(head_high, mean[...], preferred_element_type=F32) + jnp.dot(
        head_low, mean[...], preferred_element_type=F32
    )
    parity = lax.broadcasted_iota(jnp.int32, (LANES, LANES), 0) % 2
    sums = jnp.where(parity == 0, sums[0:1], sums[1:2])

    def table(index, row):
        base = twists[2 * index], twists[2 * index + 1]
        return turn(*base, vectors[2 * row : 2 * row + 1], vectors[2 * row + 1 : 2 * row + 2])

    in_cos, in_sin = table(0, 0)
    out_cos, out_sin = table(1, 1)
    rim_cos, rim_sin = table(2, 2)

    pltpu.make_async_copy(
        recv1.at[pl.ds(0, SEG - 1)], recv1.at[pl.ds(0, SEG - 1)], recv_sems.at[0]
    ).wait()

    mixed = left_dot(middle[0], recv1[...].reshape(LANES, LANES))
    real, imag = turn(mixed[:SEG], mixed[SEG:], in_cos, in_sin)
    wide = right_dot(jnp.concatenate([real, imag], axis=0), spread)
    pieces = []
    for j in range(5):
        cosine, sine = (out_cos, out_sin) if j < 4 else (rim_cos, rim_sin)
        part = wide[:, LANES * j : LANES * (j + 1)]
        real, imag = turn(part[:SEG], part[SEG:], cosine, sine)
        pieces.append(jnp.concatenate([real, imag], axis=0))
    back = left_dot(middle[1], jnp.concatenate(pieces, axis=1))
    for j in range(5):
        part = back[:, LANES * j : LANES * (j + 1)]
        if j == 4:
            part = part + sums
        send2[j] = part.reshape(SEG, 2, LANES)
    for j in range(5):
        recv2[j, me] = send2[j, me]

    def post2(k, carry):
        peer = lax.rem(me + k, SEG)
        pltpu.make_async_remote_copy(
            src_ref=send2.at[:, peer], dst_ref=recv2.at[:, me],
            send_sem=send_sems.at[1], recv_sem=recv_sems.at[1],
            device_id={"row": peer}, device_id_type=MESH,
        ).start()
        return carry

    lax.fori_loop(1, SEG, post2, 0)
    quot_cos, quot_sin = table(3, 3)
    pltpu.make_async_copy(
        recv2.at[:, pl.ds(0, SEG - 1)], recv2.at[:, pl.ds(0, SEG - 1)], recv_sems.at[1]
    ).wait()

    arrived = jnp.concatenate([recv2[j].reshape(LANES, LANES) for j in range(5)], axis=1)
    field = left_dot(first[1], arrived)

    def scale(row):
        return scales[2 * row : 2 * row + 1], scales[2 * row + 1 : 2 * row + 2]

    rim_part = field[:, 4 * LANES :]
    lane = lax.broadcasted_iota(jnp.int32, (SEG, LANES), 1)
    gain_real, gain_imag = scale(0)
    ahead = jnp.zeros((SEG, LANES), F32)
    own = jnp.zeros((SEG, LANES), F32)
    product = jnp.zeros((SEG, LANES), F32)
    cross = jnp.zeros((SEG, LANES), F32)
    rim_weight = [jnp.zeros((SEG, LANES), F32)] * 2
    level_ahead = jnp.zeros((1, 1), F32)
    level_own = jnp.zeros((1, 1), F32)
    level_product = jnp.zeros((1, 1), F32)
    for j in range(PAIRS):
        mean_c = rim_part[0:1, j : j + 1]
        mean_d = rim_part[SEG : SEG + 1, j : j + 1]
        chal_c, chal_d = chal_ref[2 * j], chal_ref[2 * j + 1]
        step_c, step_d = chal_c * step_ref[2 * j], chal_d * step_ref[2 * j + 1]
        weight = chal_c * pair_ref[2 * j] + chal_d * pair_ref[2 * j + 1]
        raw_c = field[:SEG, LANES * j : LANES * (j + 1)]
        raw_d = field[SEG:, LANES * j : LANES * (j + 1)]
        real_c = raw_c + mean_d
        real_d = raw_d - mean_c
        ext[0, 2 * j] = gain_real * real_c - gain_imag * mean_c
        ext[1, 2 * j] = gain_imag * real_c + gain_real * mean_c
        ext[0, 2 * j + 1] = gain_real * real_d - gain_imag * mean_d
        ext[1, 2 * j + 1] = gain_imag * real_d + gain_real * mean_d
        ahead += chal_c * raw_c + chal_d * raw_d
        own += step_c * real_c + step_d * real_d
        product += weight * (real_c * real_d)
        cross += weight * (real_c * mean_d + real_d * mean_c)
        group = (lane >= LANES - 16 + 4 * j) & (lane < LANES - 12 + 4 * j)
        rim_weight = [
            jnp.where(group, chal_c, rim_weight[0]),
            jnp.where(group, chal_d, rim_weight[1]),
        ]
        level_ahead += chal_c * mean_d - chal_d * mean_c
        level_own += (chal_c - step_c) * mean_c + (chal_d - step_d) * mean_d
        level_product += weight * (mean_c * mean_d)
    ext_copy = pltpu.make_async_copy(ext, ext_hbm, store_sems.at[0])
    ext_copy.start()
    rim_sum = rim_part[:SEG] * rim_weight[0] + rim_part[SEG:] * rim_weight[1]
    rim_sum = rim_sum + pltpu.roll(rim_sum, 4, 1)
    rim_sum = rim_sum + pltpu.roll(rim_sum, 8, 1)
    ahead = jnp.where(lane < LANES - 4, pltpu.roll(ahead, LANES - 4, 1), rim_sum)
    line_real = ahead + level_ahead - own
    line_imag = level_own
    square_real = product - level_product
    square_imag = cross
    line_scale, square_scale = scale(1), scale(2)
    value_real = (
        line_scale[0] * line_real
        - line_scale[1] * line_imag
        - square_scale[0] * square_real
        + square_scale[1] * square_imag
    )
    value_imag = (
        line_scale[0] * line_imag
        + line_scale[1] * line_real
        - square_scale[0] * square_imag
        - square_scale[1] * square_real
    )
    mixed = left_dot(first[0], jnp.concatenate([value_real, value_imag], axis=0))
    for i in range(COLS):
        send3[i, 0:16] = mixed[16 * i : 16 * (i + 1)]
        send3[i, 16:24] = value_real[8 * i : 8 * (i + 1)]
        send3[i, 24:32] = value_imag[8 * i : 8 * (i + 1)]

    def post3(k, carry):
        peer = lax.rem(col + k, COLS)
        pltpu.make_async_remote_copy(
            src_ref=send3.at[peer], dst_ref=recv3.at[col],
            send_sem=send_sems.at[2], recv_sem=recv_sems.at[2],
            device_id={"col": peer}, device_id_type=MESH,
        ).start()
        return carry

    lax.fori_loop(1, COLS, post3, 0)
    recv3[col] = send3[col]
    pltpu.make_async_copy(
        recv3.at[pl.ds(0, COLS - 1)], recv3.at[pl.ds(0, COLS - 1)], recv_sems.at[2]
    ).wait()
    total = recv3[0]
    for i in range(1, COLS):
        total = total + recv3[i]
    send4[...] = total[:16].reshape(8, 2, LANES)
    send5[...] = total[16:]

    here = lax.div(me, COLS) == col

    def post4(k, carry):
        line = lax.rem(lax.div(k, COLS) + me, COLS)
        across = lax.rem(k + col, COLS)
        target = col * COLS + line
        alone = (target == me) & (across == col)

        @pl.when(jnp.logical_not(alone))
        def _():
            pltpu.make_async_remote_copy(
                src_ref=send4.at[line], dst_ref=recv4.at[me],
                send_sem=send_sems.at[3], recv_sem=recv_sems.at[3],
                device_id={"col": across, "row": target}, device_id_type=MESH,
            ).start()

        @pl.when(alone)
        def _():
            pltpu.make_async_copy(send4.at[line], recv4.at[me], recv_sems.at[3]).start()

        return carry

    lax.fori_loop(0, SEG, post4, 0)

    def post5(k, carry):
        pltpu.make_async_remote_copy(
            src_ref=send5, dst_ref=recv5.at[col],
            send_sem=send_sems.at[4], recv_sem=recv_sems.at[4],
            device_id={"col": lax.rem(col + k, COLS)}, device_id_type=MESH,
        ).start()
        return carry

    lax.fori_loop(1, COLS, post5, 0)
    recv5[col] = send5[...]

    pltpu.make_async_copy(recv4, recv4, recv_sems.at[3]).wait()
    mixed = left_dot(middle[0], recv4[...].reshape(LANES, LANES))
    real, imag = turn(mixed[:SEG], mixed[SEG:], quot_cos, quot_sin)
    both = jnp.concatenate([real, imag], axis=1)
    both = jnp.concatenate([both, both], axis=0)
    high, low = parts_of(both)
    result = lax.dot_general(
        jnp.concatenate([last[0], last[0], last[1]], axis=1),
        jnp.concatenate([high, low, high], axis=1),
        (((1,), (1,)), ((), ())),
        preferred_element_type=F32,
    )
    for c in range(2):
        even = result[LANES * c : LANES * c + SEG]
        odd = result[LANES * c + SEG : LANES * (c + 1)]
        quot[c] = jnp.where(lane < SEG, even, odd)
    quot_copy = pltpu.make_async_copy(quot, quot_hbm, store_sems.at[1])
    quot_copy.start()

    pltpu.make_async_copy(
        recv5.at[pl.ds(0, COLS - 1)], recv5.at[pl.ds(0, COLS - 1)], recv_sems.at[4]
    ).wait()
    for i in range(COLS):
        val[0, 8 * i : 8 * (i + 1)] = recv5[i, 0:8]
        val[1, 8 * i : 8 * (i + 1)] = recv5[i, 8:16]
    val_copy = pltpu.make_async_copy(val, val_hbm, store_sems.at[2])
    val_copy.start()

    pltpu.make_async_copy(
        send1.at[pl.ds(0, SEG - 1)], send1.at[pl.ds(0, SEG - 1)], send_sems.at[0]
    ).wait()
    pltpu.make_async_copy(
        send2.at[:, pl.ds(0, SEG - 1)], send2.at[:, pl.ds(0, SEG - 1)], send_sems.at[1]
    ).wait()
    pltpu.make_async_copy(
        send3.at[pl.ds(0, COLS - 1)], send3.at[pl.ds(0, COLS - 1)], send_sems.at[2]
    ).wait()

    @pl.when(here)
    def _():
        pltpu.make_async_copy(
            recv4.at[pl.ds(0, SEG - 1)], recv4.at[pl.ds(0, SEG - 1)], send_sems.at[3]
        ).wait()

    @pl.when(jnp.logical_not(here))
    def _():
        pltpu.make_async_copy(recv4, recv4, send_sems.at[3]).wait()

    pltpu.make_async_copy(
        recv5.at[pl.ds(0, COLS - 1)], recv5.at[pl.ds(0, COLS - 1)], send_sems.at[4]
    ).wait()
    ext_copy.wait()
    quot_copy.wait()
    val_copy.wait()


def shards(trace, step_coeff, pair_coeff, challenges):
    tables = build_tables()
    names = ["vectors", "middle", "first", "twists", "spread", "mean", "last", "scales"]
    constants = [jnp.asarray(tables[name]) for name in names]
    vmem = pltpu.VMEM
    anywhere = pl.BlockSpec(memory_space=pl.ANY)
    scalar = pl.BlockSpec(memory_space=pltpu.SMEM)
    outs = (
        jax.ShapeDtypeStruct((2, COLS, SEG, LANES), F32),
        jax.ShapeDtypeStruct((2, SEG, LANES), F32),
        jax.ShapeDtypeStruct((2, SEG, LANES), F32),
    )
    tables_scratch = [
        vmem(c.shape[1:] if n in ("vectors", "middle") else c.shape, c.dtype)
        for n, c in zip(names, constants, strict=True)
    ]
    extension, values, quotient = pl.pallas_call(
        kernel,
        out_shape=outs,
        in_specs=[anywhere, scalar, scalar, scalar] + [anywhere] * len(constants),
        out_specs=(anywhere,) * 3,
        scratch_shapes=[
            vmem(trace.shape, F32),
            *tables_scratch,
            *[vmem(o.shape, F32) for o in outs],
            vmem((SEG, 2, LANES), F32),
            vmem((SEG, 2, LANES), F32),
            vmem((5, SEG, 2, LANES), F32),
            vmem((5, SEG, 2, LANES), F32),
            vmem((COLS, 32, LANES), F32),
            vmem((COLS, 32, LANES), F32),
            vmem((8, 2, LANES), F32),
            vmem((SEG, 2, LANES), F32),
            vmem((16, LANES), F32),
            vmem((COLS, 16, LANES), F32),
            pltpu.SemaphoreType.DMA((9,)),
            pltpu.SemaphoreType.DMA((3,)),
            pltpu.SemaphoreType.DMA((5,)),
            pltpu.SemaphoreType.DMA((5,)),
        ],
        compiler_params=pltpu.CompilerParams(
            collective_id=0, has_side_effects=True, vmem_limit_bytes=32 * 1024 * 1024
        ),
    )(trace, step_coeff, pair_coeff, challenges, *constants)
    return extension, values, quotient.reshape(2, 1, SEG * LANES)


def solution(mesh):
    placed = (P("col", None, "row"), P("col"), P("col"), P("col"))
    return jax.shard_map(
        shards,
        mesh=mesh,
        in_specs=placed,
        out_specs=(P(None, "col", None, "row"), P(None, None, "row"), P(None, "row", None)),
        check_vma=False,
    )
```

```python
import math

import jax
import jax.numpy as jnp
import numpy as np
from jax import lax
from jax.experimental import pallas as pl
from jax.experimental.pallas import tpu as pltpu
from jax.sharding import PartitionSpec as P

SEG = 64
COLS = 8
PAIRS = 4
RUN = 32
LANES = 128
TRACE_LEN = SEG * SEG * RUN
COSET_LEN = 4 * TRACE_LEN
MESH = pl.DeviceIdType.MESH
F32 = jnp.float32
BF16 = jnp.bfloat16


def halves(matrix):
    high = matrix.astype(BF16)
    low = (matrix - high.astype(np.float64)).astype(BF16)
    return np.stack([high, low])


def complex_rows(angle):
    return np.stack([np.cos(angle), np.sin(angle)])


def real_form(angle, out_order, in_order):
    cosine, sine = np.cos(angle), np.sin(angle)
    grid = np.stack([np.stack([cosine, -sine]), np.stack([sine, cosine])])
    places = {"co": (0, 2), "oc": (2, 0), "ci": (1, 3), "ic": (3, 1)}
    rows, cols = angle.shape
    return grid.transpose(places[out_order] + places[in_order]).reshape(2 * rows, 2 * cols)


def build_tables():
    tau = 2.0 * np.pi
    seg = np.arange(SEG)
    run = np.arange(RUN)
    first = real_form(tau * np.outer(seg, seg) / SEG, "oc", "ci")
    middle = []
    vectors = []
    lane = np.arange(LANES)
    offset = lane // 4 + (2 * (lane % 4) + 1) / 8.0
    rim = RUN + (2 * (lane % 4) + 1) / 8.0
    rim_here = (lane >= LANES - 16).astype(np.float64)
    beta = np.tile(run, PAIRS)
    for u in range(SEG):
        angle = tau * np.outer(SEG * seg + u, seg) / (SEG * SEG)
        matrix = real_form(angle, "co", "ic")
        middle.append(np.stack([halves(matrix), halves(matrix.T)]))
        vectors.append(
            np.concatenate(
                [
                    complex_rows(tau * beta * u / TRACE_LEN),
                    complex_rows(-tau * offset * u / TRACE_LEN),
                    complex_rows(-tau * rim * u / TRACE_LEN),
                    complex_rows(tau * (2 * lane + 1) * u / (2 * COSET_LEN)),
                ]
            )
        )
    twist_in = complex_rows(tau * beta * (64 * seg[:, None] - 2048) / TRACE_LEN)
    twist_out = complex_rows(-tau * offset * (64 * seg[:, None] - 2048) / TRACE_LEN) / TRACE_LEN
    twist_rim = (
        complex_rows(-tau * rim * (64 * seg[:, None] - 2048) / TRACE_LEN) / TRACE_LEN * rim_here
    )
    twist_quot = complex_rows(
        tau * (2 * lane + 1) * (64 * seg[:, None]) / (2 * COSET_LEN)
    ) / math.sqrt(COSET_LEN)
    twists = np.concatenate([twist_in, twist_out, twist_rim, twist_quot])
    spread = np.zeros((PAIRS, RUN, 5, LANES))
    mean = np.zeros((PAIRS, RUN, LANES))
    for j in range(PAIRS):
        spread[j, :, j, :] = 1.0 / np.sin(np.pi * (offset[None, :] - run[:, None]) / RUN)
        own = (lane >= LANES - 16) & ((lane - (LANES - 16)) // 4 == j)
        spread[j, :, 4, :] = own / np.sin(np.pi * (rim[None, :] - run[:, None]) / RUN)
        mean[j, :, j] = 1.0 / TRACE_LEN
    spread = spread.reshape(LANES, 5 * LANES)
    half = np.arange(SEG)
    order = np.concatenate([2 * half, 2 * half + 1])
    last = real_form(tau * np.outer(order, 2 * lane + 1) / 256.0, "co", "ci")
    shape = (2 * (lane % 4) + 1) / 8.0
    gain = np.exp(-1j * np.pi * shape) * np.sin(np.pi * shape)
    vanish = 1.0 / (np.exp(-1j * np.pi * (2 * (lane % 4) + 1) / 4.0) - 1.0)
    scales = []
    for value in (gain, gain * vanish, gain * gain * vanish):
        scales += [value.real, value.imag]
    scales += [np.zeros(LANES)] * 2
    return {
        "vectors": np.stack(vectors).astype(np.float32),
        "middle": np.stack(middle),
        "first": np.stack([halves(first), halves(first.T)]),
        "twists": twists.astype(np.float32),
        "spread": halves(spread),
        "mean": mean.reshape(LANES, LANES).astype(BF16),
        "last": halves(last),
        "scales": np.stack(scales).astype(np.float32),
    }


def parts_of(value):
    high = value.astype(BF16)
    low = (value - high.astype(F32)).astype(BF16)
    return high, low


def left_dot(table, value):
    high, low = parts_of(value)
    left = jnp.concatenate([table[0], table[0], table[1]], axis=1)
    right = jnp.concatenate([high, low, high], axis=0)
    return jnp.dot(left, right, preferred_element_type=F32)


def left_dot_turned(table, value):
    high, low = parts_of(value)
    return lax.dot_general(
        jnp.concatenate([table[0], table[0], table[1]], axis=1),
        jnp.concatenate([high, low, high], axis=1),
        (((1,), (1,)), ((), ())),
        preferred_element_type=F32,
    )


def right_dot(value, table):
    high, low = parts_of(value)
    left = jnp.concatenate([high, low, high], axis=1)
    right = jnp.concatenate([table[0], table[0], table[1]], axis=0)
    return jnp.dot(left, right, preferred_element_type=F32)


def ring_step(k, me):
    yi, xi, zi = k & 7, (k >> 3) & 3, k >> 5
    half = (yi + 1) >> 1
    dy = 4 + half * (1 - 2 * (yi & 1))
    dx = (xi ^ (xi >> 1)) ^ 2
    dz = 1 - zi
    return ((me + 8 * dy) & 56) | ((me + 2 * dx) & 6) | ((me ^ dz) & 1)


def turn(real, imag, cosine, sine):
    return real * cosine - imag * sine, real * sine + imag * cosine


def kernel(
    trace_hbm, step_hbm, pair_hbm, chal_hbm,
    vectors_hbm, middle_hbm, first_hbm, twists_hbm, spread_hbm, mean_hbm, last_hbm, scales_hbm,
    ext, val, quot,
    trace, vectors, middle, first, twists, spread, mean, last, scales,
    step_ref, pair_ref, chal_ref,
    send1, recv1, send2, recv2, send3, recv3, send4, recv4, send5, recv5, send6, recv6,
    load_sems, send_sems, recv_sems,
):
    me = lax.axis_index("row")
    col = lax.axis_index("col")

    barrier = pltpu.get_barrier_semaphore()

    def greet_row(k, carry):
        pl.semaphore_signal(
            barrier, inc=1, device_id={"row": ring_step(k, me)}, device_id_type=MESH
        )
        return carry

    def greet_col(k, carry):
        pl.semaphore_signal(
            barrier, inc=1, device_id={"col": (col + k) & 7}, device_id_type=MESH
        )
        return carry

    lax.fori_loop(0, SEG - 1, greet_row, 0)
    lax.fori_loop(1, COLS, greet_col, 0)

    loads = [
        pltpu.make_async_copy(src, dst, load_sems.at[i])
        for i, (src, dst) in enumerate(
            [
                (trace_hbm, trace),
                (first_hbm, first),
                (vectors_hbm.at[me], vectors),
                (middle_hbm.at[me], middle),
                (twists_hbm, twists),
                (spread_hbm, spread),
                (mean_hbm, mean),
                (scales_hbm, scales),
                (last_hbm, last),
                (step_hbm, step_ref),
                (pair_hbm, pair_ref),
                (chal_hbm, chal_ref),
            ]
        )
    ]
    for load in loads:
        load.start()

    loads[0].wait()
    loads[1].wait()
    grid = jnp.concatenate(
        [
            jnp.concatenate([trace[2 * j + c] for j in range(PAIRS)], axis=0)
            for c in range(2)
        ],
        axis=1,
    )
    head = left_dot_turned(first[0], grid)
    send1[...] = head.reshape(SEG, 2, LANES)
    recv1[me] = send1[me]
    pl.semaphore_wait(barrier, SEG - 1 + COLS - 1)

    def post1(k, carry):
        peer = ring_step(k, me)
        pltpu.make_async_remote_copy(
            src_ref=send1.at[peer], dst_ref=recv1.at[me],
            send_sem=send_sems.at[0], recv_sem=recv_sems.at[0],
            device_id={"row": peer}, device_id_type=MESH,
        ).start()
        return carry

    lax.fori_loop(0, SEG - 1, post1, 0)

    for load in loads[2:]:
        load.wait()
    head_high, head_low = parts_of(head[:8])
    sums = jnp.dot(head_high, mean[...], preferred_element_type=F32) + jnp.dot(
        head_low, mean[...], preferred_element_type=F32
    )
    parity = lax.broadcasted_iota(jnp.int32, (LANES, LANES), 0) % 2
    sums = jnp.where(parity == 0, sums[0:1], sums[1:2])

    def table(index, row):
        base = twists[2 * index], twists[2 * index + 1]
        return turn(*base, vectors[2 * row : 2 * row + 1], vectors[2 * row + 1 : 2 * row + 2])

    in_cos, in_sin = table(0, 0)
    out_cos, out_sin = table(1, 1)
    rim_cos, rim_sin = table(2, 2)

    pltpu.make_async_copy(
        recv1.at[pl.ds(0, SEG - 1)], recv1.at[pl.ds(0, SEG - 1)], recv_sems.at[0]
    ).wait()

    mixed = left_dot(middle[0], recv1[...].reshape(LANES, LANES))
    real, imag = turn(mixed[:SEG], mixed[SEG:], in_cos, in_sin)
    wide = right_dot(jnp.concatenate([real, imag], axis=0), spread)
    pieces = []
    for j in range(5):
        cosine, sine = (out_cos, out_sin) if j < 4 else (rim_cos, rim_sin)
        part = wide[:, LANES * j : LANES * (j + 1)]
        real, imag = turn(part[:SEG], part[SEG:], cosine, sine)
        pieces.append(jnp.concatenate([real, imag], axis=0))
    back = left_dot(middle[1], jnp.concatenate(pieces, axis=1))
    for j in range(5):
        part = back[:, LANES * j : LANES * (j + 1)]
        if j == 4:
            part = part + sums
        send2[j] = part.reshape(SEG, 2, LANES)
    for j in range(5):
        recv2[j, me] = send2[j, me]

    def post2(k, carry):
        peer = ring_step(k, me)
        pltpu.make_async_remote_copy(
            src_ref=send2.at[:, peer], dst_ref=recv2.at[:, me],
            send_sem=send_sems.at[1], recv_sem=recv_sems.at[1],
            device_id={"row": peer}, device_id_type=MESH,
        ).start()
        return carry

    lax.fori_loop(0, SEG - 1, post2, 0)
    quot_cos, quot_sin = table(3, 3)
    pltpu.make_async_copy(
        recv2.at[:, pl.ds(0, SEG - 1)], recv2.at[:, pl.ds(0, SEG - 1)], recv_sems.at[1]
    ).wait()

    arrived = jnp.concatenate([recv2[j].reshape(LANES, LANES) for j in range(5)], axis=1)
    field = left_dot(first[1], arrived)

    def scale(row):
        return scales[2 * row : 2 * row + 1], scales[2 * row + 1 : 2 * row + 2]

    rim_part = field[:, 4 * LANES :]
    lane = lax.broadcasted_iota(jnp.int32, (SEG, LANES), 1)
    gain_real, gain_imag = scale(0)
    ahead = jnp.zeros((SEG, LANES), F32)
    own = jnp.zeros((SEG, LANES), F32)
    product = jnp.zeros((SEG, LANES), F32)
    cross = jnp.zeros((SEG, LANES), F32)
    rim_weight = [jnp.zeros((SEG, LANES), F32)] * 2
    level_ahead = jnp.zeros((1, 1), F32)
    level_own = jnp.zeros((1, 1), F32)
    level_product = jnp.zeros((1, 1), F32)
    for j in range(PAIRS):
        mean_c = rim_part[0:1, j : j + 1]
        mean_d = rim_part[SEG : SEG + 1, j : j + 1]
        chal_c, chal_d = chal_ref[2 * j], chal_ref[2 * j + 1]
        step_c, step_d = chal_c * step_ref[2 * j], chal_d * step_ref[2 * j + 1]
        weight = chal_c * pair_ref[2 * j] + chal_d * pair_ref[2 * j + 1]
        raw_c = field[:SEG, LANES * j : LANES * (j + 1)]
        raw_d = field[SEG:, LANES * j : LANES * (j + 1)]
        real_c = raw_c + mean_d
        real_d = raw_d - mean_c
        ext[0, 2 * j] = gain_real * real_c - gain_imag * mean_c
        ext[1, 2 * j] = gain_imag * real_c + gain_real * mean_c
        ext[0, 2 * j + 1] = gain_real * real_d - gain_imag * mean_d
        ext[1, 2 * j + 1] = gain_imag * real_d + gain_real * mean_d
        ahead += chal_c * raw_c + chal_d * raw_d
        own += step_c * real_c + step_d * real_d
        product += weight * (real_c * real_d)
        cross += weight * (real_c * mean_d + real_d * mean_c)
        group = (lane >= LANES - 16 + 4 * j) & (lane < LANES - 12 + 4 * j)
        rim_weight = [
            jnp.where(group, chal_c, rim_weight[0]),
            jnp.where(group, chal_d, rim_weight[1]),
        ]
        level_ahead += chal_c * mean_d - chal_d * mean_c
        level_own += (chal_c - step_c) * mean_c + (chal_d - step_d) * mean_d
        level_product += weight * (mean_c * mean_d)
    rim_sum = rim_part[:SEG] * rim_weight[0] + rim_part[SEG:] * rim_weight[1]
    rim_sum = rim_sum + pltpu.roll(rim_sum, 4, 1)
    rim_sum = rim_sum + pltpu.roll(rim_sum, 8, 1)
    ahead = jnp.where(lane < LANES - 4, pltpu.roll(ahead, LANES - 4, 1), rim_sum)
    line_real = ahead + level_ahead - own
    line_imag = level_own
    square_real = product - level_product
    square_imag = cross
    line_scale, square_scale = scale(1), scale(2)
    value_real = (
        line_scale[0] * line_real
        - line_scale[1] * line_imag
        - square_scale[0] * square_real
        + square_scale[1] * square_imag
    )
    value_imag = (
        line_scale[0] * line_imag
        + line_scale[1] * line_real
        - square_scale[0] * square_imag
        - square_scale[1] * square_real
    )
    mixed = left_dot(first[0], jnp.concatenate([value_real, value_imag], axis=0))
    for i in range(COLS):
        send3[i] = mixed[16 * i : 16 * (i + 1)]
        send6[i, 0:8] = value_real[8 * i : 8 * (i + 1)]
        send6[i, 8:16] = value_imag[8 * i : 8 * (i + 1)]

    def post3(k, carry):
        peer = (col + k) & 7
        pltpu.make_async_remote_copy(
            src_ref=send3.at[peer], dst_ref=recv3.at[col],
            send_sem=send_sems.at[2], recv_sem=recv_sems.at[2],
            device_id={"col": peer}, device_id_type=MESH,
        ).start()
        return carry

    lax.fori_loop(1, COLS, post3, 0)

    def post6(k, carry):
        peer = (col + k) & 7
        pltpu.make_async_remote_copy(
            src_ref=send6.at[peer], dst_ref=recv6.at[col],
            send_sem=send_sems.at[5], recv_sem=recv_sems.at[5],
            device_id={"col": peer}, device_id_type=MESH,
        ).start()
        return carry

    lax.fori_loop(1, COLS, post6, 0)
    recv3[col] = send3[col]
    recv6[col] = send6[col]
    pltpu.make_async_copy(
        recv3.at[pl.ds(0, COLS - 1)], recv3.at[pl.ds(0, COLS - 1)], recv_sems.at[2]
    ).wait()
    total = recv3[0]
    for i in range(1, COLS):
        total = total + recv3[i]
    send4[...] = total.reshape(8, 2, LANES)

    here = (me >> 3) == col

    def post4(k, carry):
        line = (k + me) & 7
        across = ((k >> 3) + col) & 7
        target = col * COLS + line
        alone = (target == me) & (across == col)

        @pl.when(jnp.logical_not(alone))
        def _():
            pltpu.make_async_remote_copy(
                src_ref=send4.at[line], dst_ref=recv4.at[me],
                send_sem=send_sems.at[3], recv_sem=recv_sems.at[3],
                device_id={"col": across, "row": target}, device_id_type=MESH,
            ).start()

        @pl.when(alone)
        def _():
            pltpu.make_async_copy(send4.at[line], recv4.at[me], recv_sems.at[3]).start()

        return carry

    lax.fori_loop(0, SEG, post4, 0)

    pltpu.make_async_copy(
        recv6.at[pl.ds(0, COLS - 1)], recv6.at[pl.ds(0, COLS - 1)], recv_sems.at[5]
    ).wait()
    value = recv6[0]
    for i in range(1, COLS):
        value = value + recv6[i]
    send5[...] = value

    def post5(k, carry):
        pltpu.make_async_remote_copy(
            src_ref=send5, dst_ref=recv5.at[col],
            send_sem=send_sems.at[4], recv_sem=recv_sems.at[4],
            device_id={"col": (col + k) & 7}, device_id_type=MESH,
        ).start()
        return carry

    lax.fori_loop(1, COLS, post5, 0)
    recv5[col] = send5[...]

    pltpu.make_async_copy(recv4, recv4, recv_sems.at[3]).wait()
    mixed = left_dot(middle[0], recv4[...].reshape(LANES, LANES))
    real, imag = turn(mixed[:SEG], mixed[SEG:], quot_cos, quot_sin)
    both = jnp.concatenate([real, imag], axis=1)
    both = jnp.concatenate([both, both], axis=0)
    result = left_dot_turned(last, both)
    for c in range(2):
        even = result[LANES * c : LANES * c + SEG]
        odd = result[LANES * c + SEG : LANES * (c + 1)]
        quot[c] = jnp.where(lane < SEG, even, odd)

    pltpu.make_async_copy(
        recv5.at[pl.ds(0, COLS - 1)], recv5.at[pl.ds(0, COLS - 1)], recv_sems.at[4]
    ).wait()
    for i in range(COLS):
        val[0, 8 * i : 8 * (i + 1)] = recv5[i, 0:8]
        val[1, 8 * i : 8 * (i + 1)] = recv5[i, 8:16]

    pltpu.make_async_copy(
        send1.at[pl.ds(0, SEG - 1)], send1.at[pl.ds(0, SEG - 1)], send_sems.at[0]
    ).wait()
    pltpu.make_async_copy(
        send2.at[:, pl.ds(0, SEG - 1)], send2.at[:, pl.ds(0, SEG - 1)], send_sems.at[1]
    ).wait()
    pltpu.make_async_copy(
        send3.at[pl.ds(0, COLS - 1)], send3.at[pl.ds(0, COLS - 1)], send_sems.at[2]
    ).wait()

    @pl.when(here)
    def _():
        pltpu.make_async_copy(
            recv4.at[pl.ds(0, SEG - 1)], recv4.at[pl.ds(0, SEG - 1)], send_sems.at[3]
        ).wait()

    @pl.when(jnp.logical_not(here))
    def _():
        pltpu.make_async_copy(recv4, recv4, send_sems.at[3]).wait()

    for i in (4, 5):
        pltpu.make_async_copy(
            recv5.at[pl.ds(0, COLS - 1)], recv5.at[pl.ds(0, COLS - 1)], send_sems.at[i]
        ).wait()


def carry_out(ext, val, quot, ext_out, val_out, quot_out, sems):
    moves = [
        pltpu.make_async_copy(src, dst, sems.at[i])
        for i, (src, dst) in enumerate([(ext, ext_out), (val, val_out), (quot, quot_out)])
    ]
    for move in moves:
        move.start()
    for move in moves:
        move.wait()


def shards(trace, step_coeff, pair_coeff, challenges):
    trace = trace.transpose(0, 2, 1)
    tables = build_tables()
    names = ["vectors", "middle", "first", "twists", "spread", "mean", "last", "scales"]
    constants = [jnp.asarray(tables[name]) for name in names]
    operands = [
        pltpu.with_memory_space_constraint(x, pltpu.HBM)
        for x in (trace, step_coeff, pair_coeff, challenges, *constants)
    ]
    vmem = pltpu.VMEM
    hbm = pl.BlockSpec(memory_space=pltpu.HBM)
    inside = pl.BlockSpec(memory_space=pltpu.VMEM)
    outs = (
        jax.ShapeDtypeStruct((2, COLS, SEG, LANES), F32),
        jax.ShapeDtypeStruct((2, SEG, LANES), F32),
        jax.ShapeDtypeStruct((2, SEG, LANES), F32),
    )
    tables_scratch = [
        vmem(c.shape[1:] if n in ("vectors", "middle") else c.shape, c.dtype)
        for n, c in zip(names, constants, strict=True)
    ]
    extension, values, quotient = pl.pallas_call(
        kernel,
        out_shape=tuple(vmem(o.shape, F32) for o in outs),
        in_specs=[hbm] * (4 + len(constants)),
        out_specs=(inside,) * 3,
        scratch_shapes=[
            vmem(trace.shape, F32),
            *tables_scratch,
            *[pltpu.SMEM((COLS,), F32)] * 3,
            vmem((SEG, 2, LANES), F32),
            vmem((SEG, 2, LANES), F32),
            vmem((5, SEG, 2, LANES), F32),
            vmem((5, SEG, 2, LANES), F32),
            vmem((COLS, 16, LANES), F32),
            vmem((COLS, 16, LANES), F32),
            vmem((8, 2, LANES), F32),
            vmem((SEG, 2, LANES), F32),
            vmem((16, LANES), F32),
            vmem((COLS, 16, LANES), F32),
            vmem((COLS, 16, LANES), F32),
            vmem((COLS, 16, LANES), F32),
            pltpu.SemaphoreType.DMA((12,)),
            pltpu.SemaphoreType.DMA((6,)),
            pltpu.SemaphoreType.DMA((6,)),
        ],
        compiler_params=pltpu.CompilerParams(
            collective_id=0, has_side_effects=True, vmem_limit_bytes=32 * 1024 * 1024
        ),
    )(*operands)
    extension, values, quotient = pl.pallas_call(
        carry_out,
        out_shape=outs,
        in_specs=[inside] * 3,
        out_specs=(hbm,) * 3,
        scratch_shapes=[pltpu.SemaphoreType.DMA((3,))],
    )(*[pltpu.with_memory_space_constraint(x, vmem) for x in (extension, values, quotient)])
    return extension, values, quotient.reshape(2, 1, SEG * LANES)


def solution(mesh):
    placed = (P("col", None, "row"), P("col"), P("col"), P("col"))
    return jax.shard_map(
        shards,
        mesh=mesh,
        in_specs=placed,
        out_specs=(P(None, "col", None, "row"), P(None, None, "row"), P(None, "row", None)),
        check_vma=False,
    )
```

```python
import math

import jax
import jax.numpy as jnp
import numpy as np
from jax import lax
from jax.experimental import pallas as pl
from jax.experimental.pallas import tpu as pltpu
from jax.sharding import PartitionSpec as P

SEG = 64
HALF = 32
COLS = 8
PAIRS = 4
RUN = 32
LANES = 128
TRACE_LEN = SEG * SEG * RUN
COSET_LEN = 4 * TRACE_LEN
MESH = pl.DeviceIdType.MESH
F32 = jnp.float32
BF16 = jnp.bfloat16


def halves(matrix):
    high = matrix.astype(BF16)
    low = (matrix - high.astype(np.float64)).astype(BF16)
    return np.stack([high, low])


def complex_rows(angle):
    return np.stack([np.cos(angle), np.sin(angle)])


def real_form(angle, out_order, in_order):
    cosine, sine = np.cos(angle), np.sin(angle)
    grid = np.stack([np.stack([cosine, -sine]), np.stack([sine, cosine])])
    places = {"co": (0, 2), "oc": (2, 0), "ci": (1, 3), "ic": (3, 1)}
    rows, cols = angle.shape
    return grid.transpose(places[out_order] + places[in_order]).reshape(2 * rows, 2 * cols)


def build_tables():
    tau = 2.0 * np.pi
    seg = np.arange(SEG)
    run = np.arange(RUN)
    first = real_form(tau * np.outer(seg, seg) / SEG, "oc", "ci")
    final = first.T.reshape(2 * SEG, SEG // 2, 2, 2).transpose(0, 2, 1, 3).reshape(2 * SEG, 2 * SEG)
    lane = np.arange(LANES)
    offset = lane // 4 + (2 * (lane % 4) + 1) / 8.0
    rim = RUN + (2 * (lane % 4) + 1) / 8.0
    rim_here = (lane >= LANES - 16).astype(np.float64)
    beta = np.tile(run, PAIRS)
    slots = np.concatenate([seg[0::2], seg[1::2]])
    matrices = []
    vectors = []
    for u in range(SEG):
        angle = tau * np.outer(SEG * seg + u, slots) / (SEG * SEG)
        matrices.append(real_form(angle, "co", "ic"))
        vectors.append(
            np.concatenate(
                [
                    complex_rows(tau * beta * u / TRACE_LEN),
                    complex_rows(-tau * offset * u / TRACE_LEN),
                    complex_rows(-tau * rim * u / TRACE_LEN),
                    complex_rows(tau * (2 * lane + 1) * u / (2 * COSET_LEN)),
                ]
            )
        )
    into, outof, turns = [], [], []
    for g in range(HALF):
        pair = (2 * g, 2 * g + 1)
        into.append(np.stack([halves(matrices[u]) for u in pair]))
        for zh in range(2):
            rows = slice(SEG * zh, SEG * (zh + 1))
            outof.append(np.stack([halves(matrices[u].T[rows]) for u in pair]))
            turns.append(np.concatenate([vectors[u][:6] for u in pair] + [vectors[2 * g + zh][6:]]))
    vectors = np.pad(np.stack(turns), ((0, 0), (0, 2), (0, 0)))
    twist_in = complex_rows(tau * beta * (64 * seg[:, None] - 2048) / TRACE_LEN)
    twist_out = complex_rows(-tau * offset * (64 * seg[:, None] - 2048) / TRACE_LEN) / TRACE_LEN
    twist_rim = (
        complex_rows(-tau * rim * (64 * seg[:, None] - 2048) / TRACE_LEN) / TRACE_LEN * rim_here
    )
    twist_quot = complex_rows(
        tau * (2 * lane + 1) * (64 * seg[:, None]) / (2 * COSET_LEN)
    ) / math.sqrt(COSET_LEN)
    twists = np.concatenate([twist_in, twist_out, twist_rim, twist_quot])
    spread = np.zeros((PAIRS, RUN, 5, LANES))
    mean = np.zeros((PAIRS, RUN, LANES))
    for j in range(PAIRS):
        spread[j, :, j, :] = 1.0 / np.sin(np.pi * (offset[None, :] - run[:, None]) / RUN)
        own = (lane >= LANES - 16) & ((lane - (LANES - 16)) // 4 == j)
        spread[j, :, 4, :] = own / np.sin(np.pi * (rim[None, :] - run[:, None]) / RUN)
        mean[j, :, j] = 1.0 / TRACE_LEN
    spread = spread.reshape(LANES, 5 * LANES)
    half = np.arange(SEG)
    order = np.concatenate([2 * half, 2 * half + 1])
    last = real_form(tau * np.outer(order, 2 * lane + 1) / 256.0, "co", "ci")
    shape = (2 * (lane % 4) + 1) / 8.0
    gain = np.exp(-1j * np.pi * shape) * np.sin(np.pi * shape)
    vanish = 1.0 / (np.exp(-1j * np.pi * (2 * (lane % 4) + 1) / 4.0) - 1.0)
    scales = []
    for value in (gain, gain * vanish, gain * gain * vanish):
        scales += [value.real, value.imag]
    scales += [np.zeros(LANES)] * 2
    return {
        "vectors": vectors.astype(np.float32),
        "into": np.stack(into),
        "outof": np.stack(outof),
        "first": np.stack([halves(first), halves(final)]),
        "twists": twists.astype(np.float32),
        "spread": halves(spread),
        "mean": mean.reshape(LANES, LANES).astype(BF16),
        "last": halves(last),
        "scales": np.stack(scales).astype(np.float32),
    }


def parts_of(value):
    high = value.astype(BF16)
    low = (value - high.astype(F32)).astype(BF16)
    return high, low


def left_dot(table, value):
    high, low = parts_of(value)
    left = jnp.concatenate([table[0], table[0], table[1]], axis=1)
    right = jnp.concatenate([high, low, high], axis=0)
    return jnp.dot(left, right, preferred_element_type=F32)


def left_dot_turned(table, value):
    high, low = parts_of(value)
    return lax.dot_general(
        jnp.concatenate([table[0], table[0], table[1]], axis=1),
        jnp.concatenate([high, low, high], axis=1),
        (((1,), (1,)), ((), ())),
        preferred_element_type=F32,
    )


def right_dot(value, table):
    high, low = parts_of(value)
    left = jnp.concatenate([high, low, high], axis=1)
    right = jnp.concatenate([table[0], table[0], table[1]], axis=0)
    return jnp.dot(left, right, preferred_element_type=F32)


def ring_step(k, me):
    yi, xi, zi = k & 7, (k >> 3) & 3, k >> 5
    half = (yi + 1) >> 1
    dy = 4 + half * (1 - 2 * (yi & 1))
    dx = (xi ^ (xi >> 1)) ^ 2
    dz = 1 - zi
    return ((me + 8 * dy) & 56) | ((me + 2 * dx) & 6) | ((me ^ dz) & 1)


def turn(real, imag, cosine, sine):
    return real * cosine - imag * sine, real * sine + imag * cosine


def kernel(
    trace_hbm, step_hbm, pair_hbm, chal_hbm,
    vectors_hbm, into_hbm, outof_hbm, first_hbm, twists_hbm, spread_hbm, mean_hbm, last_hbm, scales_hbm,
    ext, val, quot,
    trace, vectors, into, outof, first, twists, spread, mean, last, scales,
    step_ref, pair_ref, chal_ref,
    send1, recv1, send2, recv2, send3, recv3, send4, recv4, send5, recv5, send6, recv6,
    load_sems, send_sems, recv_sems, ready,
):
    me = lax.axis_index("row")
    col = lax.axis_index("col")
    group, far = me >> 1, me & 1
    slot = HALF * far + group

    barrier = pltpu.get_barrier_semaphore()

    def greet_row(k, carry):
        pl.semaphore_signal(
            barrier, inc=1, device_id={"row": ring_step(k, me)}, device_id_type=MESH
        )
        return carry

    def greet_col(k, carry):
        pl.semaphore_signal(
            barrier, inc=1, device_id={"col": (col + k) & 7}, device_id_type=MESH
        )
        return carry

    @pl.when(far == 0)
    def _():
        lax.fori_loop(0, HALF, greet_row, 0)

    lax.fori_loop(HALF, SEG - 1, greet_row, 0)
    lax.fori_loop(1, COLS, greet_col, 0)

    loads = [
        pltpu.make_async_copy(src, dst, load_sems.at[i])
        for i, (src, dst) in enumerate(
            [
                (trace_hbm, trace),
                (first_hbm, first),
                (vectors_hbm.at[me], vectors),
                (into_hbm.at[group], into),
                (outof_hbm.at[me], outof),
                (twists_hbm, twists),
                (spread_hbm, spread),
                (mean_hbm, mean),
                (scales_hbm, scales),
                (last_hbm, last),
                (step_hbm, step_ref),
                (pair_hbm, pair_ref),
                (chal_hbm, chal_ref),
            ]
        )
    ]
    for load in loads:
        load.start()

    loads[0].wait()
    loads[1].wait()
    grid = jnp.concatenate(
        [
            jnp.concatenate([trace[2 * j + c] for j in range(PAIRS)], axis=0)
            for c in range(2)
        ],
        axis=1,
    )
    head = left_dot_turned(first[0], grid)
    send1[...] = head.reshape(SEG, 2, LANES)
    for c in range(2):
        recv1[c, slot] = send1[2 * group + c]
    pl.semaphore_wait(barrier, HALF - 1 + COLS - 1 + HALF * far)

    def post1(k, to):
        peer = ring_step(k, me)
        pltpu.make_async_remote_copy(
            src_ref=send1.at[pl.ds(2 * (peer >> 1), 2)], dst_ref=recv1.at[:, slot],
            send_sem=send_sems.at[to], recv_sem=recv_sems.at[to],
            device_id={"row": peer}, device_id_type=MESH,
        ).start()
        return to

    @pl.when(far == 1)
    def _():
        pl.semaphore_signal(ready, inc=1, device_id={"row": me ^ 1}, device_id_type=MESH)
        lax.fori_loop(0, HALF, post1, 6)

    lax.fori_loop(HALF, SEG - 1, post1, 0)

    for load in loads[2:]:
        load.wait()
    def table(index, row):
        base = twists[2 * index], twists[2 * index + 1]
        return turn(*base, vectors[2 * row : 2 * row + 1], vectors[2 * row + 1 : 2 * row + 2])

    turn_in = [table(0, 3 * c) for c in range(2)]
    turn_out = [table(1, 3 * c + 1) for c in range(2)]
    turn_rim = [table(2, 3 * c + 2) for c in range(2)]

    own_half = recv1.at[:, pl.ds(0, HALF - 1)]
    pltpu.make_async_copy(own_half, own_half, recv_sems.at[0]).wait()
    gathered = recv1.at[:, pl.ds(0, HALF)]

    @pl.when(far == 0)
    def _():
        pl.semaphore_wait(ready, 1)
        pltpu.make_async_remote_copy(
            src_ref=gathered, dst_ref=gathered,
            send_sem=send_sems.at[6], recv_sem=recv_sems.at[6],
            device_id={"row": me ^ 1}, device_id_type=MESH,
        ).start()

    pltpu.make_async_copy(gathered, gathered, recv_sems.at[6]).wait()

    rows = []
    for c in range(2):
        mixed = left_dot(into[c], recv1[c].reshape(LANES, LANES))
        if c == 0:
            lowest = jnp.concatenate([mixed[0:8], mixed[SEG : SEG + 8]], axis=0)
        rows += turn(mixed[:SEG], mixed[SEG:], *turn_in[c])
    wide = right_dot(jnp.concatenate(rows, axis=0), spread)
    high, low = parts_of(lowest)
    sums = jnp.dot(high, mean[...], preferred_element_type=F32) + jnp.dot(
        low, mean[...], preferred_element_type=F32
    )
    sums = sums * jnp.where(group == 0, 1.0, 0.0).astype(F32)
    parity = lax.broadcasted_iota(jnp.int32, (SEG, LANES), 0) % 2
    sums = jnp.where(parity == 0, sums[0:1], sums[8:9])
    for c in range(2):
        pieces = []
        for j in range(5):
            part = wide[LANES * c : LANES * (c + 1), LANES * j : LANES * (j + 1)]
            real, imag = turn(part[:SEG], part[SEG:], *(turn_out[c] if j < 4 else turn_rim[c]))
            pieces.append(jnp.concatenate([real, imag], axis=0))
        back = left_dot(outof[c], jnp.concatenate(pieces, axis=1))
        for j in range(5):
            part = back[:, LANES * j : LANES * (j + 1)]
            if j == 4 and c == 0:
                part = part + sums
            send2[2 * j + c] = part.reshape(HALF, 2, LANES)
    for i in range(10):
        recv2[i, group] = send2[i, group]

    def post2(k, carry):
        peer = ring_step(k, me)
        pltpu.make_async_remote_copy(
            src_ref=send2.at[:, peer >> 1], dst_ref=recv2.at[:, group],
            send_sem=send_sems.at[1], recv_sem=recv_sems.at[1],
            device_id={"row": peer}, device_id_type=MESH,
        ).start()
        return carry

    lax.fori_loop(HALF, SEG - 1, post2, 0)
    quot_cos, quot_sin = table(3, 6)
    others = recv2.at[:, pl.ds(0, HALF - 1)]
    pltpu.make_async_copy(others, others, recv_sems.at[1]).wait()

    arrived = jnp.concatenate(
        [
            jnp.concatenate([recv2[2 * j + c].reshape(SEG, LANES) for c in range(2)], axis=0)
            for j in range(5)
        ],
        axis=1,
    )
    field = left_dot(first[1], arrived)

    def scale(row):
        return scales[2 * row : 2 * row + 1], scales[2 * row + 1 : 2 * row + 2]

    rim_part = field[:, 4 * LANES :]
    lane = lax.broadcasted_iota(jnp.int32, (SEG, LANES), 1)
    gain_real, gain_imag = scale(0)
    ahead = jnp.zeros((SEG, LANES), F32)
    own = jnp.zeros((SEG, LANES), F32)
    product = jnp.zeros((SEG, LANES), F32)
    cross = jnp.zeros((SEG, LANES), F32)
    rim_weight = [jnp.zeros((SEG, LANES), F32)] * 2
    level_ahead = jnp.zeros((1, 1), F32)
    level_own = jnp.zeros((1, 1), F32)
    level_product = jnp.zeros((1, 1), F32)
    for j in range(PAIRS):
        mean_c = rim_part[0:1, j : j + 1]
        mean_d = rim_part[SEG : SEG + 1, j : j + 1]
        chal_c, chal_d = chal_ref[2 * j], chal_ref[2 * j + 1]
        step_c, step_d = chal_c * step_ref[2 * j], chal_d * step_ref[2 * j + 1]
        weight = chal_c * pair_ref[2 * j] + chal_d * pair_ref[2 * j + 1]
        raw_c = field[:SEG, LANES * j : LANES * (j + 1)]
        raw_d = field[SEG:, LANES * j : LANES * (j + 1)]
        real_c = raw_c + mean_d
        real_d = raw_d - mean_c
        ext[0, 2 * j] = gain_real * real_c - gain_imag * mean_c
        ext[1, 2 * j] = gain_imag * real_c + gain_real * mean_c
        ext[0, 2 * j + 1] = gain_real * real_d - gain_imag * mean_d
        ext[1, 2 * j + 1] = gain_imag * real_d + gain_real * mean_d
        ahead += chal_c * raw_c + chal_d * raw_d
        own += step_c * real_c + step_d * real_d
        product += weight * (real_c * real_d)
        cross += weight * (real_c * mean_d + real_d * mean_c)
        group = (lane >= LANES - 16 + 4 * j) & (lane < LANES - 12 + 4 * j)
        rim_weight = [
            jnp.where(group, chal_c, rim_weight[0]),
            jnp.where(group, chal_d, rim_weight[1]),
        ]
        level_ahead += chal_c * mean_d - chal_d * mean_c
        level_own += (chal_c - step_c) * mean_c + (chal_d - step_d) * mean_d
        level_product += weight * (mean_c * mean_d)
    rim_sum = rim_part[:SEG] * rim_weight[0] + rim_part[SEG:] * rim_weight[1]
    rim_sum = rim_sum + pltpu.roll(rim_sum, 4, 1)
    rim_sum = rim_sum + pltpu.roll(rim_sum, 8, 1)
    ahead = jnp.where(lane < LANES - 4, pltpu.roll(ahead, LANES - 4, 1), rim_sum)
    line_real = ahead + level_ahead - own
    line_imag = level_own
    square_real = product - level_product
    square_imag = cross
    line_scale, square_scale = scale(1), scale(2)
    value_real = (
        line_scale[0] * line_real
        - line_scale[1] * line_imag
        - square_scale[0] * square_real
        + square_scale[1] * square_imag
    )
    value_imag = (
        line_scale[0] * line_imag
        + line_scale[1] * line_real
        - square_scale[0] * square_imag
        - square_scale[1] * square_real
    )
    mixed = left_dot(first[0], jnp.concatenate([value_real, value_imag], axis=0))
    for i in range(COLS):
        send3[i] = mixed[16 * i : 16 * (i + 1)]
        send6[i, 0:8] = value_real[8 * i : 8 * (i + 1)]
        send6[i, 8:16] = value_imag[8 * i : 8 * (i + 1)]

    def post3(k, carry):
        peer = (col + k) & 7
        pltpu.make_async_remote_copy(
            src_ref=send3.at[peer], dst_ref=recv3.at[col],
            send_sem=send_sems.at[2], recv_sem=recv_sems.at[2],
            device_id={"col": peer}, device_id_type=MESH,
        ).start()
        return carry

    lax.fori_loop(1, COLS, post3, 0)

    def post6(k, carry):
        peer = (col + k) & 7
        pltpu.make_async_remote_copy(
            src_ref=send6.at[peer], dst_ref=recv6.at[col],
            send_sem=send_sems.at[5], recv_sem=recv_sems.at[5],
            device_id={"col": peer}, device_id_type=MESH,
        ).start()
        return carry

    lax.fori_loop(1, COLS, post6, 0)
    recv3[col] = send3[col]
    recv6[col] = send6[col]
    pltpu.make_async_copy(
        recv3.at[pl.ds(0, COLS - 1)], recv3.at[pl.ds(0, COLS - 1)], recv_sems.at[2]
    ).wait()
    total = recv3[0]
    for i in range(1, COLS):
        total = total + recv3[i]
    send4[...] = total.reshape(8, 2, LANES)

    here = (me >> 3) == col

    def post4(k, carry):
        line = (k + me) & 7
        across = ((k >> 3) + col) & 7
        target = col * COLS + line
        alone = (target == me) & (across == col)

        @pl.when(jnp.logical_not(alone))
        def _():
            pltpu.make_async_remote_copy(
                src_ref=send4.at[line], dst_ref=recv4.at[slot],
                send_sem=send_sems.at[3], recv_sem=recv_sems.at[3],
                device_id={"col": across, "row": target}, device_id_type=MESH,
            ).start()

        @pl.when(alone)
        def _():
            pltpu.make_async_copy(send4.at[line], recv4.at[slot], recv_sems.at[3]).start()

        return carry

    lax.fori_loop(0, SEG, post4, 0)

    pltpu.make_async_copy(
        recv6.at[pl.ds(0, COLS - 1)], recv6.at[pl.ds(0, COLS - 1)], recv_sems.at[5]
    ).wait()
    value = recv6[0]
    for i in range(1, COLS):
        value = value + recv6[i]
    send5[...] = value

    def post5(k, carry):
        pltpu.make_async_remote_copy(
            src_ref=send5, dst_ref=recv5.at[col],
            send_sem=send_sems.at[4], recv_sem=recv_sems.at[4],
            device_id={"col": (col + k) & 7}, device_id_type=MESH,
        ).start()
        return carry

    lax.fori_loop(1, COLS, post5, 0)
    recv5[col] = send5[...]

    pltpu.make_async_copy(recv4, recv4, recv_sems.at[3]).wait()
    mixed = left_dot(into[far], recv4[...].reshape(LANES, LANES))
    real, imag = turn(mixed[:SEG], mixed[SEG:], quot_cos, quot_sin)
    both = jnp.concatenate([real, imag], axis=1)
    both = jnp.concatenate([both, both], axis=0)
    result = left_dot_turned(last, both)
    for c in range(2):
        even = result[LANES * c : LANES * c + SEG]
        odd = result[LANES * c + SEG : LANES * (c + 1)]
        quot[c] = jnp.where(lane < SEG, even, odd)

    pltpu.make_async_copy(
        recv5.at[pl.ds(0, COLS - 1)], recv5.at[pl.ds(0, COLS - 1)], recv_sems.at[4]
    ).wait()
    for i in range(COLS):
        val[0, 8 * i : 8 * (i + 1)] = recv5[i, 0:8]
        val[1, 8 * i : 8 * (i + 1)] = recv5[i, 8:16]

    pltpu.make_async_copy(own_half, own_half, send_sems.at[0]).wait()
    pltpu.make_async_copy(gathered, gathered, send_sems.at[6]).wait()
    pltpu.make_async_copy(others, others, send_sems.at[1]).wait()
    pltpu.make_async_copy(
        send3.at[pl.ds(0, COLS - 1)], send3.at[pl.ds(0, COLS - 1)], send_sems.at[2]
    ).wait()

    @pl.when(here)
    def _():
        pltpu.make_async_copy(
            recv4.at[pl.ds(0, SEG - 1)], recv4.at[pl.ds(0, SEG - 1)], send_sems.at[3]
        ).wait()

    @pl.when(jnp.logical_not(here))
    def _():
        pltpu.make_async_copy(recv4, recv4, send_sems.at[3]).wait()

    for i in (4, 5):
        pltpu.make_async_copy(
            recv5.at[pl.ds(0, COLS - 1)], recv5.at[pl.ds(0, COLS - 1)], send_sems.at[i]
        ).wait()


def carry_out(ext, val, quot, ext_out, val_out, quot_out, sems):
    moves = [
        pltpu.make_async_copy(src, dst, sems.at[i])
        for i, (src, dst) in enumerate([(ext, ext_out), (val, val_out), (quot, quot_out)])
    ]
    for move in moves:
        move.start()
    for move in moves:
        move.wait()


def shards(trace, step_coeff, pair_coeff, challenges):
    trace = trace.transpose(0, 2, 1)
    tables = build_tables()
    names = ["vectors", "into", "outof", "first", "twists", "spread", "mean", "last", "scales"]
    constants = [jnp.asarray(tables[name]) for name in names]
    operands = [
        pltpu.with_memory_space_constraint(x, pltpu.HBM)
        for x in (trace, step_coeff, pair_coeff, challenges, *constants)
    ]
    vmem = pltpu.VMEM
    hbm = pl.BlockSpec(memory_space=pltpu.HBM)
    inside = pl.BlockSpec(memory_space=pltpu.VMEM)
    outs = (
        jax.ShapeDtypeStruct((2, COLS, SEG, LANES), F32),
        jax.ShapeDtypeStruct((2, SEG, LANES), F32),
        jax.ShapeDtypeStruct((2, SEG, LANES), F32),
    )
    tables_scratch = [
        vmem(c.shape[1:] if n in ("vectors", "into", "outof") else c.shape, c.dtype)
        for n, c in zip(names, constants, strict=True)
    ]
    extension, values, quotient = pl.pallas_call(
        kernel,
        out_shape=tuple(vmem(o.shape, F32) for o in outs),
        in_specs=[hbm] * (4 + len(constants)),
        out_specs=(inside,) * 3,
        scratch_shapes=[
            vmem(trace.shape, F32),
            *tables_scratch,
            *[pltpu.SMEM((COLS,), F32)] * 3,
            vmem((SEG, 2, LANES), F32),
            vmem((2, SEG, 2, LANES), F32),
            vmem((10, HALF, 2, LANES), F32),
            vmem((10, HALF, 2, LANES), F32),
            vmem((COLS, 16, LANES), F32),
            vmem((COLS, 16, LANES), F32),
            vmem((8, 2, LANES), F32),
            vmem((SEG, 2, LANES), F32),
            vmem((16, LANES), F32),
            vmem((COLS, 16, LANES), F32),
            vmem((COLS, 16, LANES), F32),
            vmem((COLS, 16, LANES), F32),
            pltpu.SemaphoreType.DMA((13,)),
            pltpu.SemaphoreType.DMA((7,)),
            pltpu.SemaphoreType.DMA((7,)),
            pltpu.SemaphoreType.REGULAR,
        ],
        compiler_params=pltpu.CompilerParams(
            collective_id=0, has_side_effects=True, vmem_limit_bytes=32 * 1024 * 1024
        ),
    )(*operands)
    extension, values, quotient = pl.pallas_call(
        carry_out,
        out_shape=outs,
        in_specs=[inside] * 3,
        out_specs=(hbm,) * 3,
        scratch_shapes=[pltpu.SemaphoreType.DMA((3,))],
    )(*[pltpu.with_memory_space_constraint(x, vmem) for x in (extension, values, quotient)])
    return extension, values, quotient.reshape(2, 1, SEG * LANES)


def solution(mesh):
    placed = (P("col", None, "row"), P("col"), P("col"), P("col"))
    return jax.shard_map(
        shards,
        mesh=mesh,
        in_specs=placed,
        out_specs=(P(None, "col", None, "row"), P(None, None, "row"), P(None, "row", None)),
        check_vma=False,
    )
```

```python
import math

import jax
import jax.numpy as jnp
import numpy as np
from jax import lax
from jax.experimental import pallas as pl
from jax.experimental.pallas import tpu as pltpu
from jax.sharding import PartitionSpec as P

SEG = 64
HALF = 32
COLS = 8
PAIRS = 4
RUN = 32
LANES = 128
TRACE_LEN = SEG * SEG * RUN
COSET_LEN = 4 * TRACE_LEN
MESH = pl.DeviceIdType.MESH
F32 = jnp.float32
BF16 = jnp.bfloat16


def halves(matrix):
    high = matrix.astype(BF16)
    low = (matrix - high.astype(np.float64)).astype(BF16)
    return np.stack([high, low])


def complex_rows(angle):
    return np.stack([np.cos(angle), np.sin(angle)])


def real_form(angle, out_order, in_order):
    cosine, sine = np.cos(angle), np.sin(angle)
    grid = np.stack([np.stack([cosine, -sine]), np.stack([sine, cosine])])
    places = {"co": (0, 2), "oc": (2, 0), "ci": (1, 3), "ic": (3, 1)}
    rows, cols = angle.shape
    return grid.transpose(places[out_order] + places[in_order]).reshape(2 * rows, 2 * cols)


def build_tables():
    tau = 2.0 * np.pi
    seg = np.arange(SEG)
    run = np.arange(RUN)
    first = real_form(tau * np.outer(seg, seg) / SEG, "oc", "ci")
    final = first.T.reshape(2 * SEG, SEG // 2, 2, 2).transpose(0, 2, 1, 3).reshape(2 * SEG, 2 * SEG)
    lane = np.arange(LANES)
    offset = lane // 4 + (2 * (lane % 4) + 1) / 8.0
    rim = RUN + (2 * (lane % 4) + 1) / 8.0
    rim_here = (lane >= LANES - 16).astype(np.float64)
    beta = np.tile(run, PAIRS)
    deal = np.array([dealt(m, i) for i in range(COLS) for m in range(8)])
    summed = first.reshape(SEG, 2, 2 * SEG)[deal].reshape(2 * SEG, 2 * SEG)
    slots = np.concatenate([seg[0::2], seg[1::2]])
    matrices = []
    vectors = []
    for u in range(SEG):
        angle = tau * np.outer(SEG * seg + u, slots) / (SEG * SEG)
        matrices.append(real_form(angle, "co", "ic"))
        vectors.append(
            np.concatenate(
                [
                    complex_rows(tau * beta * u / TRACE_LEN),
                    complex_rows(-tau * offset * u / TRACE_LEN),
                    complex_rows(-tau * rim * u / TRACE_LEN),
                    complex_rows(tau * (2 * lane + 1) * u / (2 * COSET_LEN)),
                ]
            )
        )
    into, outof, turns = [], [], []
    for g in range(HALF):
        pair = (2 * g, 2 * g + 1)
        into.append(np.stack([halves(matrices[u]) for u in pair]))
        for zh in range(2):
            rows = slice(SEG * zh, SEG * (zh + 1))
            outof.append(np.stack([halves(matrices[u].T[rows]) for u in pair]))
            turns.append(np.concatenate([vectors[u][:6] for u in pair] + [vectors[2 * g + zh][6:]]))
    vectors = np.pad(np.stack(turns), ((0, 0), (0, 2), (0, 0)))
    twist_in = complex_rows(tau * beta * (64 * seg[:, None] - 2048) / TRACE_LEN)
    twist_out = complex_rows(-tau * offset * (64 * seg[:, None] - 2048) / TRACE_LEN) / TRACE_LEN
    twist_rim = (
        complex_rows(-tau * rim * (64 * seg[:, None] - 2048) / TRACE_LEN) / TRACE_LEN * rim_here
    )
    twist_quot = complex_rows(
        tau * (2 * lane + 1) * (64 * seg[:, None]) / (2 * COSET_LEN)
    ) / math.sqrt(COSET_LEN)
    twists = np.concatenate([twist_in, twist_out, twist_rim, twist_quot])
    spread = np.zeros((PAIRS, RUN, 5, LANES))
    mean = np.zeros((PAIRS, RUN, LANES))
    for j in range(PAIRS):
        spread[j, :, j, :] = 1.0 / np.sin(np.pi * (offset[None, :] - run[:, None]) / RUN)
        own = (lane >= LANES - 16) & ((lane - (LANES - 16)) // 4 == j)
        spread[j, :, 4, :] = own / np.sin(np.pi * (rim[None, :] - run[:, None]) / RUN)
        mean[j, :, j] = 1.0 / TRACE_LEN
    spread = spread.reshape(LANES, 5 * LANES)
    half = np.arange(SEG)
    order = np.concatenate([2 * half, 2 * half + 1])
    last = real_form(tau * np.outer(order, 2 * lane + 1) / 256.0, "co", "ci")
    shape = (2 * (lane % 4) + 1) / 8.0
    gain = np.exp(-1j * np.pi * shape) * np.sin(np.pi * shape)
    vanish = 1.0 / (np.exp(-1j * np.pi * (2 * (lane % 4) + 1) / 4.0) - 1.0)
    scales = []
    for value in (gain, gain * vanish, gain * gain * vanish):
        scales += [value.real, value.imag]
    scales += [np.zeros(LANES)] * 2
    return {
        "vectors": vectors.astype(np.float32),
        "into": np.stack(into),
        "outof": np.stack(outof),
        "first": np.stack([halves(first), halves(final), halves(summed)]),
        "twists": twists.astype(np.float32),
        "spread": halves(spread),
        "mean": mean.reshape(LANES, LANES).astype(BF16),
        "last": halves(last),
        "scales": np.stack(scales).astype(np.float32),
    }


def parts_of(value):
    high = value.astype(BF16)
    low = (value - high.astype(F32)).astype(BF16)
    return high, low


def left_dot(table, value):
    high, low = parts_of(value)
    left = jnp.concatenate([table[0], table[0], table[1]], axis=1)
    right = jnp.concatenate([high, low, high], axis=0)
    return jnp.dot(left, right, preferred_element_type=F32)


def left_dot_turned(table, value):
    high, low = parts_of(value)
    return lax.dot_general(
        jnp.concatenate([table[0], table[0], table[1]], axis=1),
        jnp.concatenate([high, low, high], axis=1),
        (((1,), (1,)), ((), ())),
        preferred_element_type=F32,
    )


def right_dot(value, table):
    high, low = parts_of(value)
    left = jnp.concatenate([high, low, high], axis=1)
    right = jnp.concatenate([table[0], table[0], table[1]], axis=0)
    return jnp.dot(left, right, preferred_element_type=F32)


def ring_step(k, me):
    yi, xi, zi = k & 7, (k >> 3) & 3, k >> 5
    half = (yi + 1) >> 1
    dy = 4 + half * (1 - 2 * (yi & 1))
    dx = (xi ^ (xi >> 1)) ^ 2
    dz = 1 - zi
    return ((me + 8 * dy) & 56) | ((me + 2 * dx) & 6) | ((me ^ dz) & 1)


def dealt(m, col):
    return 8 * m + 2 * ((m + (col >> 1)) & 3) + (((m >> 2) ^ col) & 1)


def turn(real, imag, cosine, sine):
    return real * cosine - imag * sine, real * sine + imag * cosine


def kernel(
    trace_hbm, step_hbm, pair_hbm, chal_hbm,
    vectors_hbm, into_hbm, outof_hbm, first_hbm, twists_hbm, spread_hbm, mean_hbm, last_hbm, scales_hbm,
    ext, val, quot,
    trace, vectors, into, outof, first, twists, spread, mean, last, scales,
    step_ref, pair_ref, chal_ref,
    send1, recv1, send2, recv2, send3, recv3, send4, recv4, send5, recv5, send6, recv6,
    load_sems, send_sems, recv_sems, ready,
):
    me = lax.axis_index("row")
    col = lax.axis_index("col")
    group, far = me >> 1, me & 1
    slot = HALF * far + group

    barrier = pltpu.get_barrier_semaphore()

    def greet_row(k, carry):
        pl.semaphore_signal(
            barrier, inc=1, device_id={"row": ring_step(k, me)}, device_id_type=MESH
        )
        return carry

    def greet_col(k, carry):
        pl.semaphore_signal(
            barrier, inc=1, device_id={"col": (col + k) & 7}, device_id_type=MESH
        )
        return carry

    lax.fori_loop(HALF, SEG - 1, greet_row, 0)
    lax.fori_loop(1, COLS, greet_col, 0)

    @pl.when(far == 0)
    def _():
        lax.fori_loop(0, HALF, greet_row, 0)


    loads = [
        pltpu.make_async_copy(src, dst, load_sems.at[i])
        for i, (src, dst) in enumerate(
            [
                (trace_hbm, trace),
                (first_hbm, first),
                (vectors_hbm.at[me], vectors),
                (into_hbm.at[group], into),
                (outof_hbm.at[me], outof),
                (twists_hbm, twists),
                (spread_hbm, spread),
                (mean_hbm, mean),
                (scales_hbm, scales),
                (last_hbm, last),
                (step_hbm, step_ref),
                (pair_hbm, pair_ref),
                (chal_hbm, chal_ref),
            ]
        )
    ]
    for load in loads:
        load.start()

    loads[0].wait()
    loads[1].wait()
    grid = jnp.concatenate(
        [
            jnp.concatenate([trace[2 * j + c] for j in range(PAIRS)], axis=0)
            for c in range(2)
        ],
        axis=1,
    )
    head = left_dot_turned(first[0], grid)
    send1[...] = head.reshape(SEG, 2, LANES)
    for c in range(2):
        recv1[c, slot] = send1[2 * group + c]
    pl.semaphore_wait(barrier, HALF - 1 + COLS - 1 + HALF * far)

    def post1(k, to):
        peer = ring_step(k, me)
        pltpu.make_async_remote_copy(
            src_ref=send1.at[pl.ds(2 * (peer >> 1), 2)], dst_ref=recv1.at[:, slot],
            send_sem=send_sems.at[to], recv_sem=recv_sems.at[to],
            device_id={"row": peer}, device_id_type=MESH,
        ).start()
        return to

    @pl.when(far == 1)
    def _():
        pl.semaphore_signal(ready, inc=1, device_id={"row": me ^ 1}, device_id_type=MESH)
        lax.fori_loop(0, HALF, post1, 6)

    lax.fori_loop(HALF, SEG - 1, post1, 0)

    for load in loads[2:]:
        load.wait()
    def table(index, row):
        base = twists[2 * index], twists[2 * index + 1]
        return turn(*base, vectors[2 * row : 2 * row + 1], vectors[2 * row + 1 : 2 * row + 2])

    turn_in = [table(0, 3 * c) for c in range(2)]
    turn_out = [table(1, 3 * c + 1) for c in range(2)]
    turn_rim = [table(2, 3 * c + 2) for c in range(2)]

    own_half = recv1.at[:, pl.ds(0, HALF - 1)]
    pltpu.make_async_copy(own_half, own_half, recv_sems.at[0]).wait()
    gathered = recv1.at[:, pl.ds(0, HALF)]

    @pl.when(far == 0)
    def _():
        pl.semaphore_wait(ready, 1)
        pltpu.make_async_remote_copy(
            src_ref=gathered, dst_ref=gathered,
            send_sem=send_sems.at[6], recv_sem=recv_sems.at[6],
            device_id={"row": me ^ 1}, device_id_type=MESH,
        ).start()

    pltpu.make_async_copy(gathered, gathered, recv_sems.at[6]).wait()

    rows = []
    for c in range(2):
        mixed = left_dot(into[c], recv1[c].reshape(LANES, LANES))
        if c == 0:
            lowest = jnp.concatenate([mixed[0:8], mixed[SEG : SEG + 8]], axis=0)
        rows += turn(mixed[:SEG], mixed[SEG:], *turn_in[c])
    wide = right_dot(jnp.concatenate(rows, axis=0), spread)
    high, low = parts_of(lowest)
    sums = jnp.dot(high, mean[...], preferred_element_type=F32) + jnp.dot(
        low, mean[...], preferred_element_type=F32
    )
    sums = sums * jnp.where(group == 0, 1.0, 0.0).astype(F32)
    parity = lax.broadcasted_iota(jnp.int32, (SEG, LANES), 0) % 2
    sums = jnp.where(parity == 0, sums[0:1], sums[8:9])
    for c in range(2):
        pieces = []
        for j in range(5):
            part = wide[LANES * c : LANES * (c + 1), LANES * j : LANES * (j + 1)]
            real, imag = turn(part[:SEG], part[SEG:], *(turn_out[c] if j < 4 else turn_rim[c]))
            pieces.append(jnp.concatenate([real, imag], axis=0))
        back = left_dot(outof[c], jnp.concatenate(pieces, axis=1))
        for j in range(5):
            part = back[:, LANES * j : LANES * (j + 1)]
            if j < 4:
                send2[2 * j + c] = part.reshape(HALF, 2, LANES)
            elif c == 0:
                rest = part + sums
            else:
                send2[8] = (rest + pltpu.roll(part, SEG, 1)).reshape(HALF, 2, LANES)
    for i in range(9):
        recv2[i, group] = send2[i, group]

    def post2(k, carry):
        peer = ring_step(k, me)
        pltpu.make_async_remote_copy(
            src_ref=send2.at[:, peer >> 1], dst_ref=recv2.at[:, group],
            send_sem=send_sems.at[1], recv_sem=recv_sems.at[1],
            device_id={"row": peer}, device_id_type=MESH,
        ).start()
        return carry

    lax.fori_loop(HALF, SEG - 1, post2, 0)
    quot_cos, quot_sin = table(3, 6)
    others = recv2.at[:, pl.ds(0, HALF - 1)]
    pltpu.make_async_copy(others, others, recv_sems.at[1]).wait()

    blocks = [recv2[i].reshape(SEG, LANES) for i in range(9)]
    blocks.append(pltpu.roll(blocks[8], SEG, 1))
    arrived = jnp.concatenate(
        [jnp.concatenate(blocks[2 * j : 2 * j + 2], axis=0) for j in range(5)], axis=1
    )
    field = left_dot(first[1], arrived)

    def scale(row):
        return scales[2 * row : 2 * row + 1], scales[2 * row + 1 : 2 * row + 2]

    rim_part = field[:, 4 * LANES :]
    lane = lax.broadcasted_iota(jnp.int32, (SEG, LANES), 1)
    gain_real, gain_imag = scale(0)
    ahead = jnp.zeros((SEG, LANES), F32)
    own = jnp.zeros((SEG, LANES), F32)
    product = jnp.zeros((SEG, LANES), F32)
    cross = jnp.zeros((SEG, LANES), F32)
    rim_weight = [jnp.zeros((SEG, LANES), F32)] * 2
    level_ahead = jnp.zeros((1, 1), F32)
    level_own = jnp.zeros((1, 1), F32)
    level_product = jnp.zeros((1, 1), F32)
    for j in range(PAIRS):
        mean_c = rim_part[0:1, j : j + 1]
        mean_d = rim_part[SEG : SEG + 1, j : j + 1]
        chal_c, chal_d = chal_ref[2 * j], chal_ref[2 * j + 1]
        step_c, step_d = chal_c * step_ref[2 * j], chal_d * step_ref[2 * j + 1]
        weight = chal_c * pair_ref[2 * j] + chal_d * pair_ref[2 * j + 1]
        raw_c = field[:SEG, LANES * j : LANES * (j + 1)]
        raw_d = field[SEG:, LANES * j : LANES * (j + 1)]
        real_c = raw_c + mean_d
        real_d = raw_d - mean_c
        ext[0, 2 * j] = gain_real * real_c - gain_imag * mean_c
        ext[1, 2 * j] = gain_imag * real_c + gain_real * mean_c
        ext[0, 2 * j + 1] = gain_real * real_d - gain_imag * mean_d
        ext[1, 2 * j + 1] = gain_imag * real_d + gain_real * mean_d
        ahead += chal_c * raw_c + chal_d * raw_d
        own += step_c * real_c + step_d * real_d
        product += weight * (real_c * real_d)
        cross += weight * (real_c * mean_d + real_d * mean_c)
        group = (lane >= LANES - 16 + 4 * j) & (lane < LANES - 12 + 4 * j)
        rim_weight = [
            jnp.where(group, chal_c, rim_weight[0]),
            jnp.where(group, chal_d, rim_weight[1]),
        ]
        level_ahead += chal_c * mean_d - chal_d * mean_c
        level_own += (chal_c - step_c) * mean_c + (chal_d - step_d) * mean_d
        level_product += weight * (mean_c * mean_d)
    rim_sum = rim_part[:SEG] * rim_weight[0] + rim_part[SEG:] * rim_weight[1]
    rim_sum = rim_sum + pltpu.roll(rim_sum, 4, 1)
    rim_sum = rim_sum + pltpu.roll(rim_sum, 8, 1)
    ahead = jnp.where(lane < LANES - 4, pltpu.roll(ahead, LANES - 4, 1), rim_sum)
    line_real = ahead + level_ahead - own
    line_imag = level_own
    square_real = product - level_product
    square_imag = cross
    line_scale, square_scale = scale(1), scale(2)
    value_real = (
        line_scale[0] * line_real
        - line_scale[1] * line_imag
        - square_scale[0] * square_real
        + square_scale[1] * square_imag
    )
    value_imag = (
        line_scale[0] * line_imag
        + line_scale[1] * line_real
        - square_scale[0] * square_imag
        - square_scale[1] * square_real
    )
    mixed = left_dot(first[2], jnp.concatenate([value_real, value_imag], axis=0))
    for i in range(COLS):
        send3[i] = mixed[16 * i : 16 * (i + 1)]
        send6[i, 0:8] = value_real[8 * i : 8 * (i + 1)]
        send6[i, 8:16] = value_imag[8 * i : 8 * (i + 1)]

    def post3(k, carry):
        peer = (col + k) & 7
        pltpu.make_async_remote_copy(
            src_ref=send3.at[peer], dst_ref=recv3.at[col],
            send_sem=send_sems.at[2], recv_sem=recv_sems.at[2],
            device_id={"col": peer}, device_id_type=MESH,
        ).start()
        return carry

    lax.fori_loop(1, COLS, post3, 0)

    def post6(k, carry):
        peer = (col + k) & 7
        pltpu.make_async_remote_copy(
            src_ref=send6.at[peer], dst_ref=recv6.at[col],
            send_sem=send_sems.at[5], recv_sem=recv_sems.at[5],
            device_id={"col": peer}, device_id_type=MESH,
        ).start()
        return carry

    lax.fori_loop(1, COLS, post6, 0)
    recv3[col] = send3[col]
    recv6[col] = send6[col]
    pltpu.make_async_copy(
        recv3.at[pl.ds(0, COLS - 1)], recv3.at[pl.ds(0, COLS - 1)], recv_sems.at[2]
    ).wait()
    total = recv3[0]
    for i in range(1, COLS):
        total = total + recv3[i]
    send4[...] = total.reshape(8, 2, LANES)

    here = dealt(me >> 3, col) == me

    def post4(k, carry):
        line = (((k & 3) + (me >> 3)) & 3) | ((((k >> 5) ^ col) & 1) << 2)
        across = ((k >> 2) + col) & 7
        target = dealt(line, col)
        alone = (target == me) & (across == col)

        @pl.when(jnp.logical_not(alone))
        def _():
            pltpu.make_async_remote_copy(
                src_ref=send4.at[line], dst_ref=recv4.at[slot],
                send_sem=send_sems.at[3], recv_sem=recv_sems.at[3],
                device_id={"col": across, "row": target}, device_id_type=MESH,
            ).start()

        @pl.when(alone)
        def _():
            pltpu.make_async_copy(send4.at[line], recv4.at[slot], recv_sems.at[3]).start()

        return carry

    lax.fori_loop(0, SEG, post4, 0)

    pltpu.make_async_copy(
        recv6.at[pl.ds(0, COLS - 1)], recv6.at[pl.ds(0, COLS - 1)], recv_sems.at[5]
    ).wait()
    value = recv6[0]
    for i in range(1, COLS):
        value = value + recv6[i]
    send5[...] = value

    def post5(k, carry):
        pltpu.make_async_remote_copy(
            src_ref=send5, dst_ref=recv5.at[col],
            send_sem=send_sems.at[4], recv_sem=recv_sems.at[4],
            device_id={"col": (col + k) & 7}, device_id_type=MESH,
        ).start()
        return carry

    lax.fori_loop(1, COLS, post5, 0)
    recv5[col] = send5[...]

    pltpu.make_async_copy(recv4, recv4, recv_sems.at[3]).wait()
    mixed = left_dot(into[far], recv4[...].reshape(LANES, LANES))
    real, imag = turn(mixed[:SEG], mixed[SEG:], quot_cos, quot_sin)
    both = jnp.concatenate([real, imag], axis=1)
    both = jnp.concatenate([both, both], axis=0)
    result = left_dot_turned(last, both)
    for c in range(2):
        even = result[LANES * c : LANES * c + SEG]
        odd = result[LANES * c + SEG : LANES * (c + 1)]
        quot[c] = jnp.where(lane < SEG, even, odd)

    pltpu.make_async_copy(
        recv5.at[pl.ds(0, COLS - 1)], recv5.at[pl.ds(0, COLS - 1)], recv_sems.at[4]
    ).wait()
    for i in range(COLS):
        val[0, 8 * i : 8 * (i + 1)] = recv5[i, 0:8]
        val[1, 8 * i : 8 * (i + 1)] = recv5[i, 8:16]

    pltpu.make_async_copy(own_half, own_half, send_sems.at[0]).wait()
    pltpu.make_async_copy(gathered, gathered, send_sems.at[6]).wait()
    pltpu.make_async_copy(others, others, send_sems.at[1]).wait()
    pltpu.make_async_copy(
        send3.at[pl.ds(0, COLS - 1)], send3.at[pl.ds(0, COLS - 1)], send_sems.at[2]
    ).wait()

    @pl.when(here)
    def _():
        pltpu.make_async_copy(
            recv4.at[pl.ds(0, SEG - 1)], recv4.at[pl.ds(0, SEG - 1)], send_sems.at[3]
        ).wait()

    @pl.when(jnp.logical_not(here))
    def _():
        pltpu.make_async_copy(recv4, recv4, send_sems.at[3]).wait()

    for i in (4, 5):
        pltpu.make_async_copy(
            recv5.at[pl.ds(0, COLS - 1)], recv5.at[pl.ds(0, COLS - 1)], send_sems.at[i]
        ).wait()


def carry_out(ext, val, quot, ext_out, val_out, quot_out, sems):
    pieces = [(ext.at[:, c], ext_out.at[:, c]) for c in range(COLS)]
    pieces += [(val, val_out), (quot, quot_out)]
    moves = [pltpu.make_async_copy(src, dst, sems.at[i]) for i, (src, dst) in enumerate(pieces)]
    for move in moves:
        move.start()
    for move in moves:
        move.wait()


def shards(trace, step_coeff, pair_coeff, challenges):
    trace = trace.transpose(0, 2, 1)
    tables = build_tables()
    names = ["vectors", "into", "outof", "first", "twists", "spread", "mean", "last", "scales"]
    constants = [jnp.asarray(tables[name]) for name in names]
    operands = [
        pltpu.with_memory_space_constraint(x, pltpu.HBM)
        for x in (trace, step_coeff, pair_coeff, challenges, *constants)
    ]
    vmem = pltpu.VMEM
    hbm = pl.BlockSpec(memory_space=pltpu.HBM)
    inside = pl.BlockSpec(memory_space=pltpu.VMEM)
    outs = (
        jax.ShapeDtypeStruct((2, COLS, SEG, LANES), F32),
        jax.ShapeDtypeStruct((2, SEG, LANES), F32),
        jax.ShapeDtypeStruct((2, SEG, LANES), F32),
    )
    tables_scratch = [
        vmem(c.shape[1:] if n in ("vectors", "into", "outof") else c.shape, c.dtype)
        for n, c in zip(names, constants, strict=True)
    ]
    extension, values, quotient = pl.pallas_call(
        kernel,
        out_shape=tuple(vmem(o.shape, F32) for o in outs),
        in_specs=[hbm] * (4 + len(constants)),
        out_specs=(inside,) * 3,
        scratch_shapes=[
            vmem(trace.shape, F32),
            *tables_scratch,
            *[pltpu.SMEM((COLS,), F32)] * 3,
            vmem((SEG, 2, LANES), F32),
            vmem((2, SEG, 2, LANES), F32),
            vmem((9, HALF, 2, LANES), F32),
            vmem((9, HALF, 2, LANES), F32),
            vmem((COLS, 16, LANES), F32),
            vmem((COLS, 16, LANES), F32),
            vmem((8, 2, LANES), F32),
            vmem((SEG, 2, LANES), F32),
            vmem((16, LANES), F32),
            vmem((COLS, 16, LANES), F32),
            vmem((COLS, 16, LANES), F32),
            vmem((COLS, 16, LANES), F32),
            pltpu.SemaphoreType.DMA((13,)),
            pltpu.SemaphoreType.DMA((7,)),
            pltpu.SemaphoreType.DMA((7,)),
            pltpu.SemaphoreType.REGULAR,
        ],
        compiler_params=pltpu.CompilerParams(
            collective_id=0, has_side_effects=True, vmem_limit_bytes=32 * 1024 * 1024
        ),
    )(*operands)
    extension, values, quotient = pl.pallas_call(
        carry_out,
        out_shape=outs,
        in_specs=[inside] * 3,
        out_specs=(hbm,) * 3,
        scratch_shapes=[pltpu.SemaphoreType.DMA((COLS + 2,))],
    )(*[pltpu.with_memory_space_constraint(x, vmem) for x in (extension, values, quotient)])
    return extension, values, quotient.reshape(2, 1, SEG * LANES)


def solution(mesh):
    placed = (P("col", None, "row"), P("col"), P("col"), P("col"))
    return jax.shard_map(
        shards,
        mesh=mesh,
        in_specs=placed,
        out_specs=(P(None, "col", None, "row"), P(None, None, "row"), P(None, "row", None)),
        check_vma=False,
    )
```

```python
import math

import jax
import jax.numpy as jnp
import numpy as np
from jax import lax
from jax.experimental import pallas as pl
from jax.experimental.pallas import tpu as pltpu
from jax.sharding import PartitionSpec as P

SEG = 64
HALF = 32
COLS = 8
PAIRS = 4
RUN = 32
LANES = 128
TRACE_LEN = SEG * SEG * RUN
COSET_LEN = 4 * TRACE_LEN
MESH = pl.DeviceIdType.MESH
F32 = jnp.float32
BF16 = jnp.bfloat16


def halves(matrix):
    high = matrix.astype(BF16)
    low = (matrix - high.astype(np.float64)).astype(BF16)
    return np.stack([high, low])


def complex_rows(angle):
    return np.stack([np.cos(angle), np.sin(angle)])


def real_form(angle, out_order, in_order):
    cosine, sine = np.cos(angle), np.sin(angle)
    grid = np.stack([np.stack([cosine, -sine]), np.stack([sine, cosine])])
    places = {"co": (0, 2), "oc": (2, 0), "ci": (1, 3), "ic": (3, 1)}
    rows, cols = angle.shape
    return grid.transpose(places[out_order] + places[in_order]).reshape(2 * rows, 2 * cols)


def build_tables():
    tau = 2.0 * np.pi
    seg = np.arange(SEG)
    run = np.arange(RUN)
    first = real_form(tau * np.outer(seg, seg) / SEG, "oc", "ci")
    final = first.T.reshape(2 * SEG, SEG // 2, 2, 2).transpose(0, 2, 1, 3).reshape(2 * SEG, 2 * SEG)
    lane = np.arange(LANES)
    offset = lane // 4 + (2 * (lane % 4) + 1) / 8.0
    rim = RUN + (2 * (lane % 4) + 1) / 8.0
    rim_here = (lane >= LANES - 16).astype(np.float64)
    beta = np.tile(run, PAIRS)
    deal = np.array([dealt(m, i) for i in range(COLS) for m in range(8)])
    summed = first.reshape(SEG, 2, 2 * SEG)[deal].reshape(2 * SEG, 2 * SEG)
    slots = np.concatenate([seg[0::2], seg[1::2]])
    matrices = []
    vectors = []
    for u in range(SEG):
        angle = tau * np.outer(SEG * seg + u, slots) / (SEG * SEG)
        matrices.append(real_form(angle, "co", "ic"))
        vectors.append(
            np.concatenate(
                [
                    complex_rows(tau * beta * u / TRACE_LEN),
                    complex_rows(-tau * offset * u / TRACE_LEN),
                    complex_rows(-tau * rim * u / TRACE_LEN),
                    complex_rows(tau * (2 * lane + 1) * u / (2 * COSET_LEN)),
                ]
            )
        )
    into, outof, turns = [], [], []
    for g in range(HALF):
        pair = (2 * g, 2 * g + 1)
        into.append(np.stack([halves(matrices[u]) for u in pair]))
        for zh in range(2):
            rows = slice(SEG * zh, SEG * (zh + 1))
            outof.append(np.stack([halves(matrices[u].T[rows]) for u in pair]))
            turns.append(np.concatenate([vectors[u][:6] for u in pair] + [vectors[2 * g + zh][6:]]))
    vectors = np.pad(np.stack(turns), ((0, 0), (0, 2), (0, 0)))
    twist_in = complex_rows(tau * beta * (64 * seg[:, None] - 2048) / TRACE_LEN)
    twist_out = complex_rows(-tau * offset * (64 * seg[:, None] - 2048) / TRACE_LEN) / TRACE_LEN
    twist_rim = (
        complex_rows(-tau * rim * (64 * seg[:, None] - 2048) / TRACE_LEN) / TRACE_LEN * rim_here
    )
    twist_quot = complex_rows(
        tau * (2 * lane + 1) * (64 * seg[:, None]) / (2 * COSET_LEN)
    ) / math.sqrt(COSET_LEN)
    twists = np.concatenate([twist_in, twist_out, twist_rim, twist_quot])
    spread = np.zeros((PAIRS, RUN, 5, LANES))
    mean = np.zeros((PAIRS, RUN, LANES))
    for j in range(PAIRS):
        spread[j, :, j, :] = 1.0 / np.sin(np.pi * (offset[None, :] - run[:, None]) / RUN)
        own = (lane >= LANES - 16) & ((lane - (LANES - 16)) // 4 == j)
        spread[j, :, 4, :] = own / np.sin(np.pi * (rim[None, :] - run[:, None]) / RUN)
        mean[j, :, j] = 1.0 / TRACE_LEN
    spread = spread.reshape(LANES, 5 * LANES)
    half = np.arange(SEG)
    order = np.concatenate([2 * half, 2 * half + 1])
    last = real_form(tau * np.outer(order, 2 * lane + 1) / 256.0, "co", "ci")
    shape = (2 * (lane % 4) + 1) / 8.0
    gain = np.exp(-1j * np.pi * shape) * np.sin(np.pi * shape)
    vanish = 1.0 / (np.exp(-1j * np.pi * (2 * (lane % 4) + 1) / 4.0) - 1.0)
    scales = []
    for value in (gain, gain * vanish, gain * gain * vanish):
        scales += [value.real, value.imag]
    scales += [np.zeros(LANES)] * 2
    return {
        "vectors": vectors.astype(np.float32),
        "into": np.stack(into),
        "outof": np.stack(outof),
        "first": np.stack([halves(first), halves(final), halves(summed)]),
        "twists": twists.astype(np.float32),
        "spread": halves(spread),
        "mean": mean.reshape(LANES, LANES).astype(BF16),
        "last": halves(last),
        "scales": np.stack(scales).astype(np.float32),
    }


def parts_of(value):
    high = value.astype(BF16)
    low = (value - high.astype(F32)).astype(BF16)
    return high, low


def left_dot(table, value):
    high, low = parts_of(value)
    left = jnp.concatenate([table[0], table[0], table[1]], axis=1)
    right = jnp.concatenate([high, low, high], axis=0)
    return jnp.dot(left, right, preferred_element_type=F32)


def left_dot_turned(table, value):
    high, low = parts_of(value)
    return lax.dot_general(
        jnp.concatenate([table[0], table[0], table[1]], axis=1),
        jnp.concatenate([high, low, high], axis=1),
        (((1,), (1,)), ((), ())),
        preferred_element_type=F32,
    )


def right_dot(value, table):
    high, low = parts_of(value)
    left = jnp.concatenate([high, low, high], axis=1)
    right = jnp.concatenate([table[0], table[0], table[1]], axis=0)
    return jnp.dot(left, right, preferred_element_type=F32)


def ring_step(k, me):
    yi, xi, zi = k & 7, (k >> 3) & 3, k >> 5
    half = (yi + 1) >> 1
    dy = 4 + half * (1 - 2 * (yi & 1))
    dx = (xi ^ (xi >> 1)) ^ 2
    dz = 1 - zi
    return ((me + 8 * dy) & 56) | ((me + 2 * dx) & 6) | ((me ^ dz) & 1)


def dealt(m, col):
    return 8 * m + 2 * ((m + (col >> 1) + 2) & 3) + (((m >> 2) ^ col) & 1)


def turn(real, imag, cosine, sine):
    return real * cosine - imag * sine, real * sine + imag * cosine


def kernel(
    trace_hbm, step_hbm, pair_hbm, chal_hbm,
    vectors_hbm, into_hbm, outof_hbm, first_hbm, twists_hbm, spread_hbm, mean_hbm, last_hbm, scales_hbm,
    ext, val, quot,
    trace, vectors, into, outof, first, twists, spread, mean, last, scales,
    step_ref, pair_ref, chal_ref,
    send1, recv1, send2, recv2, send3, recv3, send4, recv4, send5, recv5, send6, recv6,
    load_sems, send_sems, recv_sems, ready,
):
    me = lax.axis_index("row")
    col = lax.axis_index("col")
    group, far = me >> 1, me & 1
    slot = HALF * far + group

    barrier = pltpu.get_barrier_semaphore()

    def greet_row(k, carry):
        pl.semaphore_signal(
            barrier, inc=1, device_id={"row": ring_step(k, me)}, device_id_type=MESH
        )
        return carry

    def greet_col(k, carry):
        pl.semaphore_signal(
            barrier, inc=1, device_id={"col": (col + k) & 7}, device_id_type=MESH
        )
        return carry

    lax.fori_loop(HALF, SEG - 1, greet_row, 0)
    lax.fori_loop(1, COLS, greet_col, 0)

    @pl.when(far == 0)
    def _():
        lax.fori_loop(0, HALF, greet_row, 0)


    loads = [
        pltpu.make_async_copy(src, dst, load_sems.at[i])
        for i, (src, dst) in enumerate(
            [
                (trace_hbm, trace),
                (first_hbm, first),
                (vectors_hbm.at[me], vectors),
                (into_hbm.at[group], into),
                (outof_hbm.at[me], outof),
                (twists_hbm, twists),
                (spread_hbm, spread),
                (mean_hbm, mean),
                (scales_hbm, scales),
                (last_hbm, last),
                (step_hbm, step_ref),
                (pair_hbm, pair_ref),
                (chal_hbm, chal_ref),
            ]
        )
    ]
    for load in loads:
        load.start()

    loads[0].wait()
    loads[1].wait()
    grid = jnp.concatenate(
        [
            jnp.concatenate([trace[2 * j + c] for j in range(PAIRS)], axis=0)
            for c in range(2)
        ],
        axis=1,
    )
    head = left_dot_turned(first[0], grid)
    send1.reshape(LANES, LANES)[...] = head
    for c in range(2):
        recv1[c, slot] = send1[2 * group + c]
    pl.semaphore_wait(barrier, HALF - 1 + COLS - 1 + HALF * far)

    def post1(k, to):
        peer = ring_step(k, me)
        pltpu.make_async_remote_copy(
            src_ref=send1.at[pl.ds(2 * (peer >> 1), 2)], dst_ref=recv1.at[:, slot],
            send_sem=send_sems.at[to], recv_sem=recv_sems.at[to],
            device_id={"row": peer}, device_id_type=MESH,
        ).start()
        return to

    @pl.when(far == 1)
    def _():
        pl.semaphore_signal(ready, inc=1, device_id={"row": me ^ 1}, device_id_type=MESH)
        lax.fori_loop(0, HALF, post1, 6)

    lax.fori_loop(HALF, SEG - 1, post1, 0)

    for load in loads[2:]:
        load.wait()
    def table(index, row):
        base = twists[2 * index], twists[2 * index + 1]
        return turn(*base, vectors[2 * row : 2 * row + 1], vectors[2 * row + 1 : 2 * row + 2])

    turn_in = [table(0, 3 * c) for c in range(2)]
    turn_out = [table(1, 3 * c + 1) for c in range(2)]
    turn_rim = [table(2, 3 * c + 2) for c in range(2)]

    own_half = recv1.at[:, pl.ds(0, HALF - 1)]
    pltpu.make_async_copy(own_half, own_half, recv_sems.at[0]).wait()
    gathered = recv1.at[:, pl.ds(0, HALF)]

    @pl.when(far == 0)
    def _():
        pl.semaphore_wait(ready, 1)
        pltpu.make_async_remote_copy(
            src_ref=gathered, dst_ref=gathered,
            send_sem=send_sems.at[6], recv_sem=recv_sems.at[6],
            device_id={"row": me ^ 1}, device_id_type=MESH,
        ).start()

    pltpu.make_async_copy(gathered, gathered, recv_sems.at[6]).wait()

    rows = []
    for c in range(2):
        mixed = left_dot(into[c], recv1.reshape(2, LANES, LANES)[c])
        if c == 0:
            lowest = jnp.concatenate([mixed[0:8], mixed[SEG : SEG + 8]], axis=0)
        rows += turn(mixed[:SEG], mixed[SEG:], *turn_in[c])
    wide = right_dot(jnp.concatenate(rows, axis=0), spread)
    high, low = parts_of(lowest)
    sums = jnp.dot(high, mean[...], preferred_element_type=F32) + jnp.dot(
        low, mean[...], preferred_element_type=F32
    )
    sums = sums * jnp.where(group == 0, 1.0, 0.0).astype(F32)
    parity = lax.broadcasted_iota(jnp.int32, (SEG, LANES), 0) % 2
    sums = jnp.where(parity == 0, sums[0:1], sums[8:9])
    for c in range(2):
        pieces = []
        for j in range(5):
            part = wide[LANES * c : LANES * (c + 1), LANES * j : LANES * (j + 1)]
            real, imag = turn(part[:SEG], part[SEG:], *(turn_out[c] if j < 4 else turn_rim[c]))
            pieces.append(jnp.concatenate([real, imag], axis=0))
        back = left_dot(outof[c], jnp.concatenate(pieces, axis=1))
        for j in range(5):
            part = back[:, LANES * j : LANES * (j + 1)]
            if j < 4:
                send2.reshape(9, SEG, LANES)[2 * j + c] = part
            elif c == 0:
                rest = part + sums
            else:
                send2.reshape(9, SEG, LANES)[8] = rest + pltpu.roll(part, SEG, 1)
    for i in range(9):
        recv2[i, group] = send2[i, group]

    def post2(k, carry):
        peer = ring_step(k, me)
        pltpu.make_async_remote_copy(
            src_ref=send2.at[:, peer >> 1], dst_ref=recv2.at[:, group],
            send_sem=send_sems.at[1], recv_sem=recv_sems.at[1],
            device_id={"row": peer}, device_id_type=MESH,
        ).start()
        return carry

    lax.fori_loop(HALF, SEG - 1, post2, 0)
    quot_cos, quot_sin = table(3, 6)
    others = recv2.at[:, pl.ds(0, HALF - 1)]
    pltpu.make_async_copy(others, others, recv_sems.at[1]).wait()

    blocks = [recv2.reshape(9, SEG, LANES)[i] for i in range(9)]
    blocks.append(pltpu.roll(blocks[8], SEG, 1))
    arrived = jnp.concatenate(
        [jnp.concatenate(blocks[2 * j : 2 * j + 2], axis=0) for j in range(5)], axis=1
    )
    field = left_dot(first[1], arrived)

    def scale(row):
        return scales[2 * row : 2 * row + 1], scales[2 * row + 1 : 2 * row + 2]

    rim_part = field[:, 4 * LANES :]
    lane = lax.broadcasted_iota(jnp.int32, (SEG, LANES), 1)
    gain_real, gain_imag = scale(0)
    ahead = jnp.zeros((SEG, LANES), F32)
    own = jnp.zeros((SEG, LANES), F32)
    product = jnp.zeros((SEG, LANES), F32)
    cross = jnp.zeros((SEG, LANES), F32)
    rim_weight = [jnp.zeros((SEG, LANES), F32)] * 2
    columns = []
    level_ahead = jnp.zeros((1, 1), F32)
    level_own = jnp.zeros((1, 1), F32)
    level_product = jnp.zeros((1, 1), F32)
    for j in range(PAIRS):
        mean_c = rim_part[0:1, j : j + 1]
        mean_d = rim_part[SEG : SEG + 1, j : j + 1]
        chal_c, chal_d = chal_ref[2 * j], chal_ref[2 * j + 1]
        step_c, step_d = chal_c * step_ref[2 * j], chal_d * step_ref[2 * j + 1]
        weight = chal_c * pair_ref[2 * j] + chal_d * pair_ref[2 * j + 1]
        raw_c = field[:SEG, LANES * j : LANES * (j + 1)]
        raw_d = field[SEG:, LANES * j : LANES * (j + 1)]
        real_c = raw_c + mean_d
        real_d = raw_d - mean_c
        columns += [(real_c, mean_c), (real_d, mean_d)]
        ahead += chal_c * raw_c + chal_d * raw_d
        own += step_c * real_c + step_d * real_d
        product += weight * (real_c * real_d)
        cross += weight * (real_c * mean_d + real_d * mean_c)
        group = (lane >= LANES - 16 + 4 * j) & (lane < LANES - 12 + 4 * j)
        rim_weight = [
            jnp.where(group, chal_c, rim_weight[0]),
            jnp.where(group, chal_d, rim_weight[1]),
        ]
        level_ahead += chal_c * mean_d - chal_d * mean_c
        level_own += (chal_c - step_c) * mean_c + (chal_d - step_d) * mean_d
        level_product += weight * (mean_c * mean_d)
    rim_sum = rim_part[:SEG] * rim_weight[0] + rim_part[SEG:] * rim_weight[1]
    rim_sum = rim_sum + pltpu.roll(rim_sum, 4, 1)
    rim_sum = rim_sum + pltpu.roll(rim_sum, 8, 1)
    ahead = jnp.where(lane < LANES - 4, pltpu.roll(ahead, LANES - 4, 1), rim_sum)
    line_real = ahead + level_ahead - own
    line_imag = level_own
    square_real = product - level_product
    square_imag = cross
    line_scale, square_scale = scale(1), scale(2)
    value_real = (
        line_scale[0] * line_real
        - line_scale[1] * line_imag
        - square_scale[0] * square_real
        + square_scale[1] * square_imag
    )
    value_imag = (
        line_scale[0] * line_imag
        + line_scale[1] * line_real
        - square_scale[0] * square_imag
        - square_scale[1] * square_real
    )
    mixed = left_dot(first[2], jnp.concatenate([value_real, value_imag], axis=0))
    for i in range(COLS):
        send3[i] = mixed[16 * i : 16 * (i + 1)]

    def post3(k, carry):
        peer = (col + k) & 7
        pltpu.make_async_remote_copy(
            src_ref=send3.at[peer], dst_ref=recv3.at[col],
            send_sem=send_sems.at[2], recv_sem=recv_sems.at[2],
            device_id={"col": peer}, device_id_type=MESH,
        ).start()
        return carry

    lax.fori_loop(1, COLS, post3, 0)
    for i in range(COLS):
        send6[i, 0:8] = value_real[8 * i : 8 * (i + 1)]
        send6[i, 8:16] = value_imag[8 * i : 8 * (i + 1)]

    def post6(k, carry):
        peer = (col + k) & 7
        pltpu.make_async_remote_copy(
            src_ref=send6.at[peer], dst_ref=recv6.at[col],
            send_sem=send_sems.at[5], recv_sem=recv_sems.at[5],
            device_id={"col": peer}, device_id_type=MESH,
        ).start()
        return carry

    lax.fori_loop(1, COLS, post6, 0)
    recv3[col] = send3[col]
    recv6[col] = send6[col]
    for c, (real, mean_here) in enumerate(columns):
        ext[0, c] = gain_real * real - gain_imag * mean_here
        ext[1, c] = gain_imag * real + gain_real * mean_here
    pltpu.make_async_copy(
        recv3.at[pl.ds(0, COLS - 1)], recv3.at[pl.ds(0, COLS - 1)], recv_sems.at[2]
    ).wait()
    total = recv3[0]
    for i in range(1, COLS):
        total = total + recv3[i]
    send4.reshape(16, LANES)[...] = total

    here = dealt(me >> 3, col) == me

    def post4(k, carry):
        across = ((k >> 2) & 7) ^ 1
        line = (k & 3) ^ (7 * (((k >> 5) ^ col) & 1))
        target = dealt(line, col)
        alone = (target == me) & (across == col)

        @pl.when(jnp.logical_not(alone))
        def _():
            pltpu.make_async_remote_copy(
                src_ref=send4.at[line], dst_ref=recv4.at[slot],
                send_sem=send_sems.at[3], recv_sem=recv_sems.at[3],
                device_id={"col": across, "row": target}, device_id_type=MESH,
            ).start()

        @pl.when(alone)
        def _():
            pltpu.make_async_copy(send4.at[line], recv4.at[slot], recv_sems.at[3]).start()

        return carry

    lax.fori_loop(0, SEG, post4, 0)
    pltpu.make_async_copy(
        recv6.at[pl.ds(0, COLS - 1)], recv6.at[pl.ds(0, COLS - 1)], recv_sems.at[5]
    ).wait()
    value = recv6[0]
    for i in range(1, COLS):
        value = value + recv6[i]
    send5[...] = value

    def post5(k, carry):
        pltpu.make_async_remote_copy(
            src_ref=send5, dst_ref=recv5.at[col],
            send_sem=send_sems.at[4], recv_sem=recv_sems.at[4],
            device_id={"col": (col + k) & 7}, device_id_type=MESH,
        ).start()
        return carry

    lax.fori_loop(1, COLS, post5, 0)
    recv5[col] = send5[...]

    pltpu.make_async_copy(recv4, recv4, recv_sems.at[3]).wait()
    mixed = left_dot(into[far], recv4.reshape(LANES, LANES)[...])
    real, imag = turn(mixed[:SEG], mixed[SEG:], quot_cos, quot_sin)
    both = jnp.concatenate([real, imag], axis=1)
    both = jnp.concatenate([both, both], axis=0)
    result = left_dot_turned(last, both)
    for c in range(2):
        even = result[LANES * c : LANES * c + SEG]
        odd = result[LANES * c + SEG : LANES * (c + 1)]
        quot[c] = jnp.where(lane < SEG, even, odd)

    pltpu.make_async_copy(
        recv5.at[pl.ds(0, COLS - 1)], recv5.at[pl.ds(0, COLS - 1)], recv_sems.at[4]
    ).wait()
    for i in range(COLS):
        val[0, 8 * i : 8 * (i + 1)] = recv5[i, 0:8]
        val[1, 8 * i : 8 * (i + 1)] = recv5[i, 8:16]

    pltpu.make_async_copy(own_half, own_half, send_sems.at[0]).wait()
    pltpu.make_async_copy(gathered, gathered, send_sems.at[6]).wait()
    pltpu.make_async_copy(others, others, send_sems.at[1]).wait()
    pltpu.make_async_copy(
        send3.at[pl.ds(0, COLS - 1)], send3.at[pl.ds(0, COLS - 1)], send_sems.at[2]
    ).wait()

    @pl.when(here)
    def _():
        pltpu.make_async_copy(
            recv4.at[pl.ds(0, SEG - 1)], recv4.at[pl.ds(0, SEG - 1)], send_sems.at[3]
        ).wait()

    @pl.when(jnp.logical_not(here))
    def _():
        pltpu.make_async_copy(recv4, recv4, send_sems.at[3]).wait()

    for i in (4, 5):
        pltpu.make_async_copy(
            recv5.at[pl.ds(0, COLS - 1)], recv5.at[pl.ds(0, COLS - 1)], send_sems.at[i]
        ).wait()


def carry_out(ext, val, quot, ext_out, val_out, quot_out, sems):
    pieces = [(ext.at[:, c], ext_out.at[:, c]) for c in range(COLS)]
    pieces += [(val, val_out), (quot, quot_out)]
    moves = [pltpu.make_async_copy(src, dst, sems.at[i]) for i, (src, dst) in enumerate(pieces)]
    for move in moves:
        move.start()
    for move in moves:
        move.wait()


def shards(trace, step_coeff, pair_coeff, challenges):
    trace = trace.transpose(0, 2, 1)
    tables = build_tables()
    names = ["vectors", "into", "outof", "first", "twists", "spread", "mean", "last", "scales"]
    constants = [jnp.asarray(tables[name]) for name in names]
    operands = [
        pltpu.with_memory_space_constraint(x, pltpu.HBM)
        for x in (trace, step_coeff, pair_coeff, challenges, *constants)
    ]
    vmem = pltpu.VMEM
    hbm = pl.BlockSpec(memory_space=pltpu.HBM)
    inside = pl.BlockSpec(memory_space=pltpu.VMEM)
    outs = (
        jax.ShapeDtypeStruct((2, COLS, SEG, LANES), F32),
        jax.ShapeDtypeStruct((2, SEG, LANES), F32),
        jax.ShapeDtypeStruct((2, SEG, LANES), F32),
    )
    tables_scratch = [
        vmem(c.shape[1:] if n in ("vectors", "into", "outof") else c.shape, c.dtype)
        for n, c in zip(names, constants, strict=True)
    ]
    extension, values, quotient = pl.pallas_call(
        kernel,
        out_shape=tuple(vmem(o.shape, F32) for o in outs),
        in_specs=[hbm] * (4 + len(constants)),
        out_specs=(inside,) * 3,
        scratch_shapes=[
            vmem(trace.shape, F32),
            *tables_scratch,
            *[pltpu.SMEM((COLS,), F32)] * 3,
            vmem((SEG, 2, LANES), F32),
            vmem((2, SEG, 2, LANES), F32),
            vmem((9, HALF, 2, LANES), F32),
            vmem((9, HALF, 2, LANES), F32),
            vmem((COLS, 16, LANES), F32),
            vmem((COLS, 16, LANES), F32),
            vmem((8, 2, LANES), F32),
            vmem((SEG, 2, LANES), F32),
            vmem((16, LANES), F32),
            vmem((COLS, 16, LANES), F32),
            vmem((COLS, 16, LANES), F32),
            vmem((COLS, 16, LANES), F32),
            pltpu.SemaphoreType.DMA((13,)),
            pltpu.SemaphoreType.DMA((7,)),
            pltpu.SemaphoreType.DMA((7,)),
            pltpu.SemaphoreType.REGULAR,
        ],
        compiler_params=pltpu.CompilerParams(
            collective_id=0, has_side_effects=True, vmem_limit_bytes=32 * 1024 * 1024
        ),
    )(*operands)
    extension, values, quotient = pl.pallas_call(
        carry_out,
        out_shape=outs,
        in_specs=[inside] * 3,
        out_specs=(hbm,) * 3,
        scratch_shapes=[pltpu.SemaphoreType.DMA((COLS + 2,))],
    )(*[pltpu.with_memory_space_constraint(x, vmem) for x in (extension, values, quotient)])
    return extension, values, quotient.reshape(2, 1, SEG * LANES)


def solution(mesh):
    placed = (P("col", None, "row"), P("col"), P("col"), P("col"))
    return jax.shard_map(
        shards,
        mesh=mesh,
        in_specs=placed,
        out_specs=(P(None, "col", None, "row"), P(None, None, "row"), P(None, "row", None)),
        check_vma=False,
    )
```

```python
import math

import jax
import jax.numpy as jnp
import numpy as np
from jax import lax
from jax.experimental import pallas as pl
from jax.experimental.pallas import tpu as pltpu
from jax.sharding import PartitionSpec as P

SEG = 64
HALF = 32
COLS = 8
PAIRS = 4
RUN = 32
LANES = 128
TRACE_LEN = SEG * SEG * RUN
COSET_LEN = 4 * TRACE_LEN
MESH = pl.DeviceIdType.MESH
F32 = jnp.float32
BF16 = jnp.bfloat16


def halves(matrix):
    high = matrix.astype(BF16)
    low = (matrix - high.astype(np.float64)).astype(BF16)
    return np.stack([high, low])


def complex_rows(angle):
    return np.stack([np.cos(angle), np.sin(angle)])


def real_form(angle, out_order, in_order):
    cosine, sine = np.cos(angle), np.sin(angle)
    grid = np.stack([np.stack([cosine, -sine]), np.stack([sine, cosine])])
    places = {"co": (0, 2), "oc": (2, 0), "ci": (1, 3), "ic": (3, 1)}
    rows, cols = angle.shape
    return grid.transpose(places[out_order] + places[in_order]).reshape(2 * rows, 2 * cols)


def build_tables():
    tau = 2.0 * np.pi
    seg = np.arange(SEG)
    run = np.arange(RUN)
    first = real_form(tau * np.outer(seg, seg) / SEG, "oc", "ci")
    final = first.T.reshape(2 * SEG, SEG // 2, 2, 2).transpose(0, 2, 1, 3).reshape(2 * SEG, 2 * SEG)
    lane = np.arange(LANES)
    offset = lane // 4 + (2 * (lane % 4) + 1) / 8.0
    rim = RUN + (2 * (lane % 4) + 1) / 8.0
    rim_here = (lane >= LANES - 16).astype(np.float64)
    beta = np.tile(run, PAIRS)
    deal = np.array([dealt(m, i) for i in range(COLS) for m in range(8)])
    summed = first.reshape(SEG, 2, 2 * SEG)[deal].reshape(2 * SEG, 2 * SEG)
    slots = np.concatenate([seg[0::2], seg[1::2]])
    matrices = []
    vectors = []
    for u in range(SEG):
        angle = tau * np.outer(SEG * seg + u, slots) / (SEG * SEG)
        matrices.append(real_form(angle, "co", "ic"))
        vectors.append(
            np.concatenate(
                [
                    complex_rows(tau * beta * u / TRACE_LEN),
                    complex_rows(-tau * offset * u / TRACE_LEN),
                    complex_rows(-tau * rim * u / TRACE_LEN),
                    complex_rows(tau * (2 * lane + 1) * u / (2 * COSET_LEN)),
                ]
            )
        )
    into, outof, turns = [], [], []
    for g in range(HALF):
        pair = (2 * g, 2 * g + 1)
        into.append(np.stack([halves(matrices[u]) for u in pair]))
        for zh in range(2):
            rows = slice(SEG * zh, SEG * (zh + 1))
            outof.append(np.stack([halves(matrices[u].T[rows]) for u in pair]))
            turns.append(np.concatenate([vectors[u][:6] for u in pair] + [vectors[2 * g + zh][6:]]))
    vectors = np.pad(np.stack(turns), ((0, 0), (0, 2), (0, 0)))
    twist_in = complex_rows(tau * beta * (64 * seg[:, None] - 2048) / TRACE_LEN)
    twist_out = complex_rows(-tau * offset * (64 * seg[:, None] - 2048) / TRACE_LEN) / TRACE_LEN
    twist_rim = (
        complex_rows(-tau * rim * (64 * seg[:, None] - 2048) / TRACE_LEN) / TRACE_LEN * rim_here
    )
    twist_quot = complex_rows(
        tau * (2 * lane + 1) * (64 * seg[:, None]) / (2 * COSET_LEN)
    ) / math.sqrt(COSET_LEN)
    twists = np.concatenate([twist_in, twist_out, twist_rim, twist_quot])
    spread = np.zeros((PAIRS, RUN, 5, LANES))
    mean = np.zeros((PAIRS, RUN, LANES))
    for j in range(PAIRS):
        spread[j, :, j, :] = 1.0 / np.sin(np.pi * (offset[None, :] - run[:, None]) / RUN)
        own = (lane >= LANES - 16) & ((lane - (LANES - 16)) // 4 == j)
        spread[j, :, 4, :] = own / np.sin(np.pi * (rim[None, :] - run[:, None]) / RUN)
        mean[j, :, j] = 1.0 / TRACE_LEN
    spread = spread.reshape(LANES, 5 * LANES)
    half = np.arange(SEG)
    order = np.concatenate([2 * half, 2 * half + 1])
    last = real_form(tau * np.outer(order, 2 * lane + 1) / 256.0, "co", "ci")
    shape = (2 * (lane % 4) + 1) / 8.0
    gain = np.exp(-1j * np.pi * shape) * np.sin(np.pi * shape)
    vanish = 1.0 / (np.exp(-1j * np.pi * (2 * (lane % 4) + 1) / 4.0) - 1.0)
    scales = []
    for value in (gain, gain * vanish, gain * gain * vanish):
        scales += [value.real, value.imag]
    scales += [np.zeros(LANES)] * 2
    return {
        "vectors": vectors.astype(np.float32),
        "into": np.stack(into),
        "outof": np.stack(outof),
        "first": np.stack([halves(first), halves(final), halves(summed)]),
        "twists": twists.astype(np.float32),
        "spread": halves(spread),
        "mean": mean.reshape(LANES, LANES).astype(BF16),
        "last": halves(last),
        "scales": np.stack(scales).astype(np.float32),
    }


def parts_of(value):
    high = value.astype(BF16)
    low = (value - high.astype(F32)).astype(BF16)
    return high, low


def left_dot(table, value):
    high, low = parts_of(value)
    left = jnp.concatenate([table[0], table[0], table[1]], axis=1)
    right = jnp.concatenate([high, low, high], axis=0)
    return jnp.dot(left, right, preferred_element_type=F32)


def left_dot_turned(table, value):
    high, low = parts_of(value)
    return lax.dot_general(
        jnp.concatenate([table[0], table[0], table[1]], axis=1),
        jnp.concatenate([high, low, high], axis=1),
        (((1,), (1,)), ((), ())),
        preferred_element_type=F32,
    )


def right_dot(value, table):
    high, low = parts_of(value)
    left = jnp.concatenate([high, low, high], axis=1)
    right = jnp.concatenate([table[0], table[0], table[1]], axis=0)
    return jnp.dot(left, right, preferred_element_type=F32)


def ring_step(k, me):
    yi, xi, zi = k & 7, (k >> 3) & 3, k >> 5
    half = (yi + 1) >> 1
    dy = 4 + half * (1 - 2 * (yi & 1))
    dx = (xi ^ (xi >> 1)) ^ 2
    dz = 1 - zi
    return ((me + 8 * dy) & 56) | ((me + 2 * dx) & 6) | ((me ^ dz) & 1)


def dealt(m, col):
    return 8 * m + 2 * ((m + (col >> 1) + 2) & 3) + (((m >> 2) ^ col ^ 1) & 1)


def turn(real, imag, cosine, sine):
    return real * cosine - imag * sine, real * sine + imag * cosine


def kernel(
    trace_hbm, step_hbm, pair_hbm, chal_hbm,
    vectors_hbm, into_hbm, outof_hbm, first_hbm, twists_hbm, spread_hbm, mean_hbm, last_hbm, scales_hbm,
    ext, val, quot,
    trace, vectors, into, outof, first, twists, spread, mean, last, scales,
    step_ref, pair_ref, chal_ref,
    send1, recv1, send2, recv2, send3, recv3, send4, recv4, send5, recv5, send6, recv6,
    load_sems, send_sems, recv_sems, ready,
):
    me = lax.axis_index("row")
    col = lax.axis_index("col")
    group, far = me >> 1, me & 1
    slot = HALF * far + group

    barrier = pltpu.get_barrier_semaphore()

    def greet_row(k, carry):
        pl.semaphore_signal(
            barrier, inc=1, device_id={"row": ring_step(k, me)}, device_id_type=MESH
        )
        return carry

    def greet_col(k, carry):
        pl.semaphore_signal(
            barrier, inc=1, device_id={"col": (col + k) & 7}, device_id_type=MESH
        )
        return carry

    lax.fori_loop(HALF, SEG - 1, greet_row, 0)
    lax.fori_loop(1, COLS, greet_col, 0)

    @pl.when(far == 0)
    def _():
        lax.fori_loop(0, HALF, greet_row, 0)


    loads = [
        pltpu.make_async_copy(src, dst, load_sems.at[i])
        for i, (src, dst) in enumerate(
            [
                (trace_hbm, trace),
                (first_hbm, first),
                (vectors_hbm.at[me], vectors),
                (into_hbm.at[group], into),
                (outof_hbm.at[me], outof),
                (twists_hbm, twists),
                (spread_hbm, spread),
                (mean_hbm, mean),
                (scales_hbm, scales),
                (last_hbm, last),
                (step_hbm, step_ref),
                (pair_hbm, pair_ref),
                (chal_hbm, chal_ref),
            ]
        )
    ]
    for load in loads:
        load.start()

    loads[0].wait()
    loads[1].wait()
    grid = jnp.concatenate(
        [
            jnp.concatenate([trace[2 * j + c] for j in range(PAIRS)], axis=0)
            for c in range(2)
        ],
        axis=1,
    )
    head = left_dot_turned(first[0], grid)
    send1.reshape(LANES, LANES)[...] = head
    for c in range(2):
        recv1[c, slot] = send1[2 * group + c]
    pl.semaphore_wait(barrier, HALF - 1 + COLS - 1 + HALF * far)

    def post1(k, to):
        peer = ring_step(k, me)
        pltpu.make_async_remote_copy(
            src_ref=send1.at[pl.ds(2 * (peer >> 1), 2)], dst_ref=recv1.at[:, slot],
            send_sem=send_sems.at[to], recv_sem=recv_sems.at[to],
            device_id={"row": peer}, device_id_type=MESH,
        ).start()
        return to

    @pl.when(far == 1)
    def _():
        pl.semaphore_signal(ready, inc=1, device_id={"row": me ^ 1}, device_id_type=MESH)
        lax.fori_loop(0, HALF, post1, 6)

    lax.fori_loop(HALF, SEG - 1, post1, 0)

    for load in loads[2:]:
        load.wait()
    def table(index, row):
        base = twists[2 * index], twists[2 * index + 1]
        return turn(*base, vectors[2 * row : 2 * row + 1], vectors[2 * row + 1 : 2 * row + 2])

    turn_in = [table(0, 3 * c) for c in range(2)]
    turn_out = [table(1, 3 * c + 1) for c in range(2)]
    turn_rim = [table(2, 3 * c + 2) for c in range(2)]

    own_half = recv1.at[:, pl.ds(0, HALF - 1)]
    pltpu.make_async_copy(own_half, own_half, recv_sems.at[0]).wait()
    gathered = recv1.at[:, pl.ds(0, HALF)]

    @pl.when(far == 0)
    def _():
        pl.semaphore_wait(ready, 1)
        pltpu.make_async_remote_copy(
            src_ref=gathered, dst_ref=gathered,
            send_sem=send_sems.at[6], recv_sem=recv_sems.at[6],
            device_id={"row": me ^ 1}, device_id_type=MESH,
        ).start()

    pltpu.make_async_copy(gathered, gathered, recv_sems.at[6]).wait()

    rows = []
    for c in range(2):
        mixed = left_dot(into[c], recv1.reshape(2, LANES, LANES)[c])
        if c == 0:
            lowest = jnp.concatenate([mixed[0:8], mixed[SEG : SEG + 8]], axis=0)
        rows += turn(mixed[:SEG], mixed[SEG:], *turn_in[c])
    wide = right_dot(jnp.concatenate(rows, axis=0), spread)
    high, low = parts_of(lowest)
    sums = jnp.dot(high, mean[...], preferred_element_type=F32) + jnp.dot(
        low, mean[...], preferred_element_type=F32
    )
    sums = sums * jnp.where(group == 0, 1.0, 0.0).astype(F32)
    parity = lax.broadcasted_iota(jnp.int32, (SEG, LANES), 0) % 2
    sums = jnp.where(parity == 0, sums[0:1], sums[8:9])
    for c in range(2):
        pieces = []
        for j in range(5):
            part = wide[LANES * c : LANES * (c + 1), LANES * j : LANES * (j + 1)]
            real, imag = turn(part[:SEG], part[SEG:], *(turn_out[c] if j < 4 else turn_rim[c]))
            pieces.append(jnp.concatenate([real, imag], axis=0))
        back = left_dot(outof[c], jnp.concatenate(pieces, axis=1))
        for j in range(5):
            part = back[:, LANES * j : LANES * (j + 1)]
            if j < 4:
                send2.reshape(9, SEG, LANES)[2 * j + c] = part
            elif c == 0:
                rest = part + sums
            else:
                send2.reshape(9, SEG, LANES)[8] = rest + pltpu.roll(part, SEG, 1)
    for i in range(9):
        recv2[i, group] = send2[i, group]

    def post2(k, carry):
        peer = ring_step(k, me)
        pltpu.make_async_remote_copy(
            src_ref=send2.at[:, peer >> 1], dst_ref=recv2.at[:, group],
            send_sem=send_sems.at[1], recv_sem=recv_sems.at[1],
            device_id={"row": peer}, device_id_type=MESH,
        ).start()
        return carry

    lax.fori_loop(HALF, SEG - 1, post2, 0)
    quot_cos, quot_sin = table(3, 6)
    others = recv2.at[:, pl.ds(0, HALF - 1)]
    pltpu.make_async_copy(others, others, recv_sems.at[1]).wait()

    blocks = [recv2.reshape(9, SEG, LANES)[i] for i in range(9)]
    blocks.append(pltpu.roll(blocks[8], SEG, 1))
    arrived = jnp.concatenate(
        [jnp.concatenate(blocks[2 * j : 2 * j + 2], axis=0) for j in range(5)], axis=1
    )
    field = left_dot(first[1], arrived)

    def scale(row):
        return scales[2 * row : 2 * row + 1], scales[2 * row + 1 : 2 * row + 2]

    rim_part = field[:, 4 * LANES :]
    lane = lax.broadcasted_iota(jnp.int32, (SEG, LANES), 1)
    gain_real, gain_imag = scale(0)
    ahead = jnp.zeros((SEG, LANES), F32)
    own = jnp.zeros((SEG, LANES), F32)
    product = jnp.zeros((SEG, LANES), F32)
    cross = jnp.zeros((SEG, LANES), F32)
    rim_weight = [jnp.zeros((SEG, LANES), F32)] * 2
    columns = []
    level_ahead = jnp.zeros((1, 1), F32)
    level_own = jnp.zeros((1, 1), F32)
    level_product = jnp.zeros((1, 1), F32)
    for j in range(PAIRS):
        mean_c = rim_part[0:1, j : j + 1]
        mean_d = rim_part[SEG : SEG + 1, j : j + 1]
        chal_c, chal_d = chal_ref[2 * j], chal_ref[2 * j + 1]
        step_c, step_d = chal_c * step_ref[2 * j], chal_d * step_ref[2 * j + 1]
        weight = chal_c * pair_ref[2 * j] + chal_d * pair_ref[2 * j + 1]
        raw_c = field[:SEG, LANES * j : LANES * (j + 1)]
        raw_d = field[SEG:, LANES * j : LANES * (j + 1)]
        real_c = raw_c + mean_d
        real_d = raw_d - mean_c
        columns += [(real_c, mean_c), (real_d, mean_d)]
        ahead += chal_c * raw_c + chal_d * raw_d
        own += step_c * real_c + step_d * real_d
        product += weight * (real_c * real_d)
        cross += weight * (real_c * mean_d + real_d * mean_c)
        group = (lane >= LANES - 16 + 4 * j) & (lane < LANES - 12 + 4 * j)
        rim_weight = [
            jnp.where(group, chal_c, rim_weight[0]),
            jnp.where(group, chal_d, rim_weight[1]),
        ]
        level_ahead += chal_c * mean_d - chal_d * mean_c
        level_own += (chal_c - step_c) * mean_c + (chal_d - step_d) * mean_d
        level_product += weight * (mean_c * mean_d)
    rim_sum = rim_part[:SEG] * rim_weight[0] + rim_part[SEG:] * rim_weight[1]
    rim_sum = rim_sum + pltpu.roll(rim_sum, 4, 1)
    rim_sum = rim_sum + pltpu.roll(rim_sum, 8, 1)
    ahead = jnp.where(lane < LANES - 4, pltpu.roll(ahead, LANES - 4, 1), rim_sum)
    line_real = ahead + level_ahead - own
    line_imag = level_own
    square_real = product - level_product
    square_imag = cross
    line_scale, square_scale = scale(1), scale(2)
    value_real = (
        line_scale[0] * line_real
        - line_scale[1] * line_imag
        - square_scale[0] * square_real
        + square_scale[1] * square_imag
    )
    value_imag = (
        line_scale[0] * line_imag
        + line_scale[1] * line_real
        - square_scale[0] * square_imag
        - square_scale[1] * square_real
    )
    mixed = left_dot(first[2], jnp.concatenate([value_real, value_imag], axis=0))
    for i in range(COLS):
        send3[i] = mixed[16 * i : 16 * (i + 1)]

    def post3(k, carry):
        peer = (col + k) & 7
        pltpu.make_async_remote_copy(
            src_ref=send3.at[peer], dst_ref=recv3.at[col],
            send_sem=send_sems.at[2], recv_sem=recv_sems.at[2],
            device_id={"col": peer}, device_id_type=MESH,
        ).start()
        return carry

    lax.fori_loop(1, COLS, post3, 0)
    for i in range(COLS):
        send6[i, 0:8] = value_real[8 * i : 8 * (i + 1)]
        send6[i, 8:16] = value_imag[8 * i : 8 * (i + 1)]

    def post6(k, carry):
        peer = (col + k) & 7
        pltpu.make_async_remote_copy(
            src_ref=send6.at[peer], dst_ref=recv6.at[col],
            send_sem=send_sems.at[5], recv_sem=recv_sems.at[5],
            device_id={"col": peer}, device_id_type=MESH,
        ).start()
        return carry

    lax.fori_loop(1, COLS, post6, 0)
    recv3[col] = send3[col]
    recv6[col] = send6[col]
    for c, (real, mean_here) in enumerate(columns):
        ext[0, c] = gain_real * real - gain_imag * mean_here
        ext[1, c] = gain_imag * real + gain_real * mean_here
    pltpu.make_async_copy(
        recv3.at[pl.ds(0, COLS - 1)], recv3.at[pl.ds(0, COLS - 1)], recv_sems.at[2]
    ).wait()
    total = recv3[0]
    for i in range(1, COLS):
        total = total + recv3[i]
    send4.reshape(16, LANES)[...] = total

    here = dealt(me >> 3, col) == me

    def post4(k, carry):
        across = ((k >> 2) & 7) ^ 1
        line = (k & 3) ^ (7 * (((k >> 5) ^ col ^ 1) & 1))
        target = dealt(line, col)
        alone = (target == me) & (across == col)

        @pl.when(jnp.logical_not(alone))
        def _():
            pltpu.make_async_remote_copy(
                src_ref=send4.at[line], dst_ref=recv4.at[slot],
                send_sem=send_sems.at[3], recv_sem=recv_sems.at[3],
                device_id={"col": across, "row": target}, device_id_type=MESH,
            ).start()

        @pl.when(alone)
        def _():
            pltpu.make_async_copy(send4.at[line], recv4.at[slot], recv_sems.at[3]).start()

        return carry

    lax.fori_loop(0, SEG, post4, 0)
    pltpu.make_async_copy(
        recv6.at[pl.ds(0, COLS - 1)], recv6.at[pl.ds(0, COLS - 1)], recv_sems.at[5]
    ).wait()
    value = recv6[0]
    for i in range(1, COLS):
        value = value + recv6[i]
    send5[...] = value

    def post5(k, carry):
        pltpu.make_async_remote_copy(
            src_ref=send5, dst_ref=recv5.at[col],
            send_sem=send_sems.at[4], recv_sem=recv_sems.at[4],
            device_id={"col": (col + k) & 7}, device_id_type=MESH,
        ).start()
        return carry

    lax.fori_loop(1, COLS, post5, 0)
    recv5[col] = send5[...]

    pltpu.make_async_copy(recv4, recv4, recv_sems.at[3]).wait()
    mixed = left_dot(into[far], recv4.reshape(LANES, LANES)[...])
    real, imag = turn(mixed[:SEG], mixed[SEG:], quot_cos, quot_sin)
    both = jnp.concatenate([real, imag], axis=1)
    both = jnp.concatenate([both, both], axis=0)
    result = left_dot_turned(last, both)
    for c in range(2):
        even = result[LANES * c : LANES * c + SEG]
        odd = result[LANES * c + SEG : LANES * (c + 1)]
        quot[c] = jnp.where(lane < SEG, even, odd)

    pltpu.make_async_copy(
        recv5.at[pl.ds(0, COLS - 1)], recv5.at[pl.ds(0, COLS - 1)], recv_sems.at[4]
    ).wait()
    for i in range(COLS):
        val[0, 8 * i : 8 * (i + 1)] = recv5[i, 0:8]
        val[1, 8 * i : 8 * (i + 1)] = recv5[i, 8:16]

    pltpu.make_async_copy(own_half, own_half, send_sems.at[0]).wait()
    pltpu.make_async_copy(gathered, gathered, send_sems.at[6]).wait()
    pltpu.make_async_copy(others, others, send_sems.at[1]).wait()
    pltpu.make_async_copy(
        send3.at[pl.ds(0, COLS - 1)], send3.at[pl.ds(0, COLS - 1)], send_sems.at[2]
    ).wait()

    @pl.when(here)
    def _():
        pltpu.make_async_copy(
            recv4.at[pl.ds(0, SEG - 1)], recv4.at[pl.ds(0, SEG - 1)], send_sems.at[3]
        ).wait()

    @pl.when(jnp.logical_not(here))
    def _():
        pltpu.make_async_copy(recv4, recv4, send_sems.at[3]).wait()

    for i in (4, 5):
        pltpu.make_async_copy(
            recv5.at[pl.ds(0, COLS - 1)], recv5.at[pl.ds(0, COLS - 1)], send_sems.at[i]
        ).wait()


def carry_out(ext, val, quot, ext_out, val_out, quot_out, sems):
    pieces = [(ext, ext_out), (val, val_out), (quot, quot_out)]
    moves = [pltpu.make_async_copy(src, dst, sems.at[i]) for i, (src, dst) in enumerate(pieces)]
    for move in moves:
        move.start()
    for move in moves:
        move.wait()


def shards(trace, step_coeff, pair_coeff, challenges):
    trace = trace.transpose(0, 2, 1)
    tables = build_tables()
    names = ["vectors", "into", "outof", "first", "twists", "spread", "mean", "last", "scales"]
    constants = [jnp.asarray(tables[name]) for name in names]
    operands = [
        pltpu.with_memory_space_constraint(x, pltpu.HBM)
        for x in (trace, step_coeff, pair_coeff, challenges, *constants)
    ]
    vmem = pltpu.VMEM
    hbm = pl.BlockSpec(memory_space=pltpu.HBM)
    inside = pl.BlockSpec(memory_space=pltpu.VMEM)
    outs = (
        jax.ShapeDtypeStruct((2, COLS, SEG, LANES), F32),
        jax.ShapeDtypeStruct((2, SEG, LANES), F32),
        jax.ShapeDtypeStruct((2, SEG, LANES), F32),
    )
    tables_scratch = [
        vmem(c.shape[1:] if n in ("vectors", "into", "outof") else c.shape, c.dtype)
        for n, c in zip(names, constants, strict=True)
    ]
    extension, values, quotient = pl.pallas_call(
        kernel,
        out_shape=tuple(vmem(o.shape, F32) for o in outs),
        in_specs=[hbm] * (4 + len(constants)),
        out_specs=(inside,) * 3,
        scratch_shapes=[
            vmem(trace.shape, F32),
            *tables_scratch,
            *[pltpu.SMEM((COLS,), F32)] * 3,
            vmem((SEG, 2, LANES), F32),
            vmem((2, SEG, 2, LANES), F32),
            vmem((9, HALF, 2, LANES), F32),
            vmem((9, HALF, 2, LANES), F32),
            vmem((COLS, 16, LANES), F32),
            vmem((COLS, 16, LANES), F32),
            vmem((8, 2, LANES), F32),
            vmem((SEG, 2, LANES), F32),
            vmem((16, LANES), F32),
            vmem((COLS, 16, LANES), F32),
            vmem((COLS, 16, LANES), F32),
            vmem((COLS, 16, LANES), F32),
            pltpu.SemaphoreType.DMA((13,)),
            pltpu.SemaphoreType.DMA((7,)),
            pltpu.SemaphoreType.DMA((7,)),
            pltpu.SemaphoreType.REGULAR,
        ],
        compiler_params=pltpu.CompilerParams(
            collective_id=0, has_side_effects=True, vmem_limit_bytes=32 * 1024 * 1024
        ),
    )(*operands)
    extension, values, quotient = pl.pallas_call(
        carry_out,
        out_shape=outs,
        in_specs=[inside] * 3,
        out_specs=(hbm,) * 3,
        scratch_shapes=[pltpu.SemaphoreType.DMA((3,))],
    )(*[pltpu.with_memory_space_constraint(x, vmem) for x in (extension, values, quotient)])
    return extension, values, quotient.reshape(2, 1, SEG * LANES)


def solution(mesh):
    placed = (P("col", None, "row"), P("col"), P("col"), P("col"))
    return jax.shard_map(
        shards,
        mesh=mesh,
        in_specs=placed,
        out_specs=(P(None, "col", None, "row"), P(None, None, "row"), P(None, "row", None)),
        check_vma=False,
    )
```

```python
import math

import jax
import jax.numpy as jnp
import numpy as np
from jax import lax
from jax.experimental import pallas as pl
from jax.experimental.pallas import tpu as pltpu
from jax.sharding import PartitionSpec as P

SEG = 64
HALF = 32
COLS = 8
PAIRS = 4
RUN = 32
LANES = 128
TRACE_LEN = SEG * SEG * RUN
COSET_LEN = 4 * TRACE_LEN
MESH = pl.DeviceIdType.MESH
F32 = jnp.float32
BF16 = jnp.bfloat16


def halves(matrix):
    high = matrix.astype(BF16)
    low = (matrix - high.astype(np.float64)).astype(BF16)
    return np.stack([high, low])


def complex_rows(angle):
    return np.stack([np.cos(angle), np.sin(angle)])


def real_form(angle, out_order, in_order):
    cosine, sine = np.cos(angle), np.sin(angle)
    grid = np.stack([np.stack([cosine, -sine]), np.stack([sine, cosine])])
    places = {"co": (0, 2), "oc": (2, 0), "ci": (1, 3), "ic": (3, 1)}
    rows, cols = angle.shape
    return grid.transpose(places[out_order] + places[in_order]).reshape(2 * rows, 2 * cols)


def build_tables():
    tau = 2.0 * np.pi
    seg = np.arange(SEG)
    run = np.arange(RUN)
    first = real_form(tau * np.outer(seg, seg) / SEG, "oc", "ci")
    final = first.T.reshape(2 * SEG, SEG // 2, 2, 2).transpose(0, 2, 1, 3).reshape(2 * SEG, 2 * SEG)
    lane = np.arange(LANES)
    offset = lane // 4 + (2 * (lane % 4) + 1) / 8.0
    rim = RUN + (2 * (lane % 4) + 1) / 8.0
    rim_here = (lane >= LANES - 16).astype(np.float64)
    beta = np.tile(run, PAIRS)
    deal = np.array([dealt(m, i) for i in range(COLS) for m in range(8)])
    summed = first.reshape(SEG, 2, 2 * SEG)[deal].reshape(2 * SEG, 2 * SEG)
    slots = np.concatenate([seg[0::2], seg[1::2]])
    matrices = []
    vectors = []
    for u in range(SEG):
        angle = tau * np.outer(SEG * seg + u, slots) / (SEG * SEG)
        matrices.append(real_form(angle, "co", "ic"))
        vectors.append(
            np.concatenate(
                [
                    complex_rows(tau * beta * u / TRACE_LEN),
                    complex_rows(-tau * offset * u / TRACE_LEN),
                    complex_rows(-tau * rim * u / TRACE_LEN),
                    complex_rows(tau * (2 * lane + 1) * u / (2 * COSET_LEN)),
                ]
            )
        )
    into, outof, turns = [], [], []
    for g in range(HALF):
        pair = (2 * g, 2 * g + 1)
        into.append(np.stack([halves(matrices[u]) for u in pair]))
        for zh in range(2):
            rows = slice(SEG * zh, SEG * (zh + 1))
            outof.append(np.stack([halves(matrices[u].T[rows]) for u in pair]))
            turns.append(np.concatenate([vectors[u][:6] for u in pair] + [vectors[2 * g + zh][6:]]))
    vectors = np.pad(np.stack(turns), ((0, 0), (0, 2), (0, 0)))
    twist_in = complex_rows(tau * beta * (64 * seg[:, None] - 2048) / TRACE_LEN)
    twist_out = complex_rows(-tau * offset * (64 * seg[:, None] - 2048) / TRACE_LEN) / TRACE_LEN
    twist_rim = (
        complex_rows(-tau * rim * (64 * seg[:, None] - 2048) / TRACE_LEN) / TRACE_LEN * rim_here
    )
    twist_quot = complex_rows(
        tau * (2 * lane + 1) * (64 * seg[:, None]) / (2 * COSET_LEN)
    ) / math.sqrt(COSET_LEN)
    twists = np.concatenate([twist_in, twist_out, twist_rim, twist_quot])
    spread = np.zeros((PAIRS, RUN, 5, LANES))
    mean = np.zeros((PAIRS, RUN, LANES))
    for j in range(PAIRS):
        spread[j, :, j, :] = 1.0 / np.sin(np.pi * (offset[None, :] - run[:, None]) / RUN)
        own = (lane >= LANES - 16) & ((lane - (LANES - 16)) // 4 == j)
        spread[j, :, 4, :] = own / np.sin(np.pi * (rim[None, :] - run[:, None]) / RUN)
        mean[j, :, j] = 1.0 / TRACE_LEN
    spread = spread.reshape(LANES, 5 * LANES)
    half = np.arange(SEG)
    order = np.concatenate([2 * half, 2 * half + 1])
    last = real_form(tau * np.outer(order, 2 * lane + 1) / 256.0, "co", "ci")
    shape = (2 * (lane % 4) + 1) / 8.0
    gain = np.exp(-1j * np.pi * shape) * np.sin(np.pi * shape)
    vanish = 1.0 / (np.exp(-1j * np.pi * (2 * (lane % 4) + 1) / 4.0) - 1.0)
    scales = []
    for value in (gain, gain * vanish, gain * gain * vanish):
        scales += [value.real, value.imag]
    scales += [np.zeros(LANES)] * 2
    return {
        "vectors": vectors.astype(np.float32),
        "into": np.stack(into),
        "outof": np.stack(outof),
        "first": np.stack([halves(first), halves(final), halves(summed)]),
        "twists": twists.astype(np.float32),
        "spread": halves(spread),
        "mean": mean.reshape(LANES, LANES).astype(BF16),
        "last": halves(last),
        "scales": np.stack(scales).astype(np.float32),
    }


def parts_of(value):
    high = value.astype(BF16)
    low = (value - high.astype(F32)).astype(BF16)
    return high, low


def left_dot(table, value):
    high, low = parts_of(value)
    left = jnp.concatenate([table[0], table[0], table[1]], axis=1)
    right = jnp.concatenate([high, low, high], axis=0)
    return jnp.dot(left, right, preferred_element_type=F32)


def left_dot_turned(table, value):
    high, low = parts_of(value)
    return lax.dot_general(
        jnp.concatenate([table[0], table[0], table[1]], axis=1),
        jnp.concatenate([high, low, high], axis=1),
        (((1,), (1,)), ((), ())),
        preferred_element_type=F32,
    )


def right_dot(value, table):
    high, low = parts_of(value)
    left = jnp.concatenate([high, low, high], axis=1)
    right = jnp.concatenate([table[0], table[0], table[1]], axis=0)
    return jnp.dot(left, right, preferred_element_type=F32)


def ring_step(k, me):
    yi, xi, zi = k & 7, (k >> 3) & 3, k >> 5
    half = (yi + 1) >> 1
    dy = 4 + half * (1 - 2 * (yi & 1))
    dx = (xi ^ (xi >> 1)) ^ 2
    dz = 1 - zi
    return ((me + 8 * dy) & 56) | ((me + 2 * dx) & 6) | ((me ^ dz) & 1)


def dealt(m, col):
    return 8 * m + 2 * ((m + (col >> 1) + 2) & 3) + (((m >> 2) ^ col ^ 1) & 1)


def turn(real, imag, cosine, sine):
    return real * cosine - imag * sine, real * sine + imag * cosine


def kernel(
    trace_hbm, step_hbm, pair_hbm, chal_hbm,
    vectors_hbm, into_hbm, outof_hbm, first_hbm, twists_hbm, spread_hbm, mean_hbm, last_hbm, scales_hbm,
    ext, val, arrived_rows, own_into, last, spin,
    trace, vectors, into, outof, first, twists, spread, mean, scales,
    step_ref, pair_ref, chal_ref,
    send1, recv1, send2, recv2, send3, recv3, send4, recv4, send5, recv5, send6, recv6,
    load_sems, send_sems, recv_sems, ready,
):
    me = lax.axis_index("row")
    col = lax.axis_index("col")
    group, far = me >> 1, me & 1
    slot = HALF * far + group

    barrier = pltpu.get_barrier_semaphore()

    def greet_row(k, carry):
        pl.semaphore_signal(
            barrier, inc=1, device_id={"row": ring_step(k, me)}, device_id_type=MESH
        )
        return carry

    def greet_col(k, carry):
        pl.semaphore_signal(
            barrier, inc=1, device_id={"col": (col + k) & 7}, device_id_type=MESH
        )
        return carry

    lax.fori_loop(HALF, SEG - 1, greet_row, 0)
    lax.fori_loop(1, COLS, greet_col, 0)

    @pl.when(far == 0)
    def _():
        lax.fori_loop(0, HALF, greet_row, 0)


    loads = [
        pltpu.make_async_copy(src, dst, load_sems.at[i])
        for i, (src, dst) in enumerate(
            [
                (trace_hbm, trace),
                (first_hbm, first),
                (vectors_hbm.at[me], vectors),
                (into_hbm.at[group], into),
                (outof_hbm.at[me], outof),
                (twists_hbm, twists),
                (spread_hbm, spread),
                (mean_hbm, mean),
                (scales_hbm, scales),
                (last_hbm, last),
                (step_hbm, step_ref),
                (pair_hbm, pair_ref),
                (chal_hbm, chal_ref),
            ]
        )
    ]
    for load in loads:
        load.start()

    loads[0].wait()
    loads[1].wait()
    grid = jnp.concatenate(
        [
            jnp.concatenate([trace[2 * j + c] for j in range(PAIRS)], axis=0)
            for c in range(2)
        ],
        axis=1,
    )
    head = left_dot_turned(first[0], grid)
    send1.reshape(LANES, LANES)[...] = head
    for c in range(2):
        recv1[c, slot] = send1[2 * group + c]
    pl.semaphore_wait(barrier, HALF - 1 + COLS - 1 + HALF * far)

    def post1(k, to):
        peer = ring_step(k, me)
        pltpu.make_async_remote_copy(
            src_ref=send1.at[pl.ds(2 * (peer >> 1), 2)], dst_ref=recv1.at[:, slot],
            send_sem=send_sems.at[to], recv_sem=recv_sems.at[to],
            device_id={"row": peer}, device_id_type=MESH,
        ).start()
        return to

    @pl.when(far == 1)
    def _():
        pl.semaphore_signal(ready, inc=1, device_id={"row": me ^ 1}, device_id_type=MESH)
        lax.fori_loop(0, HALF, post1, 6)

    lax.fori_loop(HALF, SEG - 1, post1, 0)

    for load in loads[2:]:
        load.wait()
    def table(index, row):
        base = twists[2 * index], twists[2 * index + 1]
        return turn(*base, vectors[2 * row : 2 * row + 1], vectors[2 * row + 1 : 2 * row + 2])

    turn_in = [table(0, 3 * c) for c in range(2)]
    turn_out = [table(1, 3 * c + 1) for c in range(2)]
    turn_rim = [table(2, 3 * c + 2) for c in range(2)]

    own_half = recv1.at[:, pl.ds(0, HALF - 1)]
    pltpu.make_async_copy(own_half, own_half, recv_sems.at[0]).wait()
    gathered = recv1.at[:, pl.ds(0, HALF)]

    @pl.when(far == 0)
    def _():
        pl.semaphore_wait(ready, 1)
        pltpu.make_async_remote_copy(
            src_ref=gathered, dst_ref=gathered,
            send_sem=send_sems.at[6], recv_sem=recv_sems.at[6],
            device_id={"row": me ^ 1}, device_id_type=MESH,
        ).start()

    pltpu.make_async_copy(gathered, gathered, recv_sems.at[6]).wait()

    rows = []
    for c in range(2):
        mixed = left_dot(into[c], recv1.reshape(2, LANES, LANES)[c])
        if c == 0:
            lowest = jnp.concatenate([mixed[0:8], mixed[SEG : SEG + 8]], axis=0)
        rows += turn(mixed[:SEG], mixed[SEG:], *turn_in[c])
    wide = right_dot(jnp.concatenate(rows, axis=0), spread)
    high, low = parts_of(lowest)
    sums = jnp.dot(high, mean[...], preferred_element_type=F32) + jnp.dot(
        low, mean[...], preferred_element_type=F32
    )
    sums = sums * jnp.where(group == 0, 1.0, 0.0).astype(F32)
    parity = lax.broadcasted_iota(jnp.int32, (SEG, LANES), 0) % 2
    sums = jnp.where(parity == 0, sums[0:1], sums[8:9])
    for c in range(2):
        pieces = []
        for j in range(5):
            part = wide[LANES * c : LANES * (c + 1), LANES * j : LANES * (j + 1)]
            real, imag = turn(part[:SEG], part[SEG:], *(turn_out[c] if j < 4 else turn_rim[c]))
            pieces.append(jnp.concatenate([real, imag], axis=0))
        back = left_dot(outof[c], jnp.concatenate(pieces, axis=1))
        for j in range(5):
            part = back[:, LANES * j : LANES * (j + 1)]
            if j < 4:
                send2.reshape(9, SEG, LANES)[2 * j + c] = part
            elif c == 0:
                rest = part + sums
            else:
                send2.reshape(9, SEG, LANES)[8] = rest + pltpu.roll(part, SEG, 1)
    for i in range(9):
        recv2[i, group] = send2[i, group]

    def post2(k, carry):
        peer = ring_step(k, me)
        pltpu.make_async_remote_copy(
            src_ref=send2.at[:, peer >> 1], dst_ref=recv2.at[:, group],
            send_sem=send_sems.at[1], recv_sem=recv_sems.at[1],
            device_id={"row": peer}, device_id_type=MESH,
        ).start()
        return carry

    lax.fori_loop(HALF, SEG - 1, post2, 0)
    spin[0], spin[1] = table(3, 6)
    own_into[...] = into[far]
    others = recv2.at[:, pl.ds(0, HALF - 1)]
    pltpu.make_async_copy(others, others, recv_sems.at[1]).wait()

    blocks = [recv2.reshape(9, SEG, LANES)[i] for i in range(9)]
    blocks.append(pltpu.roll(blocks[8], SEG, 1))
    arrived = jnp.concatenate(
        [jnp.concatenate(blocks[2 * j : 2 * j + 2], axis=0) for j in range(5)], axis=1
    )
    field = left_dot(first[1], arrived)

    def scale(row):
        return scales[2 * row : 2 * row + 1], scales[2 * row + 1 : 2 * row + 2]

    rim_part = field[:, 4 * LANES :]
    lane = lax.broadcasted_iota(jnp.int32, (SEG, LANES), 1)
    gain_real, gain_imag = scale(0)
    ahead = jnp.zeros((SEG, LANES), F32)
    own = jnp.zeros((SEG, LANES), F32)
    product = jnp.zeros((SEG, LANES), F32)
    cross = jnp.zeros((SEG, LANES), F32)
    rim_weight = [jnp.zeros((SEG, LANES), F32)] * 2
    columns = []
    level_ahead = jnp.zeros((1, 1), F32)
    level_own = jnp.zeros((1, 1), F32)
    level_product = jnp.zeros((1, 1), F32)
    for j in range(PAIRS):
        mean_c = rim_part[0:1, j : j + 1]
        mean_d = rim_part[SEG : SEG + 1, j : j + 1]
        chal_c, chal_d = chal_ref[2 * j], chal_ref[2 * j + 1]
        step_c, step_d = chal_c * step_ref[2 * j], chal_d * step_ref[2 * j + 1]
        weight = chal_c * pair_ref[2 * j] + chal_d * pair_ref[2 * j + 1]
        raw_c = field[:SEG, LANES * j : LANES * (j + 1)]
        raw_d = field[SEG:, LANES * j : LANES * (j + 1)]
        real_c = raw_c + mean_d
        real_d = raw_d - mean_c
        columns += [(real_c, mean_c), (real_d, mean_d)]
        ahead += chal_c * raw_c + chal_d * raw_d
        own += step_c * real_c + step_d * real_d
        product += weight * (real_c * real_d)
        cross += weight * (real_c * mean_d + real_d * mean_c)
        group = (lane >= LANES - 16 + 4 * j) & (lane < LANES - 12 + 4 * j)
        rim_weight = [
            jnp.where(group, chal_c, rim_weight[0]),
            jnp.where(group, chal_d, rim_weight[1]),
        ]
        level_ahead += chal_c * mean_d - chal_d * mean_c
        level_own += (chal_c - step_c) * mean_c + (chal_d - step_d) * mean_d
        level_product += weight * (mean_c * mean_d)
    rim_sum = rim_part[:SEG] * rim_weight[0] + rim_part[SEG:] * rim_weight[1]
    rim_sum = rim_sum + pltpu.roll(rim_sum, 4, 1)
    rim_sum = rim_sum + pltpu.roll(rim_sum, 8, 1)
    ahead = jnp.where(lane < LANES - 4, pltpu.roll(ahead, LANES - 4, 1), rim_sum)
    line_real = ahead + level_ahead - own
    line_imag = level_own
    square_real = product - level_product
    square_imag = cross
    line_scale, square_scale = scale(1), scale(2)
    value_real = (
        line_scale[0] * line_real
        - line_scale[1] * line_imag
        - square_scale[0] * square_real
        + square_scale[1] * square_imag
    )
    value_imag = (
        line_scale[0] * line_imag
        + line_scale[1] * line_real
        - square_scale[0] * square_imag
        - square_scale[1] * square_real
    )
    mixed = left_dot(first[2], jnp.concatenate([value_real, value_imag], axis=0))
    for i in range(COLS):
        send3[i] = mixed[16 * i : 16 * (i + 1)]

    def post3(k, carry):
        peer = (col + k) & 7
        pltpu.make_async_remote_copy(
            src_ref=send3.at[peer], dst_ref=recv3.at[col],
            send_sem=send_sems.at[2], recv_sem=recv_sems.at[2],
            device_id={"col": peer}, device_id_type=MESH,
        ).start()
        return carry

    lax.fori_loop(1, COLS, post3, 0)
    for i in range(COLS):
        send6[i, 0:8] = value_real[8 * i : 8 * (i + 1)]
        send6[i, 8:16] = value_imag[8 * i : 8 * (i + 1)]

    def post6(k, carry):
        peer = (col + k) & 7
        pltpu.make_async_remote_copy(
            src_ref=send6.at[peer], dst_ref=recv6.at[col],
            send_sem=send_sems.at[5], recv_sem=recv_sems.at[5],
            device_id={"col": peer}, device_id_type=MESH,
        ).start()
        return carry

    lax.fori_loop(1, COLS, post6, 0)
    recv3[col] = send3[col]
    recv6[col] = send6[col]
    for c, (real, mean_here) in enumerate(columns):
        ext[0, c] = gain_real * real - gain_imag * mean_here
        ext[1, c] = gain_imag * real + gain_real * mean_here
    pltpu.make_async_copy(
        recv3.at[pl.ds(0, COLS - 1)], recv3.at[pl.ds(0, COLS - 1)], recv_sems.at[2]
    ).wait()
    total = recv3[0]
    for i in range(1, COLS):
        total = total + recv3[i]
    send4.reshape(16, LANES)[...] = total

    here = dealt(me >> 3, col) == me

    def post4(k, carry):
        across = ((k >> 2) & 7) ^ 1
        line = (k & 3) ^ (7 * (((k >> 5) ^ col ^ 1) & 1))
        target = dealt(line, col)
        alone = (target == me) & (across == col)

        @pl.when(jnp.logical_not(alone))
        def _():
            pltpu.make_async_remote_copy(
                src_ref=send4.at[line], dst_ref=recv4.at[slot],
                send_sem=send_sems.at[3], recv_sem=recv_sems.at[3],
                device_id={"col": across, "row": target}, device_id_type=MESH,
            ).start()

        @pl.when(alone)
        def _():
            pltpu.make_async_copy(send4.at[line], recv4.at[slot], recv_sems.at[3]).start()

        return carry

    lax.fori_loop(0, SEG, post4, 0)
    pltpu.make_async_copy(
        recv6.at[pl.ds(0, COLS - 1)], recv6.at[pl.ds(0, COLS - 1)], recv_sems.at[5]
    ).wait()
    value = recv6[0]
    for i in range(1, COLS):
        value = value + recv6[i]
    send5[...] = value

    def post5(k, carry):
        pltpu.make_async_remote_copy(
            src_ref=send5, dst_ref=recv5.at[col],
            send_sem=send_sems.at[4], recv_sem=recv_sems.at[4],
            device_id={"col": (col + k) & 7}, device_id_type=MESH,
        ).start()
        return carry

    lax.fori_loop(1, COLS, post5, 0)
    recv5[col] = send5[...]

    pltpu.make_async_copy(recv4, recv4, recv_sems.at[3]).wait()
    arrived_rows[...] = recv4.reshape(LANES, LANES)[...]
    pltpu.make_async_copy(
        recv5.at[pl.ds(0, COLS - 1)], recv5.at[pl.ds(0, COLS - 1)], recv_sems.at[4]
    ).wait()
    for i in range(COLS):
        val[0, 8 * i : 8 * (i + 1)] = recv5[i, 0:8]
        val[1, 8 * i : 8 * (i + 1)] = recv5[i, 8:16]

    pltpu.make_async_copy(own_half, own_half, send_sems.at[0]).wait()
    pltpu.make_async_copy(gathered, gathered, send_sems.at[6]).wait()
    pltpu.make_async_copy(others, others, send_sems.at[1]).wait()
    pltpu.make_async_copy(
        send3.at[pl.ds(0, COLS - 1)], send3.at[pl.ds(0, COLS - 1)], send_sems.at[2]
    ).wait()

    @pl.when(here)
    def _():
        pltpu.make_async_copy(
            recv4.at[pl.ds(0, SEG - 1)], recv4.at[pl.ds(0, SEG - 1)], send_sems.at[3]
        ).wait()

    @pl.when(jnp.logical_not(here))
    def _():
        pltpu.make_async_copy(recv4, recv4, send_sems.at[3]).wait()

    for i in (4, 5):
        pltpu.make_async_copy(
            recv5.at[pl.ds(0, COLS - 1)], recv5.at[pl.ds(0, COLS - 1)], send_sems.at[i]
        ).wait()


def finish(
    ext, val, arrived_rows, own_into, last, spin, ext_out, val_out, quot_out, quot, sems
):
    pairs = [(ext, ext_out), (val, val_out), (quot, quot_out)]
    moves = [pltpu.make_async_copy(src, dst, sems.at[i]) for i, (src, dst) in enumerate(pairs)]
    moves[0].start()
    moves[1].start()
    mixed = left_dot(own_into, arrived_rows[...])
    real, imag = turn(mixed[:SEG], mixed[SEG:], spin[0], spin[1])
    both = jnp.concatenate([real, imag], axis=1)
    both = jnp.concatenate([both, both], axis=0)
    result = left_dot_turned(last, both)
    lane = lax.broadcasted_iota(jnp.int32, (SEG, LANES), 1)
    for c in range(2):
        even = result[LANES * c : LANES * c + SEG]
        odd = result[LANES * c + SEG : LANES * (c + 1)]
        quot[c] = jnp.where(lane < SEG, even, odd)
    moves[2].start()
    for move in moves:
        move.wait()


def shards(trace, step_coeff, pair_coeff, challenges):
    trace = trace.transpose(0, 2, 1)
    tables = build_tables()
    names = ["vectors", "into", "outof", "first", "twists", "spread", "mean", "last", "scales"]
    constants = [jnp.asarray(tables[name]) for name in names]
    operands = [
        pltpu.with_memory_space_constraint(x, pltpu.HBM)
        for x in (trace, step_coeff, pair_coeff, challenges, *constants)
    ]
    vmem = pltpu.VMEM
    hbm = pl.BlockSpec(memory_space=pltpu.HBM)
    inside = pl.BlockSpec(memory_space=pltpu.VMEM)
    outs = (
        jax.ShapeDtypeStruct((2, COLS, SEG, LANES), F32),
        jax.ShapeDtypeStruct((2, SEG, LANES), F32),
        jax.ShapeDtypeStruct((2, SEG, LANES), F32),
    )
    tables_scratch = [
        vmem(c.shape[1:] if n in ("vectors", "into", "outof") else c.shape, c.dtype)
        for n, c in zip(names, constants, strict=True)
        if n != "last"
    ]
    passed = pl.pallas_call(
        kernel,
        out_shape=(
            vmem(outs[0].shape, F32),
            vmem(outs[1].shape, F32),
            vmem((LANES, LANES), F32),
            vmem((2, LANES, LANES), BF16),
            vmem((2, 2 * LANES, 2 * LANES), BF16),
            vmem((2, SEG, LANES), F32),
        ),
        in_specs=[hbm] * (4 + len(constants)),
        out_specs=(inside,) * 6,
        scratch_shapes=[
            vmem(trace.shape, F32),
            *tables_scratch,
            *[pltpu.SMEM((COLS,), F32)] * 3,
            vmem((SEG, 2, LANES), F32),
            vmem((2, SEG, 2, LANES), F32),
            vmem((9, HALF, 2, LANES), F32),
            vmem((9, HALF, 2, LANES), F32),
            vmem((COLS, 16, LANES), F32),
            vmem((COLS, 16, LANES), F32),
            vmem((8, 2, LANES), F32),
            vmem((SEG, 2, LANES), F32),
            vmem((16, LANES), F32),
            vmem((COLS, 16, LANES), F32),
            vmem((COLS, 16, LANES), F32),
            vmem((COLS, 16, LANES), F32),
            pltpu.SemaphoreType.DMA((13,)),
            pltpu.SemaphoreType.DMA((7,)),
            pltpu.SemaphoreType.DMA((7,)),
            pltpu.SemaphoreType.REGULAR,
        ],
        compiler_params=pltpu.CompilerParams(
            collective_id=0, has_side_effects=True, vmem_limit_bytes=32 * 1024 * 1024
        ),
    )(*operands)
    extension, values, quotient = pl.pallas_call(
        finish,
        out_shape=outs,
        in_specs=[inside] * 6,
        out_specs=(hbm,) * 3,
        scratch_shapes=[vmem(outs[2].shape, F32), pltpu.SemaphoreType.DMA((3,))],
    )(*[pltpu.with_memory_space_constraint(x, vmem) for x in passed])
    return extension, values, quotient.reshape(2, 1, SEG * LANES)


def solution(mesh):
    placed = (P("col", None, "row"), P("col"), P("col"), P("col"))
    return jax.shard_map(
        shards,
        mesh=mesh,
        in_specs=placed,
        out_specs=(P(None, "col", None, "row"), P(None, None, "row"), P(None, "row", None)),
        check_vma=False,
    )
```

```python
import math

import jax
import jax.numpy as jnp
import numpy as np
from jax import lax
from jax.experimental import pallas as pl
from jax.experimental.pallas import tpu as pltpu
from jax.sharding import PartitionSpec as P

SEG = 64
HALF = 32
COLS = 8
PAIRS = 4
RUN = 32
LANES = 128
TRACE_LEN = SEG * SEG * RUN
COSET_LEN = 4 * TRACE_LEN
MESH = pl.DeviceIdType.MESH
F32 = jnp.float32
BF16 = jnp.bfloat16


def halves(matrix):
    high = matrix.astype(BF16)
    low = (matrix - high.astype(np.float64)).astype(BF16)
    return np.stack([high, low])


def complex_rows(angle):
    return np.stack([np.cos(angle), np.sin(angle)])


def real_form(angle, out_order, in_order):
    cosine, sine = np.cos(angle), np.sin(angle)
    grid = np.stack([np.stack([cosine, -sine]), np.stack([sine, cosine])])
    places = {"co": (0, 2), "oc": (2, 0), "ci": (1, 3), "ic": (3, 1)}
    rows, cols = angle.shape
    return grid.transpose(places[out_order] + places[in_order]).reshape(2 * rows, 2 * cols)


def build_tables():
    tau = 2.0 * np.pi
    seg = np.arange(SEG)
    run = np.arange(RUN)
    first = real_form(tau * np.outer(seg, seg) / SEG, "oc", "ci")
    final = first.T.reshape(2 * SEG, SEG // 2, 2, 2).transpose(0, 2, 1, 3).reshape(2 * SEG, 2 * SEG)
    lane = np.arange(LANES)
    offset = lane // 4 + (2 * (lane % 4) + 1) / 8.0
    rim = RUN + (2 * (lane % 4) + 1) / 8.0
    rim_here = (lane >= LANES - 16).astype(np.float64)
    beta = np.tile(run, PAIRS)
    deal = np.array([dealt(m, i) for i in range(COLS) for m in range(8)])
    summed = first.reshape(SEG, 2, 2 * SEG)[deal].reshape(2 * SEG, 2 * SEG)
    slots = np.concatenate([seg[0::2], seg[1::2]])
    matrices = []
    vectors = []
    for u in range(SEG):
        angle = tau * np.outer(SEG * seg + u, slots) / (SEG * SEG)
        matrices.append(real_form(angle, "co", "ic"))
        vectors.append(
            np.concatenate(
                [
                    complex_rows(tau * beta * u / TRACE_LEN),
                    complex_rows(-tau * offset * u / TRACE_LEN),
                    complex_rows(-tau * rim * u / TRACE_LEN),
                    complex_rows(tau * (2 * lane + 1) * u / (2 * COSET_LEN)),
                ]
            )
        )
    into, outof, turns = [], [], []
    for g in range(HALF):
        pair = (2 * g, 2 * g + 1)
        into.append(np.stack([halves(matrices[u]) for u in pair]))
        for zh in range(2):
            rows = slice(SEG * zh, SEG * (zh + 1))
            outof.append(np.stack([halves(matrices[u].T[rows]) for u in pair]))
            turns.append(np.concatenate([vectors[u][:6] for u in pair] + [vectors[2 * g + zh][6:]]))
    vectors = np.pad(np.stack(turns), ((0, 0), (0, 2), (0, 0)))
    twist_in = complex_rows(tau * beta * (64 * seg[:, None] - 2048) / TRACE_LEN)
    twist_out = complex_rows(-tau * offset * (64 * seg[:, None] - 2048) / TRACE_LEN) / TRACE_LEN
    twist_rim = (
        complex_rows(-tau * rim * (64 * seg[:, None] - 2048) / TRACE_LEN) / TRACE_LEN * rim_here
    )
    twist_quot = complex_rows(
        tau * (2 * lane + 1) * (64 * seg[:, None]) / (2 * COSET_LEN)
    ) / math.sqrt(COSET_LEN)
    twists = np.concatenate([twist_in, twist_out, twist_rim, twist_quot])
    spread = np.zeros((PAIRS, RUN, 5, LANES))
    mean = np.zeros((PAIRS, RUN, LANES))
    for j in range(PAIRS):
        spread[j, :, j, :] = 1.0 / np.sin(np.pi * (offset[None, :] - run[:, None]) / RUN)
        own = (lane >= LANES - 16) & ((lane - (LANES - 16)) // 4 == j)
        spread[j, :, 4, :] = own / np.sin(np.pi * (rim[None, :] - run[:, None]) / RUN)
        mean[j, :, j] = 1.0 / TRACE_LEN
    spread = spread.reshape(LANES, 5 * LANES)
    half = np.arange(SEG)
    order = np.concatenate([2 * half, 2 * half + 1])
    last = real_form(tau * np.outer(order, 2 * lane + 1) / 256.0, "co", "ci")
    shape = (2 * (lane % 4) + 1) / 8.0
    gain = np.exp(-1j * np.pi * shape) * np.sin(np.pi * shape)
    vanish = 1.0 / (np.exp(-1j * np.pi * (2 * (lane % 4) + 1) / 4.0) - 1.0)
    scales = []
    for value in (gain, gain * vanish, gain * gain * vanish):
        scales += [value.real, value.imag]
    scales += [np.zeros(LANES)] * 2
    return {
        "vectors": vectors.astype(np.float32),
        "into": np.stack(into),
        "outof": np.stack(outof),
        "first": np.stack([halves(first), halves(final), halves(summed)]),
        "twists": twists.astype(np.float32),
        "spread": halves(spread),
        "mean": mean.reshape(LANES, LANES).astype(BF16),
        "last": halves(last),
        "scales": np.stack(scales).astype(np.float32),
    }


def parts_of(value):
    high = value.astype(BF16)
    low = (value - high.astype(F32)).astype(BF16)
    return high, low


def left_dot(table, value):
    high, low = parts_of(value)
    left = jnp.concatenate([table[0], table[0], table[1]], axis=1)
    right = jnp.concatenate([high, low, high], axis=0)
    return jnp.dot(left, right, preferred_element_type=F32)


def left_dot_turned(table, value):
    high, low = parts_of(value)
    return lax.dot_general(
        jnp.concatenate([table[0], table[0], table[1]], axis=1),
        jnp.concatenate([high, low, high], axis=1),
        (((1,), (1,)), ((), ())),
        preferred_element_type=F32,
    )


def right_dot(value, table):
    high, low = parts_of(value)
    left = jnp.concatenate([high, low, high], axis=1)
    right = jnp.concatenate([table[0], table[0], table[1]], axis=0)
    return jnp.dot(left, right, preferred_element_type=F32)


def ring_step(k, me):
    yi, xi, zi = k & 7, (k >> 3) & 3, k >> 5
    half = (yi + 1) >> 1
    dy = 4 + half * (1 - 2 * (yi & 1))
    dx = (xi ^ (xi >> 1)) ^ 2
    dz = 1 - zi
    return ((me + 8 * dy) & 56) | ((me + 2 * dx) & 6) | ((me ^ dz) & 1)


def dealt(m, col):
    return 8 * m + 2 * ((m + (col >> 1) + 2) & 3) + (((m >> 2) ^ col ^ 1) & 1)


def turn(real, imag, cosine, sine):
    return real * cosine - imag * sine, real * sine + imag * cosine


def kernel(
    trace_hbm, step_hbm, pair_hbm, chal_hbm,
    vectors_hbm, into_hbm, outof_hbm, first_hbm, twists_hbm, spread_hbm, mean_hbm, last_hbm, scales_hbm,
    ext, val, arrived_rows, own_into, last, spin,
    trace, vectors, into, outof, first, twists, spread, mean, scales,
    step_ref, pair_ref, chal_ref,
    send1, recv1, send2, recv2, send3, recv3, send4, recv4, send5, recv5, send6, recv6,
    load_sems, send_sems, recv_sems, ready,
):
    me = lax.axis_index("row")
    col = lax.axis_index("col")
    group, far = me >> 1, me & 1
    slot = HALF * far + group

    barrier = pltpu.get_barrier_semaphore()

    def greet_row(k, carry):
        pl.semaphore_signal(
            barrier, inc=1, device_id={"row": ring_step(k, me)}, device_id_type=MESH
        )
        return carry

    def greet_col(k, carry):
        pl.semaphore_signal(
            barrier, inc=1, device_id={"col": (col + k) & 7}, device_id_type=MESH
        )
        return carry

    lax.fori_loop(HALF, SEG - 1, greet_row, 0)
    lax.fori_loop(1, COLS, greet_col, 0)

    @pl.when(far == 0)
    def _():
        lax.fori_loop(0, HALF, greet_row, 0)


    loads = [
        pltpu.make_async_copy(src, dst, load_sems.at[i])
        for i, (src, dst) in enumerate(
            [
                (trace_hbm, trace),
                (first_hbm, first),
                (vectors_hbm.at[me], vectors),
                (into_hbm.at[group], into),
                (outof_hbm.at[me], outof),
                (twists_hbm, twists),
                (spread_hbm, spread),
                (mean_hbm, mean),
                (scales_hbm, scales),
                (last_hbm, last),
                (step_hbm, step_ref),
                (pair_hbm, pair_ref),
                (chal_hbm, chal_ref),
            ]
        )
    ]
    for load in loads:
        load.start()

    loads[0].wait()
    loads[1].wait()
    grid = jnp.concatenate(
        [
            jnp.concatenate([trace[2 * j + c] for j in range(PAIRS)], axis=0)
            for c in range(2)
        ],
        axis=1,
    )
    head = left_dot_turned(first[0], grid)
    send1.reshape(LANES, LANES)[...] = head
    for c in range(2):
        recv1[c, slot] = send1[2 * group + c]
    pl.semaphore_wait(barrier, HALF - 1 + COLS - 1 + HALF * far)

    def post1(k, to):
        peer = ring_step(k, me)
        pltpu.make_async_remote_copy(
            src_ref=send1.at[pl.ds(2 * (peer >> 1), 2)], dst_ref=recv1.at[:, slot],
            send_sem=send_sems.at[to], recv_sem=recv_sems.at[to],
            device_id={"row": peer}, device_id_type=MESH,
        ).start()
        return to

    @pl.when(far == 1)
    def _():
        pl.semaphore_signal(ready, inc=1, device_id={"row": me ^ 1}, device_id_type=MESH)
        lax.fori_loop(0, HALF, post1, 6)

    lax.fori_loop(HALF, SEG - 1, post1, 0)

    for load in loads[2:]:
        load.wait()
    def table(index, row):
        base = twists[2 * index], twists[2 * index + 1]
        return turn(*base, vectors[2 * row : 2 * row + 1], vectors[2 * row + 1 : 2 * row + 2])

    turn_in = [table(0, 3 * c) for c in range(2)]
    turn_out = [table(1, 3 * c + 1) for c in range(2)]
    turn_rim = [table(2, 3 * c + 2) for c in range(2)]

    own_half = recv1.at[:, pl.ds(0, HALF - 1)]
    pltpu.make_async_copy(own_half, own_half, recv_sems.at[0]).wait()
    gathered = recv1.at[:, pl.ds(0, HALF)]

    @pl.when(far == 0)
    def _():
        pl.semaphore_wait(ready, 1)
        pltpu.make_async_remote_copy(
            src_ref=gathered, dst_ref=gathered,
            send_sem=send_sems.at[6], recv_sem=recv_sems.at[6],
            device_id={"row": me ^ 1}, device_id_type=MESH,
        ).start()

    pltpu.make_async_copy(gathered, gathered, recv_sems.at[6]).wait()

    rows = []
    for c in range(2):
        mixed = left_dot(into[c], recv1.reshape(2, LANES, LANES)[c])
        if c == 0:
            lowest = jnp.concatenate([mixed[0:8], mixed[SEG : SEG + 8]], axis=0)
        rows += turn(mixed[:SEG], mixed[SEG:], *turn_in[c])
    wide = right_dot(jnp.concatenate(rows, axis=0), spread)
    high, low = parts_of(lowest)
    sums = jnp.dot(high, mean[...], preferred_element_type=F32) + jnp.dot(
        low, mean[...], preferred_element_type=F32
    )
    sums = sums * jnp.where(group == 0, 1.0, 0.0).astype(F32)
    parity = lax.broadcasted_iota(jnp.int32, (SEG, LANES), 0) % 2
    sums = jnp.where(parity == 0, sums[0:1], sums[8:9])
    for c in range(2):
        pieces = []
        for j in range(5):
            part = wide[LANES * c : LANES * (c + 1), LANES * j : LANES * (j + 1)]
            real, imag = turn(part[:SEG], part[SEG:], *(turn_out[c] if j < 4 else turn_rim[c]))
            pieces.append(jnp.concatenate([real, imag], axis=0))
        back = left_dot(outof[c], jnp.concatenate(pieces, axis=1))
        for j in range(5):
            part = back[:, LANES * j : LANES * (j + 1)]
            if j < 4:
                send2.reshape(9, SEG, LANES)[2 * j + c] = part
            elif c == 0:
                rest = part + sums
            else:
                send2.reshape(9, SEG, LANES)[8] = rest + pltpu.roll(part, SEG, 1)
    def post2(k, carry):
        peer = ring_step(k, me)
        pltpu.make_async_remote_copy(
            src_ref=send2.at[:, peer >> 1], dst_ref=recv2.at[:, group],
            send_sem=send_sems.at[1], recv_sem=recv_sems.at[1],
            device_id={"row": peer}, device_id_type=MESH,
        ).start()
        return carry

    lax.fori_loop(HALF, SEG - 1, post2, 0)
    for i in range(9):
        recv2[i, group] = send2[i, group]
    spin[0], spin[1] = table(3, 6)
    own_into[...] = into[far]
    others = recv2.at[:, pl.ds(0, HALF - 1)]
    pltpu.make_async_copy(others, others, recv_sems.at[1]).wait()

    blocks = [recv2.reshape(9, SEG, LANES)[i] for i in range(9)]
    blocks.append(pltpu.roll(blocks[8], SEG, 1))
    arrived = jnp.concatenate(
        [jnp.concatenate(blocks[2 * j : 2 * j + 2], axis=0) for j in range(5)], axis=1
    )
    field = left_dot(first[1], arrived)

    def scale(row):
        return scales[2 * row : 2 * row + 1], scales[2 * row + 1 : 2 * row + 2]

    rim_part = field[:, 4 * LANES :]
    lane = lax.broadcasted_iota(jnp.int32, (SEG, LANES), 1)
    gain_real, gain_imag = scale(0)
    ahead = jnp.zeros((SEG, LANES), F32)
    own = jnp.zeros((SEG, LANES), F32)
    product = jnp.zeros((SEG, LANES), F32)
    cross = jnp.zeros((SEG, LANES), F32)
    rim_weight = [jnp.zeros((SEG, LANES), F32)] * 2
    columns = []
    level_ahead = jnp.zeros((1, 1), F32)
    level_own = jnp.zeros((1, 1), F32)
    level_product = jnp.zeros((1, 1), F32)
    for j in range(PAIRS):
        mean_c = rim_part[0:1, j : j + 1]
        mean_d = rim_part[SEG : SEG + 1, j : j + 1]
        chal_c, chal_d = chal_ref[2 * j], chal_ref[2 * j + 1]
        step_c, step_d = chal_c * step_ref[2 * j], chal_d * step_ref[2 * j + 1]
        weight = chal_c * pair_ref[2 * j] + chal_d * pair_ref[2 * j + 1]
        raw_c = field[:SEG, LANES * j : LANES * (j + 1)]
        raw_d = field[SEG:, LANES * j : LANES * (j + 1)]
        real_c = raw_c + mean_d
        real_d = raw_d - mean_c
        columns += [(real_c, mean_c), (real_d, mean_d)]
        ahead += chal_c * raw_c + chal_d * raw_d
        own += step_c * real_c + step_d * real_d
        product += weight * (real_c * real_d)
        cross += weight * (real_c * mean_d + real_d * mean_c)
        group = (lane >= LANES - 16 + 4 * j) & (lane < LANES - 12 + 4 * j)
        rim_weight = [
            jnp.where(group, chal_c, rim_weight[0]),
            jnp.where(group, chal_d, rim_weight[1]),
        ]
        level_ahead += chal_c * mean_d - chal_d * mean_c
        level_own += (chal_c - step_c) * mean_c + (chal_d - step_d) * mean_d
        level_product += weight * (mean_c * mean_d)
    rim_sum = rim_part[:SEG] * rim_weight[0] + rim_part[SEG:] * rim_weight[1]
    rim_sum = rim_sum + pltpu.roll(rim_sum, 4, 1)
    rim_sum = rim_sum + pltpu.roll(rim_sum, 8, 1)
    ahead = jnp.where(lane < LANES - 4, pltpu.roll(ahead, LANES - 4, 1), rim_sum)
    line_real = ahead + level_ahead - own
    line_imag = level_own
    square_real = product - level_product
    square_imag = cross
    line_scale, square_scale = scale(1), scale(2)
    value_real = (
        line_scale[0] * line_real
        - line_scale[1] * line_imag
        - square_scale[0] * square_real
        + square_scale[1] * square_imag
    )
    value_imag = (
        line_scale[0] * line_imag
        + line_scale[1] * line_real
        - square_scale[0] * square_imag
        - square_scale[1] * square_real
    )
    mixed = left_dot(first[2], jnp.concatenate([value_real, value_imag], axis=0))
    for i in range(COLS):
        send3[i] = mixed[16 * i : 16 * (i + 1)]

    def post3(k, carry):
        peer = (col + k) & 7
        pltpu.make_async_remote_copy(
            src_ref=send3.at[peer], dst_ref=recv3.at[col],
            send_sem=send_sems.at[2], recv_sem=recv_sems.at[2],
            device_id={"col": peer}, device_id_type=MESH,
        ).start()
        return carry

    lax.fori_loop(1, COLS, post3, 0)
    for i in range(COLS):
        send6[i, 0:8] = value_real[8 * i : 8 * (i + 1)]
        send6[i, 8:16] = value_imag[8 * i : 8 * (i + 1)]

    def post6(k, carry):
        peer = (col + k) & 7
        pltpu.make_async_remote_copy(
            src_ref=send6.at[peer], dst_ref=recv6.at[col],
            send_sem=send_sems.at[5], recv_sem=recv_sems.at[5],
            device_id={"col": peer}, device_id_type=MESH,
        ).start()
        return carry

    lax.fori_loop(1, COLS, post6, 0)
    recv3[col] = send3[col]
    recv6[col] = send6[col]
    for c, (real, mean_here) in enumerate(columns):
        ext[0, c] = gain_real * real - gain_imag * mean_here
        ext[1, c] = gain_imag * real + gain_real * mean_here
    pltpu.make_async_copy(
        recv3.at[pl.ds(0, COLS - 1)], recv3.at[pl.ds(0, COLS - 1)], recv_sems.at[2]
    ).wait()
    total = recv3[0]
    for i in range(1, COLS):
        total = total + recv3[i]
    send4.reshape(16, LANES)[...] = total

    here = dealt(me >> 3, col) == me

    def post4(k, carry):
        across = ((k >> 2) & 7) ^ 1
        line = (k & 3) ^ (7 * (((k >> 5) ^ col ^ 1) & 1))
        target = dealt(line, col)
        alone = (target == me) & (across == col)

        @pl.when(jnp.logical_not(alone))
        def _():
            pltpu.make_async_remote_copy(
                src_ref=send4.at[line], dst_ref=recv4.at[slot],
                send_sem=send_sems.at[3], recv_sem=recv_sems.at[3],
                device_id={"col": across, "row": target}, device_id_type=MESH,
            ).start()

        @pl.when(alone)
        def _():
            pltpu.make_async_copy(send4.at[line], recv4.at[slot], recv_sems.at[3]).start()

        return carry

    lax.fori_loop(0, SEG, post4, 0)
    pltpu.make_async_copy(
        recv6.at[pl.ds(0, COLS - 1)], recv6.at[pl.ds(0, COLS - 1)], recv_sems.at[5]
    ).wait()
    value = recv6[0]
    for i in range(1, COLS):
        value = value + recv6[i]
    send5[...] = value

    def post5(k, carry):
        pltpu.make_async_remote_copy(
            src_ref=send5, dst_ref=recv5.at[col],
            send_sem=send_sems.at[4], recv_sem=recv_sems.at[4],
            device_id={"col": (col + k) & 7}, device_id_type=MESH,
        ).start()
        return carry

    lax.fori_loop(1, COLS, post5, 0)
    recv5[col] = send5[...]

    pltpu.make_async_copy(recv4, recv4, recv_sems.at[3]).wait()
    arrived_rows[...] = recv4.reshape(LANES, LANES)[...]
    pltpu.make_async_copy(
        recv5.at[pl.ds(0, COLS - 1)], recv5.at[pl.ds(0, COLS - 1)], recv_sems.at[4]
    ).wait()
    for i in range(COLS):
        val[0, 8 * i : 8 * (i + 1)] = recv5[i, 0:8]
        val[1, 8 * i : 8 * (i + 1)] = recv5[i, 8:16]

    pltpu.make_async_copy(own_half, own_half, send_sems.at[0]).wait()
    pltpu.make_async_copy(gathered, gathered, send_sems.at[6]).wait()
    pltpu.make_async_copy(others, others, send_sems.at[1]).wait()
    pltpu.make_async_copy(
        send3.at[pl.ds(0, COLS - 1)], send3.at[pl.ds(0, COLS - 1)], send_sems.at[2]
    ).wait()

    @pl.when(here)
    def _():
        pltpu.make_async_copy(
            recv4.at[pl.ds(0, SEG - 1)], recv4.at[pl.ds(0, SEG - 1)], send_sems.at[3]
        ).wait()

    @pl.when(jnp.logical_not(here))
    def _():
        pltpu.make_async_copy(recv4, recv4, send_sems.at[3]).wait()

    for i in (4, 5):
        pltpu.make_async_copy(
            recv5.at[pl.ds(0, COLS - 1)], recv5.at[pl.ds(0, COLS - 1)], send_sems.at[i]
        ).wait()


def finish(
    ext, val, arrived_rows, own_into, last, spin, ext_out, val_out, quot_out, quot, sems
):
    pairs = [(ext, ext_out), (val, val_out), (quot, quot_out)]
    moves = [pltpu.make_async_copy(src, dst, sems.at[i]) for i, (src, dst) in enumerate(pairs)]
    moves[0].start()
    moves[1].start()
    mixed = left_dot(own_into, arrived_rows[...])
    real, imag = turn(mixed[:SEG], mixed[SEG:], spin[0], spin[1])
    both = jnp.concatenate([real, imag], axis=1)
    both = jnp.concatenate([both, both], axis=0)
    result = left_dot_turned(last, both)
    lane = lax.broadcasted_iota(jnp.int32, (SEG, LANES), 1)
    for c in range(2):
        even = result[LANES * c : LANES * c + SEG]
        odd = result[LANES * c + SEG : LANES * (c + 1)]
        quot[c] = jnp.where(lane < SEG, even, odd)
    moves[2].start()
    for move in moves:
        move.wait()


def shards(trace, step_coeff, pair_coeff, challenges):
    trace = trace.transpose(0, 2, 1)
    tables = build_tables()
    names = ["vectors", "into", "outof", "first", "twists", "spread", "mean", "last", "scales"]
    constants = [jnp.asarray(tables[name]) for name in names]
    operands = [
        pltpu.with_memory_space_constraint(x, pltpu.HBM)
        for x in (trace, step_coeff, pair_coeff, challenges, *constants)
    ]
    vmem = pltpu.VMEM
    hbm = pl.BlockSpec(memory_space=pltpu.HBM)
    inside = pl.BlockSpec(memory_space=pltpu.VMEM)
    outs = (
        jax.ShapeDtypeStruct((2, COLS, SEG, LANES), F32),
        jax.ShapeDtypeStruct((2, SEG, LANES), F32),
        jax.ShapeDtypeStruct((2, SEG, LANES), F32),
    )
    tables_scratch = [
        vmem(c.shape[1:] if n in ("vectors", "into", "outof") else c.shape, c.dtype)
        for n, c in zip(names, constants, strict=True)
        if n != "last"
    ]
    passed = pl.pallas_call(
        kernel,
        out_shape=(
            vmem(outs[0].shape, F32),
            vmem(outs[1].shape, F32),
            vmem((LANES, LANES), F32),
            vmem((2, LANES, LANES), BF16),
            vmem((2, 2 * LANES, 2 * LANES), BF16),
            vmem((2, SEG, LANES), F32),
        ),
        in_specs=[hbm] * (4 + len(constants)),
        out_specs=(inside,) * 6,
        scratch_shapes=[
            vmem(trace.shape, F32),
            *tables_scratch,
            *[pltpu.SMEM((COLS,), F32)] * 3,
            vmem((SEG, 2, LANES), F32),
            vmem((2, SEG, 2, LANES), F32),
            vmem((9, HALF, 2, LANES), F32),
            vmem((9, HALF, 2, LANES), F32),
            vmem((COLS, 16, LANES), F32),
            vmem((COLS, 16, LANES), F32),
            vmem((8, 2, LANES), F32),
            vmem((SEG, 2, LANES), F32),
            vmem((16, LANES), F32),
            vmem((COLS, 16, LANES), F32),
            vmem((COLS, 16, LANES), F32),
            vmem((COLS, 16, LANES), F32),
            pltpu.SemaphoreType.DMA((13,)),
            pltpu.SemaphoreType.DMA((7,)),
            pltpu.SemaphoreType.DMA((7,)),
            pltpu.SemaphoreType.REGULAR,
        ],
        compiler_params=pltpu.CompilerParams(
            collective_id=0, has_side_effects=True, vmem_limit_bytes=32 * 1024 * 1024
        ),
    )(*operands)
    extension, values, quotient = pl.pallas_call(
        finish,
        out_shape=outs,
        in_specs=[inside] * 6,
        out_specs=(hbm,) * 3,
        scratch_shapes=[vmem(outs[2].shape, F32), pltpu.SemaphoreType.DMA((3,))],
    )(*[pltpu.with_memory_space_constraint(x, vmem) for x in passed])
    return extension, values, quotient.reshape(2, 1, SEG * LANES)


def solution(mesh):
    placed = (P("col", None, "row"), P("col"), P("col"), P("col"))
    return jax.shard_map(
        shards,
        mesh=mesh,
        in_specs=placed,
        out_specs=(P(None, "col", None, "row"), P(None, None, "row"), P(None, "row", None)),
        check_vma=False,
    )
```

```python
import math

import jax
import jax.numpy as jnp
import numpy as np
from jax import lax
from jax.experimental import pallas as pl
from jax.experimental.pallas import tpu as pltpu
from jax.sharding import PartitionSpec as P

SEG = 64
HALF = 32
COLS = 8
PAIRS = 4
RUN = 32
LANES = 128
TRACE_LEN = SEG * SEG * RUN
COSET_LEN = 4 * TRACE_LEN
MESH = pl.DeviceIdType.MESH
F32 = jnp.float32
BF16 = jnp.bfloat16


def halves(matrix):
    high = matrix.astype(BF16)
    low = (matrix - high.astype(np.float64)).astype(BF16)
    return np.stack([high, low])


def complex_rows(angle):
    return np.stack([np.cos(angle), np.sin(angle)])


def real_form(angle, out_order, in_order):
    cosine, sine = np.cos(angle), np.sin(angle)
    grid = np.stack([np.stack([cosine, -sine]), np.stack([sine, cosine])])
    places = {"co": (0, 2), "oc": (2, 0), "ci": (1, 3), "ic": (3, 1)}
    rows, cols = angle.shape
    return grid.transpose(places[out_order] + places[in_order]).reshape(2 * rows, 2 * cols)


def build_tables():
    tau = 2.0 * np.pi
    seg = np.arange(SEG)
    run = np.arange(RUN)
    first = real_form(tau * np.outer(seg, seg) / SEG, "oc", "ci")
    final = first.T.reshape(2 * SEG, SEG // 2, 2, 2).transpose(0, 2, 1, 3).reshape(2 * SEG, 2 * SEG)
    lane = np.arange(LANES)
    offset = lane // 4 + (2 * (lane % 4) + 1) / 8.0
    rim = RUN + (2 * (lane % 4) + 1) / 8.0
    rim_here = (lane >= LANES - 16).astype(np.float64)
    beta = np.tile(run, PAIRS)
    deal = np.array([dealt(m, i) for i in range(COLS) for m in range(8)])
    summed = first.reshape(SEG, 2, 2 * SEG)[deal].reshape(2 * SEG, 2 * SEG)
    slots = np.concatenate([seg[0::2], seg[1::2]])
    matrices = []
    vectors = []
    for u in range(SEG):
        angle = tau * np.outer(SEG * seg + u, slots) / (SEG * SEG)
        matrices.append(real_form(angle, "co", "ic"))
        vectors.append(
            np.concatenate(
                [
                    complex_rows(tau * beta * u / TRACE_LEN),
                    complex_rows(-tau * offset * u / TRACE_LEN),
                    complex_rows(-tau * rim * u / TRACE_LEN),
                    complex_rows(tau * (2 * lane + 1) * u / (2 * COSET_LEN)),
                ]
            )
        )
    into, outof, turns = [], [], []
    for g in range(HALF):
        pair = (2 * g, 2 * g + 1)
        into.append(np.stack([halves(matrices[u]) for u in pair]))
        for zh in range(2):
            rows = slice(SEG * zh, SEG * (zh + 1))
            outof.append(np.stack([halves(matrices[u].T[rows]) for u in pair]))
            turns.append(np.concatenate([vectors[u][:6] for u in pair] + [vectors[2 * g + zh][6:]]))
    vectors = np.pad(np.stack(turns), ((0, 0), (0, 2), (0, 0)))
    twist_in = complex_rows(tau * beta * (64 * seg[:, None] - 2048) / TRACE_LEN)
    twist_out = complex_rows(-tau * offset * (64 * seg[:, None] - 2048) / TRACE_LEN) / TRACE_LEN
    twist_rim = (
        complex_rows(-tau * rim * (64 * seg[:, None] - 2048) / TRACE_LEN) / TRACE_LEN * rim_here
    )
    twist_quot = complex_rows(
        tau * (2 * lane + 1) * (64 * seg[:, None]) / (2 * COSET_LEN)
    ) / math.sqrt(COSET_LEN)
    twists = np.concatenate([twist_in, twist_out, twist_rim, twist_quot])
    spread = np.zeros((PAIRS, RUN, 5, LANES))
    mean = np.zeros((PAIRS, RUN, LANES))
    for j in range(PAIRS):
        spread[j, :, j, :] = 1.0 / np.sin(np.pi * (offset[None, :] - run[:, None]) / RUN)
        own = (lane >= LANES - 16) & ((lane - (LANES - 16)) // 4 == j)
        spread[j, :, 4, :] = own / np.sin(np.pi * (rim[None, :] - run[:, None]) / RUN)
        mean[j, :, j] = 1.0 / TRACE_LEN
    spread = spread.reshape(LANES, 5 * LANES)
    half = np.arange(SEG)
    order = np.concatenate([2 * half, 2 * half + 1])
    last = real_form(tau * np.outer(order, 2 * lane + 1) / 256.0, "co", "ci")
    shape = (2 * (lane % 4) + 1) / 8.0
    gain = np.exp(-1j * np.pi * shape) * np.sin(np.pi * shape)
    vanish = 1.0 / (np.exp(-1j * np.pi * (2 * (lane % 4) + 1) / 4.0) - 1.0)
    scales = []
    for value in (gain, gain * vanish, gain * gain * vanish):
        scales += [value.real, value.imag]
    scales += [np.zeros(LANES)] * 2
    return {
        "vectors": vectors.astype(np.float32),
        "into": np.stack(into),
        "outof": np.stack(outof),
        "first": np.stack([halves(first), halves(final), halves(summed)]),
        "twists": twists.astype(np.float32),
        "spread": halves(spread),
        "mean": mean.reshape(LANES, LANES).astype(BF16),
        "last": halves(last),
        "scales": np.stack(scales).astype(np.float32),
    }


def parts_of(value):
    high = value.astype(BF16)
    low = (value - high.astype(F32)).astype(BF16)
    return high, low


def left_dot(table, value):
    high, low = parts_of(value)
    left = jnp.concatenate([table[0], table[0], table[1]], axis=1)
    right = jnp.concatenate([high, low, high], axis=0)
    return jnp.dot(left, right, preferred_element_type=F32)


def left_dot_turned(table, value):
    high, low = parts_of(value)
    return lax.dot_general(
        jnp.concatenate([table[0], table[0], table[1]], axis=1),
        jnp.concatenate([high, low, high], axis=1),
        (((1,), (1,)), ((), ())),
        preferred_element_type=F32,
    )


def right_dot(value, table):
    high, low = parts_of(value)
    left = jnp.concatenate([high, low, high], axis=1)
    right = jnp.concatenate([table[0], table[0], table[1]], axis=0)
    return jnp.dot(left, right, preferred_element_type=F32)


def ring_step(k, me):
    yi, xi, zi = k & 7, (k >> 3) & 3, k >> 5
    half = (yi + 1) >> 1
    dy = 4 + half * (1 - 2 * (yi & 1))
    dx = (xi ^ (xi >> 1)) ^ 2
    dz = 1 - zi
    return ((me + 8 * dy) & 56) | ((me + 2 * dx) & 6) | ((me ^ dz) & 1)


def dealt(m, col):
    return 8 * m + 2 * ((m + (col >> 1) + 2) & 3) + (((m >> 2) ^ col ^ 1) & 1)


def turn(real, imag, cosine, sine):
    return real * cosine - imag * sine, real * sine + imag * cosine


def kernel(
    trace_hbm, step_hbm, pair_hbm, chal_hbm,
    vectors_hbm, into_hbm, outof_hbm, first_hbm, twists_hbm, spread_hbm, mean_hbm, last_hbm, scales_hbm,
    ext, val, arrived_rows, own_into, last, spin,
    trace, vectors, into, outof, first, twists, spread, mean, scales,
    step_ref, pair_ref, chal_ref,
    send1, recv1, send2, recv2, send3, recv3, send4, recv4, send5, recv5, send6, recv6,
    load_sems, send_sems, recv_sems, ready,
):
    me = lax.axis_index("row")
    col = lax.axis_index("col")
    group, far = me >> 1, me & 1
    slot = HALF * far + group

    barrier = pltpu.get_barrier_semaphore()

    def greet_row(k, carry):
        pl.semaphore_signal(
            barrier, inc=1, device_id={"row": ring_step(k, me)}, device_id_type=MESH
        )
        return carry

    def greet_col(k, carry):
        pl.semaphore_signal(
            barrier, inc=1, device_id={"col": (col + k) & 7}, device_id_type=MESH
        )
        return carry

    lax.fori_loop(HALF, SEG - 1, greet_row, 0)
    lax.fori_loop(1, COLS, greet_col, 0)


    loads = [
        pltpu.make_async_copy(src, dst, load_sems.at[i])
        for i, (src, dst) in enumerate(
            [
                (trace_hbm, trace),
                (first_hbm, first),
                (vectors_hbm.at[me], vectors),
                (into_hbm.at[group], into),
                (outof_hbm.at[me], outof),
                (twists_hbm, twists),
                (spread_hbm, spread),
                (mean_hbm, mean),
                (scales_hbm, scales),
                (last_hbm, last),
                (step_hbm, step_ref),
                (pair_hbm, pair_ref),
                (chal_hbm, chal_ref),
            ]
        )
    ]
    for load in loads:
        load.start()

    loads[0].wait()
    loads[1].wait()
    grid = jnp.concatenate(
        [
            jnp.concatenate([trace[2 * j + c] for j in range(PAIRS)], axis=0)
            for c in range(2)
        ],
        axis=1,
    )
    head = left_dot_turned(first[0], grid)
    send1.reshape(LANES, LANES)[...] = head
    for c in range(2):
        recv1[c, slot] = send1[2 * group + c]
    pl.semaphore_wait(barrier, HALF - 1 + COLS - 1 + far)

    @pl.when(far == 0)
    def _():
        pl.semaphore_signal(barrier, inc=1, device_id={"row": me ^ 1}, device_id_type=MESH)


    def post1(k, to):
        peer = ring_step(k, me)
        pltpu.make_async_remote_copy(
            src_ref=send1.at[pl.ds(2 * (peer >> 1), 2)], dst_ref=recv1.at[:, slot],
            send_sem=send_sems.at[to], recv_sem=recv_sems.at[to],
            device_id={"row": peer}, device_id_type=MESH,
        ).start()
        return to

    @pl.when(far == 1)
    def _():
        pl.semaphore_signal(ready, inc=1, device_id={"row": me ^ 1}, device_id_type=MESH)
        lax.fori_loop(0, HALF, post1, 6)

    lax.fori_loop(HALF, SEG - 1, post1, 0)

    for load in loads[2:]:
        load.wait()
    def table(index, row):
        base = twists[2 * index], twists[2 * index + 1]
        return turn(*base, vectors[2 * row : 2 * row + 1], vectors[2 * row + 1 : 2 * row + 2])

    turn_in = [table(0, 3 * c) for c in range(2)]
    turn_out = [table(1, 3 * c + 1) for c in range(2)]
    turn_rim = [table(2, 3 * c + 2) for c in range(2)]

    own_half = recv1.at[:, pl.ds(0, HALF - 1)]
    pltpu.make_async_copy(own_half, own_half, recv_sems.at[0]).wait()
    gathered = recv1.at[:, pl.ds(0, HALF)]

    @pl.when(far == 0)
    def _():
        pl.semaphore_wait(ready, 1)
        pltpu.make_async_remote_copy(
            src_ref=gathered, dst_ref=gathered,
            send_sem=send_sems.at[6], recv_sem=recv_sems.at[6],
            device_id={"row": me ^ 1}, device_id_type=MESH,
        ).start()

    pltpu.make_async_copy(gathered, gathered, recv_sems.at[6]).wait()

    rows = []
    for c in range(2):
        mixed = left_dot(into[c], recv1.reshape(2, LANES, LANES)[c])
        if c == 0:
            lowest = jnp.concatenate([mixed[0:8], mixed[SEG : SEG + 8]], axis=0)
        rows += turn(mixed[:SEG], mixed[SEG:], *turn_in[c])
    wide = right_dot(jnp.concatenate(rows, axis=0), spread)
    high, low = parts_of(lowest)
    sums = jnp.dot(high, mean[...], preferred_element_type=F32) + jnp.dot(
        low, mean[...], preferred_element_type=F32
    )
    sums = sums * jnp.where(group == 0, 1.0, 0.0).astype(F32)
    parity = lax.broadcasted_iota(jnp.int32, (SEG, LANES), 0) % 2
    sums = jnp.where(parity == 0, sums[0:1], sums[8:9])
    for c in range(2):
        pieces = []
        for j in range(5):
            part = wide[LANES * c : LANES * (c + 1), LANES * j : LANES * (j + 1)]
            real, imag = turn(part[:SEG], part[SEG:], *(turn_out[c] if j < 4 else turn_rim[c]))
            pieces.append(jnp.concatenate([real, imag], axis=0))
        back = left_dot(outof[c], jnp.concatenate(pieces, axis=1))
        for j in range(5):
            part = back[:, LANES * j : LANES * (j + 1)]
            if j < 4:
                send2.reshape(9, SEG, LANES)[2 * j + c] = part
            elif c == 0:
                rest = part + sums
            else:
                send2.reshape(9, SEG, LANES)[8] = rest + pltpu.roll(part, SEG, 1)
    def post2(k, carry):
        peer = ring_step(k, me)
        pltpu.make_async_remote_copy(
            src_ref=send2.at[:, peer >> 1], dst_ref=recv2.at[:, group],
            send_sem=send_sems.at[1], recv_sem=recv_sems.at[1],
            device_id={"row": peer}, device_id_type=MESH,
        ).start()
        return carry

    lax.fori_loop(HALF, SEG - 1, post2, 0)
    for i in range(9):
        recv2[i, group] = send2[i, group]
    spin[0], spin[1] = table(3, 6)
    own_into[...] = into[far]
    others = recv2.at[:, pl.ds(0, HALF - 1)]
    pltpu.make_async_copy(others, others, recv_sems.at[1]).wait()

    blocks = [recv2.reshape(9, SEG, LANES)[i] for i in range(9)]
    blocks.append(pltpu.roll(blocks[8], SEG, 1))
    arrived = jnp.concatenate(
        [jnp.concatenate(blocks[2 * j : 2 * j + 2], axis=0) for j in range(5)], axis=1
    )
    field = left_dot(first[1], arrived)

    def scale(row):
        return scales[2 * row : 2 * row + 1], scales[2 * row + 1 : 2 * row + 2]

    rim_part = field[:, 4 * LANES :]
    lane = lax.broadcasted_iota(jnp.int32, (SEG, LANES), 1)
    gain_real, gain_imag = scale(0)
    ahead = jnp.zeros((SEG, LANES), F32)
    own = jnp.zeros((SEG, LANES), F32)
    product = jnp.zeros((SEG, LANES), F32)
    cross = jnp.zeros((SEG, LANES), F32)
    rim_weight = [jnp.zeros((SEG, LANES), F32)] * 2
    columns = []
    level_ahead = jnp.zeros((1, 1), F32)
    level_own = jnp.zeros((1, 1), F32)
    level_product = jnp.zeros((1, 1), F32)
    for j in range(PAIRS):
        mean_c = rim_part[0:1, j : j + 1]
        mean_d = rim_part[SEG : SEG + 1, j : j + 1]
        chal_c, chal_d = chal_ref[2 * j], chal_ref[2 * j + 1]
        step_c, step_d = chal_c * step_ref[2 * j], chal_d * step_ref[2 * j + 1]
        weight = chal_c * pair_ref[2 * j] + chal_d * pair_ref[2 * j + 1]
        raw_c = field[:SEG, LANES * j : LANES * (j + 1)]
        raw_d = field[SEG:, LANES * j : LANES * (j + 1)]
        real_c = raw_c + mean_d
        real_d = raw_d - mean_c
        columns += [(real_c, mean_c), (real_d, mean_d)]
        ahead += chal_c * raw_c + chal_d * raw_d
        own += step_c * real_c + step_d * real_d
        product += weight * (real_c * real_d)
        cross += weight * (real_c * mean_d + real_d * mean_c)
        group = (lane >= LANES - 16 + 4 * j) & (lane < LANES - 12 + 4 * j)
        rim_weight = [
            jnp.where(group, chal_c, rim_weight[0]),
            jnp.where(group, chal_d, rim_weight[1]),
        ]
        level_ahead += chal_c * mean_d - chal_d * mean_c
        level_own += (chal_c - step_c) * mean_c + (chal_d - step_d) * mean_d
        level_product += weight * (mean_c * mean_d)
    rim_sum = rim_part[:SEG] * rim_weight[0] + rim_part[SEG:] * rim_weight[1]
    rim_sum = rim_sum + pltpu.roll(rim_sum, 4, 1)
    rim_sum = rim_sum + pltpu.roll(rim_sum, 8, 1)
    ahead = jnp.where(lane < LANES - 4, pltpu.roll(ahead, LANES - 4, 1), rim_sum)
    line_real = ahead + level_ahead - own
    line_imag = level_own
    square_real = product - level_product
    square_imag = cross
    line_scale, square_scale = scale(1), scale(2)
    value_real = (
        line_scale[0] * line_real
        - line_scale[1] * line_imag
        - square_scale[0] * square_real
        + square_scale[1] * square_imag
    )
    value_imag = (
        line_scale[0] * line_imag
        + line_scale[1] * line_real
        - square_scale[0] * square_imag
        - square_scale[1] * square_real
    )
    mixed = left_dot(first[2], jnp.concatenate([value_real, value_imag], axis=0))
    for i in range(COLS):
        send3[i] = mixed[16 * i : 16 * (i + 1)]

    def post3(k, carry):
        peer = (col + k) & 7
        pltpu.make_async_remote_copy(
            src_ref=send3.at[peer], dst_ref=recv3.at[col],
            send_sem=send_sems.at[2], recv_sem=recv_sems.at[2],
            device_id={"col": peer}, device_id_type=MESH,
        ).start()
        return carry

    lax.fori_loop(1, COLS, post3, 0)
    for i in range(COLS):
        send6[i, 0:8] = value_real[8 * i : 8 * (i + 1)]
        send6[i, 8:16] = value_imag[8 * i : 8 * (i + 1)]

    def post6(k, carry):
        peer = (col + k) & 7
        pltpu.make_async_remote_copy(
            src_ref=send6.at[peer], dst_ref=recv6.at[col],
            send_sem=send_sems.at[5], recv_sem=recv_sems.at[5],
            device_id={"col": peer}, device_id_type=MESH,
        ).start()
        return carry

    lax.fori_loop(1, COLS, post6, 0)
    recv3[col] = send3[col]
    recv6[col] = send6[col]
    for c, (real, mean_here) in enumerate(columns):
        ext[0, c] = gain_real * real - gain_imag * mean_here
        ext[1, c] = gain_imag * real + gain_real * mean_here
    pltpu.make_async_copy(
        recv3.at[pl.ds(0, COLS - 1)], recv3.at[pl.ds(0, COLS - 1)], recv_sems.at[2]
    ).wait()
    total = recv3[0]
    for i in range(1, COLS):
        total = total + recv3[i]
    send4.reshape(16, LANES)[...] = total

    here = dealt(me >> 3, col) == me

    def post4(k, carry):
        across = ((k >> 2) & 7) ^ 1
        line = (k & 3) ^ (7 * (((k >> 5) ^ col ^ 1) & 1))
        target = dealt(line, col)
        alone = (target == me) & (across == col)

        @pl.when(jnp.logical_not(alone))
        def _():
            pltpu.make_async_remote_copy(
                src_ref=send4.at[line], dst_ref=recv4.at[slot],
                send_sem=send_sems.at[3], recv_sem=recv_sems.at[3],
                device_id={"col": across, "row": target}, device_id_type=MESH,
            ).start()

        @pl.when(alone)
        def _():
            pltpu.make_async_copy(send4.at[line], recv4.at[slot], recv_sems.at[3]).start()

        return carry

    lax.fori_loop(0, SEG, post4, 0)
    pltpu.make_async_copy(
        recv6.at[pl.ds(0, COLS - 1)], recv6.at[pl.ds(0, COLS - 1)], recv_sems.at[5]
    ).wait()
    value = recv6[0]
    for i in range(1, COLS):
        value = value + recv6[i]
    send5[...] = value

    def post5(k, carry):
        pltpu.make_async_remote_copy(
            src_ref=send5, dst_ref=recv5.at[col],
            send_sem=send_sems.at[4], recv_sem=recv_sems.at[4],
            device_id={"col": (col + k) & 7}, device_id_type=MESH,
        ).start()
        return carry

    lax.fori_loop(1, COLS, post5, 0)
    recv5[col] = send5[...]

    pltpu.make_async_copy(recv4, recv4, recv_sems.at[3]).wait()
    arrived_rows[...] = recv4.reshape(LANES, LANES)[...]
    pltpu.make_async_copy(
        recv5.at[pl.ds(0, COLS - 1)], recv5.at[pl.ds(0, COLS - 1)], recv_sems.at[4]
    ).wait()
    for i in range(COLS):
        val[0, 8 * i : 8 * (i + 1)] = recv5[i, 0:8]
        val[1, 8 * i : 8 * (i + 1)] = recv5[i, 8:16]

    pltpu.make_async_copy(own_half, own_half, send_sems.at[0]).wait()
    pltpu.make_async_copy(gathered, gathered, send_sems.at[6]).wait()
    pltpu.make_async_copy(others, others, send_sems.at[1]).wait()
    pltpu.make_async_copy(
        send3.at[pl.ds(0, COLS - 1)], send3.at[pl.ds(0, COLS - 1)], send_sems.at[2]
    ).wait()

    @pl.when(here)
    def _():
        pltpu.make_async_copy(
            recv4.at[pl.ds(0, SEG - 1)], recv4.at[pl.ds(0, SEG - 1)], send_sems.at[3]
        ).wait()

    @pl.when(jnp.logical_not(here))
    def _():
        pltpu.make_async_copy(recv4, recv4, send_sems.at[3]).wait()

    for i in (4, 5):
        pltpu.make_async_copy(
            recv5.at[pl.ds(0, COLS - 1)], recv5.at[pl.ds(0, COLS - 1)], send_sems.at[i]
        ).wait()


def finish(
    ext, val, arrived_rows, own_into, last, spin, ext_out, val_out, quot_out, quot, sems
):
    pairs = [(ext, ext_out), (val, val_out), (quot, quot_out)]
    moves = [pltpu.make_async_copy(src, dst, sems.at[i]) for i, (src, dst) in enumerate(pairs)]
    moves[0].start()
    moves[1].start()
    mixed = left_dot(own_into, arrived_rows[...])
    real, imag = turn(mixed[:SEG], mixed[SEG:], spin[0], spin[1])
    both = jnp.concatenate([real, imag], axis=1)
    both = jnp.concatenate([both, both], axis=0)
    result = left_dot_turned(last, both)
    lane = lax.broadcasted_iota(jnp.int32, (SEG, LANES), 1)
    for c in range(2):
        even = result[LANES * c : LANES * c + SEG]
        odd = result[LANES * c + SEG : LANES * (c + 1)]
        quot[c] = jnp.where(lane < SEG, even, odd)
    moves[2].start()
    for move in moves:
        move.wait()


def shards(trace, step_coeff, pair_coeff, challenges):
    trace = trace.transpose(0, 2, 1)
    tables = build_tables()
    names = ["vectors", "into", "outof", "first", "twists", "spread", "mean", "last", "scales"]
    constants = [jnp.asarray(tables[name]) for name in names]
    operands = [
        pltpu.with_memory_space_constraint(x, pltpu.HBM)
        for x in (trace, step_coeff, pair_coeff, challenges, *constants)
    ]
    vmem = pltpu.VMEM
    hbm = pl.BlockSpec(memory_space=pltpu.HBM)
    inside = pl.BlockSpec(memory_space=pltpu.VMEM)
    outs = (
        jax.ShapeDtypeStruct((2, COLS, SEG, LANES), F32),
        jax.ShapeDtypeStruct((2, SEG, LANES), F32),
        jax.ShapeDtypeStruct((2, SEG, LANES), F32),
    )
    tables_scratch = [
        vmem(c.shape[1:] if n in ("vectors", "into", "outof") else c.shape, c.dtype)
        for n, c in zip(names, constants, strict=True)
        if n != "last"
    ]
    passed = pl.pallas_call(
        kernel,
        out_shape=(
            vmem(outs[0].shape, F32),
            vmem(outs[1].shape, F32),
            vmem((LANES, LANES), F32),
            vmem((2, LANES, LANES), BF16),
            vmem((2, 2 * LANES, 2 * LANES), BF16),
            vmem((2, SEG, LANES), F32),
        ),
        in_specs=[hbm] * (4 + len(constants)),
        out_specs=(inside,) * 6,
        scratch_shapes=[
            vmem(trace.shape, F32),
            *tables_scratch,
            *[pltpu.SMEM((COLS,), F32)] * 3,
            vmem((SEG, 2, LANES), F32),
            vmem((2, SEG, 2, LANES), F32),
            vmem((9, HALF, 2, LANES), F32),
            vmem((9, HALF, 2, LANES), F32),
            vmem((COLS, 16, LANES), F32),
            vmem((COLS, 16, LANES), F32),
            vmem((8, 2, LANES), F32),
            vmem((SEG, 2, LANES), F32),
            vmem((16, LANES), F32),
            vmem((COLS, 16, LANES), F32),
            vmem((COLS, 16, LANES), F32),
            vmem((COLS, 16, LANES), F32),
            pltpu.SemaphoreType.DMA((13,)),
            pltpu.SemaphoreType.DMA((7,)),
            pltpu.SemaphoreType.DMA((7,)),
            pltpu.SemaphoreType.REGULAR,
        ],
        compiler_params=pltpu.CompilerParams(
            collective_id=0, has_side_effects=True, vmem_limit_bytes=32 * 1024 * 1024
        ),
    )(*operands)
    extension, values, quotient = pl.pallas_call(
        finish,
        out_shape=outs,
        in_specs=[inside] * 6,
        out_specs=(hbm,) * 3,
        scratch_shapes=[vmem(outs[2].shape, F32), pltpu.SemaphoreType.DMA((3,))],
    )(*[pltpu.with_memory_space_constraint(x, vmem) for x in passed])
    return extension, values, quotient.reshape(2, 1, SEG * LANES)


def solution(mesh):
    placed = (P("col", None, "row"), P("col"), P("col"), P("col"))
    return jax.shard_map(
        shards,
        mesh=mesh,
        in_specs=placed,
        out_specs=(P(None, "col", None, "row"), P(None, None, "row"), P(None, "row", None)),
        check_vma=False,
    )
```
